128 devices in a mesh: dp: 4 (over x), blk: 8 (over y_lo, z), mp: 4 (over y_hi, core).
Axes of the slice: x: 4, y: 4 (y_hi: 2, y_lo: 2; y = y_hi * 2 + y_lo), z: 4, core: 2. Of those that a mesh axis runs over, the one named last changes fastest.
Arguments:
- tokens: bfloat16 [8192, 1024], P(('dp', 'blk')), may hold values from -6 to 6
- cotangent: bfloat16 [8192, 1024], P(('dp', 'blk')), may hold values from -6 to 6
- seg_ids: int32 [8192], P(('dp', 'blk')), may hold values from 0 to 15, as said below
- token_boxes: int32 [4, 8192], P(None, ('dp', 'blk')), may hold values from 0 to 500, as said below
- norm1_gain: bfloat16 [1024], P('blk'), may hold values from 0.5 to 1.5
- w_query: bfloat16 [1024, 1024], P('blk', 'mp'), may hold values from -0.1875 to 0.1875
- w_key: bfloat16 [1024, 1024], P('blk', 'mp'), may hold values from -0.1875 to 0.1875
- w_value: bfloat16 [1024, 1024], P('blk', 'mp'), may hold values from -0.1875 to 0.1875
- w_out_t: bfloat16 [1024, 1024], P('blk', 'mp'), may hold values from -0.75 to 0.75
- bias_table: bfloat16 [96, 16], P('blk', 'mp'), may hold values from -3 to 3
- norm2_gain: bfloat16 [1024], P('blk'), may hold values from 0.5 to 1.5
- w_gate: bfloat16 [1024, 2816], P('blk', 'mp'), may hold values from -0.1875 to 0.1875
- w_up: bfloat16 [1024, 2816], P('blk', 'mp'), may hold values from -0.1875 to 0.1875
- w_down_t: bfloat16 [1024, 2816], P('blk', 'mp'), may hold values from -0.109375 to 0.109375
Outputs:
- mixed: bfloat16 [8192, 1024], P(('dp', 'blk'))
- grad_tokens: float32 [8192, 1024], P(('dp', 'blk'))
- grad_norm1_gain: float32 [1024], P('blk')
- grad_w_query: float32 [1024, 1024], P('blk', 'mp')
- grad_w_key: float32 [1024, 1024], P('blk', 'mp')
- grad_w_value: float32 [1024, 1024], P('blk', 'mp')
- grad_w_out_t: float32 [1024, 1024], P('blk', 'mp')
- grad_bias_table: float32 [96, 16], P('blk', 'mp')
- grad_norm2_gain: float32 [1024], P('blk')
- grad_w_gate: float32 [1024, 2816], P('blk', 'mp')
- grad_w_up: float32 [1024, 2816], P('blk', 'mp')
- grad_w_down_t: float32 [1024, 2816], P('blk', 'mp')
The draws below stay inside these ranges and needn't reach their ends.
Inputs may be any that keep to these rules, and one draw needn't show every extreme that they name: `seg_ids`: within a group ids never fall, the first token has id 0 and the last id 15; one document of each group spans from the group's first 256 tokens to its last. `token_boxes`: x0 <= x1 and y0 <= y1.
All inputs are finite; a program needn't handle non-finite values.
Results may differ from the reference program's by a relative error of at most 0.025.
Values may be sent and summed in bfloat16 or wider, within the bound.
No kernel may reach another device: no remote copies, remote signals or barrier semaphores. Data moves between devices by JAX's collectives and lax.ppermute only.
A program may use at most 64 MiB of HBM per device.

```python
import math
import jax
import jax.numpy as jnp
from jax import lax

D = 1024
HEADS = 16
HEAD_DIM = 64
FF = 2816
TABLE_ROWS = 96
TOK_DEV = 256
TOKENS = 8192
N_DP = 4
N_BLK = 8


def draw_seg_ids(key, part):
    key = jax.random.fold_in(key, 11)
    length = TOK_DEV * N_BLK
    first_key, second_key, third_key = jax.random.split(key, 3)
    opening = jax.random.randint(first_key, (N_DP, 1), 1, TOK_DEV // 2)
    closing = length - jax.random.randint(second_key, (N_DP, 1), 1, TOK_DEV // 2 + 1)
    places = jnp.arange(length, dtype=jnp.int32)[None, :]
    coins = jax.random.randint(third_key, (N_DP, length), 0, 24)
    before = places < opening
    after = places >= closing
    front_starts = ((places == 0) | (coins == 0) & before).astype(jnp.int32)
    front_ids = jnp.minimum(jnp.cumsum(front_starts, axis=1) - 1, 6)
    back_starts = ((places == closing) | (coins == 0) & (places > closing)).astype(jnp.int32)
    later = jnp.sum(back_starts, axis=1, keepdims=True) - jnp.cumsum(back_starts, axis=1)
    back_ids = 15 - jnp.minimum(later, 7)
    ids = jnp.where(before, front_ids, jnp.where(after, back_ids, 7))
    return ids.astype(jnp.int32).reshape(-1)


def draw_token_boxes(key, part):
    key = jax.random.fold_in(key, 17)
    first_key, second_key = jax.random.split(key, 2)
    corner = jax.random.randint(first_key, (2, TOK_DEV * N_DP * N_BLK), 0, 501)
    extent = jax.random.randint(second_key, (2, TOK_DEV * N_DP * N_BLK), 0, 121)
    return jnp.concatenate([corner, jnp.minimum(corner + extent, 500)], axis=0)


def steps_of(rng, dims, cuts, least, top_value):
    level = 1.0
    for axis_at, parts in cuts:
        heights = jax.random.uniform(jax.random.fold_in(jax.random.fold_in(rng, 6), axis_at), (parts,), jnp.float32, least / len(cuts), top_value / len(cuts))
        level = level * jnp.repeat(jnp.exp(heights), dims[axis_at] // parts).reshape((-1,) + (1,) * (len(dims) - 1 - axis_at))
    return level


def normal_values(key, shape, spread, most, cuts=(), kind=jnp.bfloat16):
    values = jax.random.normal(key, shape, jnp.float32) * spread
    if len(cuts) > 0:
        values = steps_of(key, shape, cuts, -0.22, 0.18) * values
    return jnp.clip(values, min=-most, max=most).astype(kind)


def setup_inputs(seed: int = 0) -> dict:
    key_list = jax.random.split(jax.random.key(seed), 15)
    return {
        "tokens": normal_values(key_list[0], (TOKENS, D), 1.0, 6.0, ((0, 32),)),
        "cotangent": normal_values(key_list[1], (TOKENS, D), 1.0, 6.0, ((0, 32),)),
        "seg_ids": draw_seg_ids(jax.random.fold_in(key_list[14], 71), 0),
        "token_boxes": draw_token_boxes(jax.random.fold_in(key_list[14], 71), 0),
        "norm1_gain": jnp.clip(1.0 + 0.1 * jax.random.normal(key_list[4], (D,), jnp.float32), 0.5, 1.5).astype(jnp.bfloat16),
        "w_query": normal_values(key_list[5], (D, HEADS * HEAD_DIM), D ** -0.5, 0.1875, ((0, 8), (1, 4))),
        "w_key": normal_values(key_list[6], (D, HEADS * HEAD_DIM), D ** -0.5, 0.1875, ((0, 8), (1, 4))),
        "w_value": normal_values(key_list[7], (D, HEADS * HEAD_DIM), D ** -0.5, 0.1875, ((0, 8), (1, 4))),
        "w_out_t": normal_values(key_list[8], (D, HEADS * HEAD_DIM), HEAD_DIM ** -0.5, 0.75, ((0, 8), (1, 4))),
        "bias_table": normal_values(key_list[9], (TABLE_ROWS, HEADS), 0.5, 3.0, ((0, 8), (1, 4))),
        "norm2_gain": jnp.clip(1.0 + 0.1 * jax.random.normal(key_list[10], (D,), jnp.float32), 0.5, 1.5).astype(jnp.bfloat16),
        "w_gate": normal_values(key_list[11], (D, FF), D ** -0.5, 0.1875, ((0, 8), (1, 4))),
        "w_up": normal_values(key_list[12], (D, FF), D ** -0.5, 0.1875, ((0, 8), (1, 4))),
        "w_down_t": normal_values(key_list[13], (D, FF), FF ** -0.5, 0.109375, ((0, 8), (1, 4))),
    }


EPS = 1e-06
SEQ_EDGES = (1, 2, 3, 4, 5, 6, 7, 8, 12, 16, 23, 32, 46, 64, 91)
BOX_EDGES = (2, 4, 6, 8, 12, 16, 24, 32, 48, 64, 96, 128, 192, 256, 384)
PRECISE = lax.Precision.HIGHEST

@jax.custom_vjp
def low(v):
    return lax.optimization_barrier(v.astype(jnp.bfloat16)).astype(jnp.float32)

@jax.custom_vjp
def low_back(v):
    return v

def low_keep(v):
    return (low(v), None)

def low_pass(kept, grad):
    return (grad,)

def back_keep(v):
    return (v, None)

def back_low(kept, grad):
    return (low(grad),)
low.defvjp(low_keep, low_pass)
low_back.defvjp(back_keep, back_low)

def bucket_of(offset, edge_list):
    magnitude = jnp.abs(offset)
    result = jnp.zeros(offset.shape, jnp.int32)
    for border in edge_list:
        result = result + (magnitude >= border).astype(jnp.int32)
    return result + 16 * (offset > 0).astype(jnp.int32)

def rms_scale(values):
    return lax.rsqrt(lax.optimization_barrier(jnp.mean(values * values, axis=-1, keepdims=True)) + EPS)

def matmul_high(left, right):
    return jnp.dot(left, right, precision=PRECISE)

def attend_group(queries, key_rows, value_rows, token_meta, bias_rows):
    length = queries.shape[0]
    block_rows = math.gcd(length, 512)
    block_count = length // block_rows
    query_blocks = queries.reshape(block_count, block_rows, HEADS, HEAD_DIM)
    meta_blocks = jnp.transpose(token_meta.reshape(4, block_count, block_rows), (1, 0, 2))

    def attend_block(inputs_pair):
        query_block, block_meta = inputs_pair
        raw_scores = jnp.einsum('qhd,khd->hqk', query_block, key_rows, precision=PRECISE) * HEAD_DIM ** (-0.5)
        seq_bucket = bucket_of(token_meta[3][None, :] - block_meta[3][:, None], SEQ_EDGES)
        hor_bucket = bucket_of(token_meta[1][None, :] - block_meta[1][:, None], BOX_EDGES) + 32
        ver_bucket = bucket_of(token_meta[2][None, :] - block_meta[2][:, None], BOX_EDGES) + 64
        bias = bias_rows[seq_bucket] + bias_rows[hor_bucket] + bias_rows[ver_bucket]
        scores = low_back(raw_scores + jnp.transpose(bias, (2, 0, 1)))
        allowed = block_meta[0][:, None] == token_meta[0][None, :]
        scores = jnp.where(allowed[None], scores, -1e+30)
        probs = jax.nn.softmax(scores, axis=-1)
        return jnp.einsum('hqk,khd->qhd', low(probs), value_rows, precision=PRECISE)
    return lax.map(jax.checkpoint(attend_block), (query_blocks, meta_blocks)).reshape(length, HEADS, HEAD_DIM)

def forward(tokens, norm1_gain, w_query, w_key, w_value, w_out_t, bias_table, norm2_gain, w_gate, w_up, w_down_t, token_meta):
    normed_one = low(tokens * rms_scale(tokens) * norm1_gain)
    queries = low(low_back(matmul_high(normed_one, w_query)))
    key_rows = low(low_back(matmul_high(normed_one, w_key)))
    value_rows = low(low_back(matmul_high(normed_one, w_value)))
    groups = token_meta.shape[0]
    length = token_meta.shape[2]
    shape_four = (groups, length, HEADS, HEAD_DIM)

    def per_group(group_args):
        return attend_group(group_args[0], group_args[1], group_args[2], group_args[3], bias_table)
    attended = lax.map(per_group, (queries.reshape(shape_four), key_rows.reshape(shape_four), value_rows.reshape(shape_four), token_meta))
    attended = low(low_back(attended.reshape(groups * length, HEADS * HEAD_DIM)))
    branch = low_back(matmul_high(attended, w_out_t.T))
    middle = tokens + branch
    normed_two = low(middle * rms_scale(middle) * norm2_gain)
    gate = low_back(matmul_high(normed_two, w_gate))
    upward = low_back(matmul_high(normed_two, w_up))
    hidden = low(jax.nn.gelu(gate, approximate=True) * upward)
    return middle + matmul_high(hidden, w_down_t.T)

def reference(tokens, cotangent, seg_ids, token_boxes, norm1_gain, w_query, w_key, w_value, w_out_t, bias_table, norm2_gain, w_gate, w_up, w_down_t):
    length = TOK_DEV * N_BLK
    groups = seg_ids.shape[0] // length
    centre_x = (token_boxes[0] + token_boxes[2]).reshape(groups, length)
    centre_y = (token_boxes[1] + token_boxes[3]).reshape(groups, length)
    places = jnp.broadcast_to(jnp.arange(length, dtype=jnp.int32)[None, :], (groups, length))
    token_meta = jnp.stack([seg_ids.reshape(groups, length), centre_x, centre_y, places], axis=1)
    floats = tuple((item.astype(jnp.float32) for item in (tokens, norm1_gain, w_query, w_key, w_value, w_out_t, bias_table, norm2_gain, w_gate, w_up, w_down_t)))

    def layer_apply(*weights):
        return forward(*weights, token_meta)
    mixed, pull_back = jax.vjp(layer_apply, *floats)
    grads = pull_back(cotangent.astype(jnp.float32))
    return (mixed.astype(jnp.bfloat16), grads[0], grads[1], grads[2], grads[3], grads[4], grads[5], grads[6], grads[7], grads[8], grads[9], grads[10])
```

```python
import functools

import jax
import jax.numpy as jnp
from jax import lax
from jax.experimental import pallas as pl
from jax.experimental.pallas import tpu as pltpu
from jax.sharding import PartitionSpec as P

HEAD_DIM = 64
EPS = 1e-06
SEQ_EDGES = (1, 2, 3, 4, 5, 6, 7, 8, 12, 16, 23, 32, 46, 64, 91)
BOX_EDGES = (2, 4, 6, 8, 12, 16, 24, 32, 48, 64, 96, 128, 192, 256, 384)
BF16 = jnp.bfloat16
F32 = jnp.float32
LANES = 128
MIB = 2**20
VMEM = pl.BlockSpec(memory_space=pltpu.VMEM)


def params(mib, steps=1):
    return pltpu.CompilerParams(
        vmem_limit_bytes=mib * MIB, dimension_semantics=("arbitrary",) * steps
    )


def rms_scale(values):
    return lax.rsqrt(jnp.mean(values * values, axis=-1, keepdims=True) + EPS)


def contract_rows(left, right):
    return lax.dot_general(
        left, right, (((0,), (0,)), ((), ())), preferred_element_type=jnp.float32
    )


def contract_cols(left, right):
    return lax.dot_general(
        left, right, (((1,), (1,)), ((), ())), preferred_element_type=jnp.float32
    )


def gated_unit(gate, upward):
    return jax.nn.gelu(gate, approximate=True) * upward


def norm_back(inputs, scale_rows, gain, normed_grad):
    gain_grad = jnp.sum(normed_grad * inputs * scale_rows, axis=0)
    weighted = normed_grad * gain
    cubed = scale_rows * scale_rows * scale_rows
    input_grad = scale_rows * weighted - inputs * cubed * jnp.mean(
        weighted * inputs, axis=1, keepdims=True
    )
    return (gain_grad, input_grad)


def count_edges(magnitude, edge_list):
    result = jnp.zeros(magnitude.shape, jnp.int32)
    for border in edge_list:
        result = result + (magnitude >= border).astype(jnp.int32)
    return result


def box_cell(offset):
    half = jnp.abs(offset) >> 1
    cell = jnp.where(half < 64, (half >> 2) + 6, (half >> 5) + 20)
    cell = jnp.where(half < 8, half, cell)
    return cell + jnp.where(offset > 0, 64, 0)


def cell_bucket(cell):
    low = cell & 63
    half = jnp.where(low < 22, (low - 6) << 2, (low - 20) << 5)
    half = jnp.where(low < 8, low, half)
    return count_edges(half * 2, BOX_EDGES) + jnp.where(cell >= 64, 16, 0)


def lookup(table, index):
    return jnp.take_along_axis(table, index, axis=1, mode="promise_in_bounds")


def bias_kernel(blk_ref, query_ref, key_ref, table_ref, bias_ref):
    heads, rows, width = bias_ref.shape
    chunk = 32
    step = pl.program_id(0)
    ahead = (step - blk_ref[0]) * width
    lane = lax.broadcasted_iota(jnp.int32, (8, LANES), 1)
    buckets = cell_bucket(lane)
    table = table_ref[...]
    hor = lookup(table, buckets + 32)
    ver = lookup(table, buckets + 64)
    far_bucket = jnp.where(ahead > 0, 31, 15) + jnp.zeros((8, LANES), jnp.int32)
    far = lookup(table, far_bucket)
    near = jnp.abs(ahead) <= width

    def piece(at, column, with_near):
        here = pl.ds(pl.multiple_of(at * chunk, chunk), chunk)
        there = slice(column * LANES, (column + 1) * LANES)
        meta = query_ref[here, :]
        keys = key_ref[:, there]
        hor_cell = box_cell(keys[1:2, :] - meta[:, 1:2])
        ver_cell = box_cell(keys[2:3, :] - meta[:, 2:3])
        same = keys[0:1, :] == meta[:, 0:1]
        if with_near:
            first = at * chunk
            row = lax.broadcasted_iota(jnp.int32, (chunk, LANES), 0) + first
            col = lax.broadcasted_iota(jnp.int32, (chunk, LANES), 1) + (ahead + column * LANES)
            offset = col - row
            seq = count_edges(jnp.abs(offset), SEQ_EDGES) + jnp.where(offset > 0, 16, 0)
        for head in range(heads):
            spread = lambda values: jnp.broadcast_to(values[head : head + 1, :], (chunk, LANES))
            if with_near:
                total = lookup(spread(hor), hor_cell) + lookup(spread(table), seq)
            else:
                total = lookup(spread(hor + far), hor_cell)
            total = total + lookup(spread(ver), ver_cell)
            bias_ref[head, here, there] = jnp.where(same, total, -1e30)

    def all_pieces(with_near):
        def body(at, carry):
            for column in range(width // LANES):
                piece(at, column, with_near)
            return carry

        lax.fori_loop(0, rows // chunk, body, 0)

    @pl.when(near)
    def _():
        all_pieces(True)

    @pl.when(jnp.logical_not(near))
    def _():
        all_pieces(False)


def bias_scores(blk, query_meta, key_meta, table, heads):
    rows = query_meta.shape[0]
    length = key_meta.shape[1]
    return pl.pallas_call(
        bias_kernel,
        grid=(length // rows,),
        in_specs=[
            pl.BlockSpec(memory_space=pltpu.SMEM),
            pl.BlockSpec((rows, 8), lambda s: (0, 0)),
            pl.BlockSpec((8, rows), lambda s: (0, s)),
            pl.BlockSpec((8, LANES), lambda s: (0, 0)),
        ],
        out_specs=pl.BlockSpec((heads, rows, rows), lambda s: (0, 0, s)),
        out_shape=jax.ShapeDtypeStruct((heads, rows, length), F32),
        compiler_params=params(32),
        name="bias_scores",
    )(blk, query_meta, key_meta, table)


def attend_kernel(query_ref, pair_ref, bias_ref, probs_ref, exact_ref, low_ref):
    blocks, width, _ = pair_ref.shape
    heads = bias_ref.shape[0]
    features = heads * HEAD_DIM
    outs = []
    for head in range(heads):
        cols = slice(head * HEAD_DIM, (head + 1) * HEAD_DIM)
        vcols = slice(features + head * HEAD_DIM, features + (head + 1) * HEAD_DIM)
        query = query_ref[:, cols]
        scores = []
        for block in range(blocks):
            span = slice(block * width, (block + 1) * width)
            scores.append(contract_cols(query, pair_ref[block, :, cols]) + bias_ref[head, :, span])
        top = functools.reduce(jnp.maximum, scores)
        top = jnp.max(top, axis=1, keepdims=True)
        weights = [jnp.exp(score - top) for score in scores]
        total = functools.reduce(jnp.add, weights)
        inverse = 1.0 / jnp.sum(total, axis=1, keepdims=True)
        result = None
        for block in range(blocks):
            span = slice(block * width, (block + 1) * width)
            low = (weights[block] * inverse).astype(BF16)
            probs_ref[head, :, span] = low
            part = jnp.dot(low, pair_ref[block, :, vcols], preferred_element_type=F32)
            result = part if result is None else result + part
        outs.append(result)
    exact = jnp.concatenate(outs, axis=1)
    exact_ref[...] = exact
    low_ref[...] = exact.astype(BF16)


def attend(queries, pairs, bias):
    heads, rows, length = bias.shape
    blocks, width, both = pairs.shape
    tile = 128
    return pl.pallas_call(
        attend_kernel,
        grid=(rows // tile,),
        in_specs=[
            pl.BlockSpec((tile, both // 2), lambda s: (s, 0)),
            pl.BlockSpec((blocks, width, both), lambda s: (0, 0, 0)),
            pl.BlockSpec((heads, tile, length), lambda s: (0, s, 0)),
        ],
        out_specs=[
            pl.BlockSpec((heads, tile, length), lambda s: (0, s, 0)),
            pl.BlockSpec((tile, both // 2), lambda s: (s, 0)),
            pl.BlockSpec((tile, both // 2), lambda s: (s, 0)),
        ],
        out_shape=[
            jax.ShapeDtypeStruct((heads, rows, length), BF16),
            jax.ShapeDtypeStruct((rows, both // 2), F32),
            jax.ShapeDtypeStruct((rows, both // 2), BF16),
        ],
        compiler_params=params(56),
        name="attend",
    )(queries, pairs, bias)


def attend_back_kernel(
    query_ref, grad_ref, exact_ref, pair_ref, probs_ref, score_ref, pair_grad_ref, query_grad_ref, sums
):
    heads, rows, width = probs_ref.shape
    features = heads * HEAD_DIM
    step = pl.program_id(0)

    @pl.when(step == 0)
    def _():
        sums[...] = jnp.zeros_like(sums)

    for head in range(heads):
        cols = slice(head * HEAD_DIM, (head + 1) * HEAD_DIM)
        vcols = slice(features + head * HEAD_DIM, features + (head + 1) * HEAD_DIM)
        grad = grad_ref[:, cols]
        delta = jnp.sum(grad.astype(F32) * exact_ref[:, cols], axis=1, keepdims=True)
        probs = probs_ref[head]
        prob_grad = contract_cols(grad, pair_ref[0, :, vcols])
        score_grad = (probs.astype(F32) * (prob_grad - delta)).astype(BF16)
        score_ref[head] = score_grad
        sums[:, cols] += jnp.dot(score_grad, pair_ref[0, :, cols], preferred_element_type=F32)
        pair_grad_ref[0, cols, :] = contract_rows(query_ref[:, cols], score_grad).astype(BF16)
        pair_grad_ref[0, vcols, :] = contract_rows(grad, probs).astype(BF16)

    @pl.when(step == pl.num_programs(0) - 1)
    def _():
        query_grad_ref[...] = (sums[...] * HEAD_DIM ** (-0.5)).astype(BF16)


def attend_back(queries, grads, exact, pairs, probs):
    heads, rows, length = probs.shape
    blocks, width, both = pairs.shape
    whole = pl.BlockSpec((rows, both // 2), lambda s: (0, 0))
    return pl.pallas_call(
        attend_back_kernel,
        grid=(blocks,),
        in_specs=[
            whole,
            whole,
            whole,
            pl.BlockSpec((1, width, both), lambda s: (s, 0, 0)),
            pl.BlockSpec((heads, rows, width), lambda s: (0, 0, s)),
        ],
        out_specs=[
            pl.BlockSpec((heads, rows, width), lambda s: (0, 0, s)),
            pl.BlockSpec((1, both, width), lambda s: (s, 0, 0)),
            whole,
        ],
        out_shape=[
            jax.ShapeDtypeStruct((heads, rows, length), BF16),
            jax.ShapeDtypeStruct((blocks, both, width), BF16),
            jax.ShapeDtypeStruct((rows, both // 2), BF16),
        ],
        scratch_shapes=[pltpu.VMEM((rows, both // 2), F32)],
        compiler_params=params(32),
        name="attend_back",
    )(queries, grads, exact, pairs, probs)


BOX_SPAN = 1024
SEQ_SPAN = 512
TILE = 512


def threshold_row(edge_list, far, lane):
    borders = [-far] + [1 - edge for edge in reversed(edge_list)] + [1] + list(edge_list)
    result = jnp.zeros(lane.shape, jnp.int32)
    for at, border in enumerate(borders):
        result = jnp.where(lane == at, border, result)
    return result


def table_grad_kernel(query_ref, key_ref, score_ref, out_ref):
    heads, rows, length = score_ref.shape
    step = pl.program_id(0)
    axis = step // 2
    row = jnp.where(axis == 0, 1, jnp.where(axis == 1, 2, 3))
    offset = jnp.where(axis == 2, 0, (step % 2) * TILE)
    lane = lax.broadcasted_iota(jnp.int32, (rows, LANES), 1)
    box = threshold_row(BOX_EDGES, 4096, lane[:1])
    seq = threshold_row(SEQ_EDGES, 4096, lane[:1])
    mine = jnp.where(
        axis == 0, query_ref[:, 1:2], jnp.where(axis == 1, query_ref[:, 2:3], query_ref[:, 3:4])
    )
    thresholds = jnp.where(axis == 2, seq, box)
    index = jnp.clip(mine + thresholds, 0, BOX_SPAN - 1)
    index = jnp.where(axis == 2, jnp.minimum(index, SEQ_SPAN - 1), index)
    column = index & (LANES - 1)
    block = (index - offset) >> 7
    level = lax.broadcasted_iota(jnp.int32, (TILE, 1), 0) + offset
    reached = (key_ref[pl.ds(row, 1), :] >= level).astype(F32).astype(BF16)

    @pl.when((step == 0) | (step == 2) | (step == 4))
    def _():
        out_ref[...] = jnp.zeros_like(out_ref)

    for head in range(heads):
        sums = contract_cols(score_ref[head], reached)
        picked = jnp.zeros((rows, LANES), F32)
        for at in range(TILE // LANES):
            found = lookup(sums[:, at * LANES : (at + 1) * LANES], column)
            picked = picked + jnp.where(block == at, found, 0.0)
        out_ref[0, head : head + 1, :] += jnp.sum(picked, axis=0, keepdims=True)


def table_grad_sums(query_meta, key_meta, score_grad):
    heads, rows, length = score_grad.shape
    return pl.pallas_call(
        table_grad_kernel,
        grid=(5,),
        in_specs=[
            pl.BlockSpec((rows, 8), lambda s: (0, 0)),
            pl.BlockSpec((8, length), lambda s: (0, 0)),
            pl.BlockSpec((heads, rows, length), lambda s: (0, 0, 0)),
        ],
        out_specs=pl.BlockSpec((1, 8, LANES), lambda s: (s // 2, 0, 0)),
        out_shape=jax.ShapeDtypeStruct((3, 8, LANES), F32),
        compiler_params=params(56),
        name="table_grad",
    )(query_meta, key_meta, score_grad)


def table_from_sums(sums, heads):
    sums = jnp.concatenate([sums[2:], sums[:2]], axis=0)[:, :heads, :32]
    after = jnp.concatenate([sums[:, :, 1:], jnp.zeros_like(sums[:, :, :1])], axis=2)
    part = sums - after
    part = jnp.concatenate([part[:, :, :16][:, :, ::-1], part[:, :, 16:]], axis=2)
    return jnp.transpose(part, (0, 2, 1)).reshape(96, heads)


def spread_gather(values, axis_name, count):
    return lax.all_to_all(
        jnp.broadcast_to(values[None], (count,) + values.shape), axis_name, 0, 0, tiled=False
    )


def swap(values, axis_name, count, bit):
    return lax.ppermute(values, axis_name, [(at, at ^ bit) for at in range(count)])


def sum_mp(values):
    half = values.shape[0] // 2
    core = lax.axis_index("mp") % 2
    mine = lax.dynamic_slice_in_dim(values, core * half, half, 0)
    other = lax.dynamic_slice_in_dim(values, (1 - core) * half, half, 0)
    got = swap(other.astype(BF16), "mp", 4, 1)
    part = (mine.astype(F32) + got.astype(F32)).astype(BF16)
    got = swap(part, "mp", 4, 2)
    total = (part.astype(F32) + got.astype(F32)).astype(BF16)
    got = swap(total, "mp", 4, 1)
    first = jnp.where(core == 0, total, got)
    second = jnp.where(core == 0, got, total)
    return jnp.concatenate([first, second], axis=0)


def sum_dp(values):
    total = values.astype(F32)
    low = values.astype(BF16)
    for hop in (1, 2, 3):
        got = lax.ppermute(low, "dp", [(at, (at + hop) % 4) for at in range(4)])
        total = total + got.astype(F32)
    return total


def shards(
    tokens,
    cotangent,
    seg_ids,
    token_boxes,
    norm1_gain,
    w_query,
    w_key,
    w_value,
    w_out_t,
    bias_table,
    norm2_gain,
    w_gate,
    w_up,
    w_down_t,
):
    rows, model = tokens.shape
    blocks = 8
    length = rows * blocks
    features = w_query.shape[1]
    units = w_gate.shape[1]
    heads = features // HEAD_DIM
    blk = lax.axis_index("blk")

    centre_x = token_boxes[0] + token_boxes[2]
    centre_y = token_boxes[1] + token_boxes[3]
    pad = rows - bias_table.size
    small = jnp.stack(
        [
            seg_ids.astype(BF16),
            (centre_x >> 8).astype(BF16),
            (centre_x & 255).astype(BF16),
            (centre_y >> 8).astype(BF16),
            (centre_y & 255).astype(BF16),
            jnp.concatenate([norm1_gain, norm2_gain]),
            jnp.concatenate([bias_table.reshape(-1), jnp.zeros((pad,), BF16)]),
        ]
    )
    small = jnp.concatenate([small, jnp.zeros((9, rows), BF16)], axis=0)
    small_all = spread_gather(small, "blk", blocks)
    gain_one = small_all[:, 5, :LANES].reshape(1, model).astype(F32)
    gain_two = small_all[:, 5, LANES:].reshape(1, model).astype(F32)
    table = small_all[:, 6, : bias_table.size].reshape(96, heads).astype(F32)
    table = jnp.pad(table.T, ((0, 8 - heads), (0, LANES - 96)))
    places = jnp.transpose(small_all[:, :5, :], (1, 0, 2)).reshape(5, length).astype(jnp.int32)
    key_place = jnp.clip(
        jnp.arange(length, dtype=jnp.int32) - blk * rows + SEQ_SPAN // 4, 0, SEQ_SPAN - 1
    )
    zero_row = jnp.zeros((length,), jnp.int32)
    key_meta = jnp.stack(
        [
            places[0],
            places[1] * 256 + places[2],
            places[3] * 256 + places[4],
            key_place,
            zero_row,
            zero_row,
            zero_row,
            zero_row,
        ]
    )
    own_place = jnp.arange(rows, dtype=jnp.int32) + SEQ_SPAN // 4
    query_meta = jnp.stack([seg_ids, centre_x, centre_y, own_place], axis=1)
    query_meta = jnp.pad(query_meta, ((0, 0), (0, 4)))

    late = jnp.concatenate([w_out_t, w_gate, w_up, w_down_t], axis=1)
    late_all = lax.all_gather(late, "blk", axis=0, tiled=True)
    early = jnp.concatenate([w_query, w_key, w_value], axis=1)
    early_all = spread_gather(early, "blk", blocks).reshape(model, 3 * features)

    bias = bias_scores(blk.reshape(1), query_meta, key_meta, table, heads)

    inputs = tokens.astype(F32)
    scale_one = rms_scale(inputs)
    normed_one = (inputs * scale_one * gain_one).astype(BF16)
    projected = jnp.dot(normed_one, early_all, preferred_element_type=F32).astype(BF16)
    queries = projected[:, :features] * jnp.asarray(HEAD_DIM ** (-0.5), BF16)
    pairs = spread_gather(projected[:, features:], "blk", blocks)
    probs, attn_exact, attended = attend(queries, pairs, bias)

    out_w = late_all[:, :features]
    gate_w = late_all[:, features : features + units]
    upward_w = late_all[:, features + units : features + 2 * units]
    down_w = late_all[:, features + 2 * units :]
    branch = sum_mp(contract_cols(attended, out_w).astype(BF16)).astype(F32)
    middle = inputs + branch
    scale_two = rms_scale(middle)
    normed_two = (middle * scale_two * gain_two).astype(BF16)
    gate = jnp.dot(normed_two, gate_w, preferred_element_type=F32)
    upward = jnp.dot(normed_two, upward_w, preferred_element_type=F32)
    gated_vals, pull_back = jax.vjp(gated_unit, gate, upward)
    hidden = gated_vals.astype(BF16)
    hidden_grad = jnp.dot(cotangent, down_w, preferred_element_type=F32)
    gate_grad, upward_grad = pull_back(hidden_grad)
    gate_low = gate_grad.astype(BF16)
    upward_low = upward_grad.astype(BF16)
    normed_two_grad = sum_mp(
        (contract_cols(gate_low, gate_w) + contract_cols(upward_low, upward_w)).astype(BF16)
    ).astype(F32)
    ffn_out = sum_mp(contract_cols(hidden, down_w).astype(BF16)).astype(F32)
    mixed = (middle + ffn_out).astype(BF16)
    ffn_grads = jnp.concatenate(
        [
            contract_rows(normed_two, gate_low).astype(BF16),
            contract_rows(normed_two, upward_low).astype(BF16),
            contract_rows(cotangent, hidden).astype(BF16),
        ],
        axis=1,
    )
    ffn_part = lax.psum_scatter(ffn_grads, "blk", scatter_dimension=0, tiled=True)
    ffn_final = lax.psum(ffn_part, "dp").astype(F32)

    gain_two_grad, middle_part = norm_back(middle, scale_two, gain_two, normed_two_grad)
    middle_grad = cotangent.astype(F32) + middle_part
    branch_low = middle_grad.astype(BF16)
    out_grad_w = contract_rows(branch_low, attended).astype(BF16)
    attended_grad = jnp.dot(branch_low, out_w, preferred_element_type=F32).astype(BF16)
    score_grad, pair_grad, query_low = attend_back(
        queries, attended_grad, attn_exact, pairs, probs
    )
    sums = table_grad_sums(query_meta, key_meta, score_grad)
    table_grad = table_from_sums(sums, heads)
    pair_parts = lax.all_to_all(pair_grad, "blk", 0, 0, tiled=False)
    pair_low = jnp.sum(pair_parts.astype(F32), axis=0).astype(BF16)

    pair_t = pair_low.T
    triple = jnp.concatenate([query_low, pair_t], axis=1)
    triple_grad_w = contract_rows(normed_one, triple).astype(BF16)
    normed_partial = contract_cols(triple, early_all)
    normed_one_grad = sum_mp(normed_partial.astype(BF16)).astype(F32)
    gain_one_part = jnp.sum(normed_partial * inputs * scale_one, axis=0)
    _, input_part = norm_back(inputs, scale_one, gain_one, normed_one_grad)
    tokens_grad = middle_grad + input_part

    table_cols = jnp.pad(table_grad.reshape(blocks, 12, heads), ((0, 0), (0, LANES - 12), (0, 0)))
    extra = jnp.concatenate(
        [gain_one_part[:, None], gain_two_grad[:, None], table_cols.reshape(model, heads)], axis=1
    )
    extra = jnp.pad(extra, ((0, 0), (0, LANES - extra.shape[1]))).astype(BF16)
    bundle = jnp.concatenate([triple_grad_w, out_grad_w, extra], axis=1)
    bundle = lax.all_to_all(bundle.reshape(blocks, LANES, -1), "blk", 0, 0, tiled=False)
    bundle = jnp.sum(bundle.astype(F32), axis=0).astype(BF16)
    final = sum_dp(bundle)
    small_final = final[:, 4 * features :]
    gain_one_low = small_final[:, 0].reshape(1, LANES)
    gain_one_low = jnp.broadcast_to(gain_one_low, (16, LANES))
    gain_one_sum = gain_one_low.astype(F32)
    for bit in (1, 2):
        gain_one_sum = gain_one_sum + swap(gain_one_sum.astype(BF16), "mp", 4, bit).astype(F32)
    return (
        mixed,
        tokens_grad,
        gain_one_sum[0],
        final[:, :features],
        final[:, features : 2 * features],
        final[:, 2 * features : 3 * features],
        final[:, 3 * features : 4 * features],
        small_final[:12, 2 : 2 + heads],
        small_final[:, 1],
        ffn_final[:, :units],
        ffn_final[:, units : 2 * units],
        ffn_final[:, 2 * units :],
    )


def solution(mesh):
    rows = P(("dp", "blk"), None)
    weight = P("blk", "mp")
    in_specs = (
        rows,
        rows,
        P(("dp", "blk")),
        P(None, ("dp", "blk")),
        P("blk"),
        weight,
        weight,
        weight,
        weight,
        weight,
        P("blk"),
        weight,
        weight,
        weight,
    )
    out_specs = (
        rows,
        rows,
        P("blk"),
        weight,
        weight,
        weight,
        weight,
        weight,
        P("blk"),
        weight,
        weight,
        weight,
    )
    return jax.shard_map(shards, mesh=mesh, in_specs=in_specs, out_specs=out_specs, check_vma=False)
```

```python
import functools

import jax
import jax.numpy as jnp
from jax import lax
from jax.experimental import pallas as pl
from jax.experimental.pallas import tpu as pltpu
from jax.sharding import PartitionSpec as P

HEAD_DIM = 64
EPS = 1e-06
SEQ_EDGES = (1, 2, 3, 4, 5, 6, 7, 8, 12, 16, 23, 32, 46, 64, 91)
BOX_EDGES = (2, 4, 6, 8, 12, 16, 24, 32, 48, 64, 96, 128, 192, 256, 384)
BF16 = jnp.bfloat16
F32 = jnp.float32
LANES = 128
MIB = 2**20
VMEM_MIB = 32
SMEM = pl.BlockSpec(memory_space=pltpu.SMEM)


def whole(*arrays):
    return [pl.BlockSpec(item.shape, lambda s, rank=len(item.shape): (0,) * rank) for item in arrays]


def shape(dims, kind):
    return jax.ShapeDtypeStruct(dims, kind)


HBM = pl.BlockSpec(memory_space=pl.ANY)


def simple(kernel, name, out, args, place=None, deps=(), micros=0.05):
    count = len(args) + (place is not None)

    def body(*refs):
        kernel(*refs[:count], *refs[count + len(deps) :])

    single = not isinstance(out, list)
    specs = whole(*([out] if single else out))
    return pl.pallas_call(
        body,
        grid=(1,),
        in_specs=[SMEM] * (place is not None) + whole(*args) + [HBM] * len(deps),
        out_specs=specs[0] if single else specs,
        out_shape=out,
        compiler_params=params(),
        cost_estimate=cost(micros),
        name=name,
    )(*([place] if place is not None else []), *args, *deps)


def add_kernel(a_ref, b_ref, out_ref):
    out_ref[...] = (a_ref[...].astype(F32) + b_ref[...].astype(F32)).astype(BF16)


def add(a, b, deps=()):
    return simple(add_kernel, "add", shape(a.shape, BF16), (a, b), deps=deps)


def stack_kernel(*refs):
    for at, ref in enumerate(refs[:-1]):
        refs[-1][at] = ref[...]


def stack(parts, deps=()):
    out = shape((len(parts),) + parts[0].shape, BF16)
    return simple(stack_kernel, "stack", out, parts, deps=deps)


def both_halves(own, got, first):
    return jnp.where(first, own, got), jnp.where(first, got, own)


def keep_and_send(values, core, keep_ref, send_ref):
    half = values.shape[0] // 2
    first, second = values[:half], values[half:]
    keep_ref[...] = jnp.where(core == 0, first, second)
    send_ref[...] = jnp.where(core == 0, second, first)


def params(mib=VMEM_MIB):
    return pltpu.CompilerParams(
        vmem_limit_bytes=mib * MIB, dimension_semantics=("arbitrary",)
    )


def cost(micros):
    return pl.CostEstimate(flops=int(micros * 1.1e9), bytes_accessed=int(micros * 1e5), transcendentals=0)


def contract_rows(left, right):
    return lax.dot_general(
        left, right, (((0,), (0,)), ((), ())), preferred_element_type=jnp.float32
    )


def contract_cols(left, right):
    return lax.dot_general(
        left, right, (((1,), (1,)), ((), ())), preferred_element_type=jnp.float32
    )


def count_edges(magnitude, edge_list):
    result = jnp.zeros(magnitude.shape, jnp.int32)
    for border in edge_list:
        result = result + (magnitude >= border).astype(jnp.int32)
    return result


def box_cell(offset):
    half = jnp.abs(offset) >> 1
    cell = jnp.where(half < 32, half, (half >> 4) + 30)
    return cell + jnp.where(offset > 0, 64, 0)


def cell_bucket(cell):
    low = cell & 63
    half = jnp.where(low < 32, low, (low - 30) << 4)
    return count_edges(half * 2, BOX_EDGES) + jnp.where(cell >= 64, 16, 0)


def lookup(table, index):
    return jnp.take_along_axis(table, index, axis=1, mode="promise_in_bounds")


SMALL = 16


def pack_kernel(
    place_ref, seg_hbm, box_hbm, one_hbm, two_hbm, table_hbm, query_hbm, key_hbm, value_hbm, gate_hbm, up_hbm, down_hbm, early_ref, late_ref, *rest
):
    refs, sems = rest[:-1], rest[-1]
    units = gate_hbm.shape[0] // 4
    mine = pl.ds(pl.multiple_of(place_ref[2] * units, 16), units)
    sources = [seg_hbm, box_hbm, one_hbm, two_hbm, table_hbm, query_hbm, key_hbm, value_hbm]
    copies = [pltpu.make_async_copy(src, dst, sems.at[at]) for at, (src, dst) in enumerate(zip(sources, refs))]
    for at, src in enumerate((gate_hbm, up_hbm, down_hbm)):
        spot = late_ref.at[at * units : (at + 1) * units, :]
        copies.append(pltpu.make_async_copy(src.at[mine, :], spot, sems.at[len(sources) + at]))
    for copy in copies:
        copy.start()
    for copy in copies:
        copy.wait()
    seg_ref, box_ref, one_ref, two_ref, table_ref, query_ref, key_ref, value_ref = refs
    width = seg_ref.shape[1]
    pair = query_ref.shape[1] // 2
    row = lax.broadcasted_iota(jnp.int32, (SMALL, width), 0)
    boxes = box_ref[...]
    centre_x = boxes[0:1] + boxes[2:3]
    centre_y = boxes[1:2] + boxes[3:4]
    gains = jnp.concatenate([one_ref[...], two_ref[...]], axis=1).astype(F32)
    small = table_ref[...].astype(F32)
    for at, values in enumerate(
        (seg_ref[...], centre_x >> 8, centre_x & 255, centre_y >> 8, centre_y & 255, gains)
    ):
        small = jnp.where(row == at, values.astype(F32), small)
    small = small.astype(BF16)
    small = jnp.concatenate([small, jnp.zeros((SMALL, 3 * pair - width), BF16)], axis=1)
    for block in range(early_ref.shape[0]):
        half = block // 4
        cols = slice(half * pair, (half + 1) * pair)
        for at, ref in enumerate((query_ref, key_ref, value_ref)):
            early_ref[block, :LANES, at * pair : (at + 1) * pair] = ref[:, cols]
        early_ref[block, LANES:, :] = small


def pack(place, small, weights, late):
    pair = weights[0].shape[1] // 2
    args = small + weights
    out = [
        shape((8, LANES + SMALL, 3 * pair), BF16),
        shape((3 * late[0].shape[0] // 4, LANES), BF16),
    ]
    return pl.pallas_call(
        pack_kernel,
        grid=(1,),
        in_specs=[SMEM] + [HBM] * (len(args) + 3),
        out_specs=whole(*out),
        out_shape=out,
        scratch_shapes=[pltpu.VMEM(item.shape, item.dtype) for item in args]
        + [pltpu.SemaphoreType.DMA((len(args) + 3,))],
        compiler_params=params(64),
        cost_estimate=cost(0.05),
        name="pack",
    )(place, *args, *late)


def unfold_rows(values):
    return jnp.concatenate(jnp.split(values, 4, axis=0), axis=1)


def fold_rows(values):
    return jnp.concatenate(jnp.split(values, 4, axis=1), axis=0)


def project_kernel(
    place_ref, early_ref, own_ref, other_ref, out_w_ref, normed_ref, query_ref, pair_ref, gain_ref, key_ref, meta_ref, table_ref
):
    rows, model = own_ref.shape
    pair = query_ref.shape[1]
    side, depth = place_ref[0], place_ref[1]
    small = [early_ref[block, LANES:, :rows].astype(F32) for block in range(8)]
    for at in range(2):
        lanes = slice(at * LANES, (at + 1) * LANES)
        gain = jnp.concatenate([part[5:6, lanes] for part in small], axis=1)
        gain_ref[at : at + 1, :] = gain
        if at == 0:
            gain_one = gain

    out_w_other = fold_rows(other_ref[rows:, :])
    for values, half in ((out_w_ref[...], side), (out_w_other, 1 - side)):
        here = pl.ds(pl.multiple_of(2 * rows + half * LANES, LANES), LANES)
        for copy in range(4):
            pair_ref[copy, here, :] = values
    weight = jnp.concatenate([early_ref[block, :LANES, :] for block in range(8)], axis=0)
    for ref, half in ((own_ref, side), (other_ref, 1 - side)):
        inputs = ref[:rows, :].astype(F32)
        scale = lax.rsqrt(jnp.mean(inputs * inputs, axis=1, keepdims=True) + EPS)
        normed = (inputs * scale * gain_one).astype(BF16)
        here = pl.ds(pl.multiple_of(half * rows, rows), rows)
        normed_ref[here, :] = normed
        result = jnp.dot(normed, weight, preferred_element_type=F32).astype(BF16)
        query_ref[here, :] = result[:, :pair] * jnp.asarray(HEAD_DIM ** (-0.5), BF16)
        for copy in range(4):
            pair_ref[copy, here, :] = result[:, pair:]

    time = lax.broadcasted_iota(jnp.int32, (1, rows), 1)
    for block in range(8):
        part = small[block]
        at = (block % 4) * 2 + block // 4
        there = slice(at * rows, (at + 1) * rows)
        key_ref[0:1, there] = part[0:1].astype(jnp.int32)
        key_ref[1:2, there] = (part[1:2] * 256.0 + part[2:3]).astype(jnp.int32)
        key_ref[2:3, there] = (part[3:4] * 256.0 + part[4:5]).astype(jnp.int32)
        for half in range(2):
            ahead = (block - depth - 4 * half) * rows + SEQ_SPAN // 4
            key_ref[3 + half : 4 + half, there] = jnp.clip(time + ahead, 0, SEQ_SPAN - 1)
        key_ref[5:8, there] = jnp.zeros((3, rows), jnp.int32)

    for half in range(2):
        part = early_ref[depth + 4 * half, LANES:, :rows].astype(F32)
        columns = jnp.transpose(part)
        seg = columns[:, 0:1]
        centre_x = columns[:, 1:2] * 256.0 + columns[:, 2:3]
        centre_y = columns[:, 3:4] * 256.0 + columns[:, 4:5]
        for at, values in enumerate((seg, centre_x, centre_y)):
            wide = jnp.broadcast_to(values.astype(jnp.int32), (rows, LANES))
            meta_ref[at, half * rows : (half + 1) * rows, :] = wide

    lane = lax.broadcasted_iota(jnp.int32, (8, LANES), 1)
    table = jnp.zeros((8, LANES), F32)
    for block in range(8):
        entries = jnp.where(side == 0, small[block][6:8, :LANES], small[block][8:10, :LANES])
        entries = jnp.concatenate([entries, jnp.zeros((6, LANES), F32)], axis=0)
        index = jnp.clip(lane - 12 * block, 0, LANES - 1)
        found = lookup(entries, index)
        table = jnp.where((lane >= 12 * block) & (lane < 12 * block + 12), found, table)
    table_ref[...] = table


def project(place, early, own, other, out_w, deps):
    rows, model = own.shape
    pair = early.shape[2] // 3
    out = [
        shape((2 * rows, model), BF16),
        shape((2 * rows, pair), BF16),
        shape((4, 2 * rows + 2 * LANES, 2 * pair), BF16),
        shape((2, model), F32),
        shape((8, 8 * rows), jnp.int32),
        shape((3, 2 * rows, LANES), jnp.int32),
        shape((8, LANES), F32),
    ]
    return simple(
        project_kernel, "project", out, (early, own, other, out_w), place, deps
    )


STEPS = 3600.0
SHIFT = 10800.0
MASKED = -(2**31)


def bias_kernel(place_ref, meta_ref, key_ref, table_ref, *refs):
    bias_ref = refs[-1]
    chunk, length = bias_ref.shape
    width = TOKENS_BLOCK
    step = pl.program_id(0)
    half = step // (2 * width // chunk // 2)
    first_row = lax.rem(step * chunk, width)
    query_block = place_ref[1] + 4 * half
    lane = lax.broadcasted_iota(jnp.int32, (8, LANES), 1)
    buckets = cell_bucket(lane)
    table = table_ref[...]

    def packed(index):
        found = lookup(table, index)
        high = jnp.round(found[0:1, :] * STEPS).astype(jnp.int32)
        low = jnp.round(found[1:2, :] * STEPS + SHIFT).astype(jnp.int32)
        return (high << 16) + low

    def spread(values):
        return jnp.broadcast_to(values, (chunk, LANES))

    hor = packed(buckets + 32)
    ver = spread(packed(buckets + 64))
    seq_count = count_edges(jnp.abs(lane - 64), SEQ_EDGES) + jnp.where(lane > 64, 16, 0)
    seq = spread(packed(seq_count))
    behind, middle, beyond = [packed(jnp.full((8, LANES), at, jnp.int32)) for at in (15, 30, 31)]

    def key_block(at):
        return at // 2 + 4 * lax.rem(at, 2)

    def block_of_keys(at, with_near):
        ahead = key_block(at) * width - query_block * width - first_row
        far = spread(hor if with_near else hor + jnp.where(ahead > 0, beyond, behind))
        for column in range(width // LANES):
            there = pl.ds(pl.multiple_of(at * width + column * LANES, LANES), LANES)
            keys = key_ref[:, there]
            total = lookup(far, box_cell(keys[1:2, :] - meta_ref[1]))
            total = total + lookup(ver, box_cell(keys[2:3, :] - meta_ref[2]))
            if with_near:
                row = lax.broadcasted_iota(jnp.int32, (chunk, LANES), 0)
                col = lax.broadcasted_iota(jnp.int32, (chunk, LANES), 1)
                offset = col - row + (ahead + column * LANES)
                found = lookup(seq, jnp.clip(offset + 64, 0, LANES - 1))
                found = jnp.where(offset >= 64, middle, found)
                found = jnp.where(offset >= 91, beyond, found)
                total = total + jnp.where(offset <= -91, behind, found)
            bias_ref[:, there] = jnp.where(keys[0:1, :] == meta_ref[0], total, MASKED)

    def body(at, carry):
        near = jnp.abs(key_block(at) - query_block) <= 1
        pl.when(near)(functools.partial(block_of_keys, at, True))
        pl.when(jnp.logical_not(near))(functools.partial(block_of_keys, at, False))
        return carry

    lax.fori_loop(0, length // width, body, 0)


TOKENS_BLOCK = 256


def bias_scores(place, meta, key_meta, table, deps):
    rows = meta.shape[1]
    length = key_meta.shape[1]
    chunk = 128
    return pl.pallas_call(
        bias_kernel,
        grid=(rows // chunk,),
        in_specs=[
            pl.BlockSpec(memory_space=pltpu.SMEM),
            pl.BlockSpec((3, chunk, LANES), lambda s: (0, s, 0)),
            pl.BlockSpec((8, length), lambda s: (0, 0)),
            pl.BlockSpec((8, LANES), lambda s: (0, 0)),
        ]
        + [HBM] * len(deps),
        out_specs=pl.BlockSpec((chunk, length), lambda s: (s, 0)),
        out_shape=jax.ShapeDtypeStruct((rows, length), jnp.int32),
        compiler_params=params(),
        cost_estimate=cost(10),
        name="bias_scores",
    )(place, meta, key_meta, table, *deps)


def head_masks(shape):
    lane = lax.broadcasted_iota(jnp.int32, shape, 1)
    return lane < HEAD_DIM, lane >= HEAD_DIM


def attend_kernel(place_ref, query_ref, bias_ref, pair_ref, *refs):
    probs_ref, exact_ref, mine_ref, other_ref = refs[-4:]
    count, _, both = pair_ref.shape
    width = bias_ref.shape[1] // count
    features = both // 2
    rows = query_ref.shape[0]
    masks = head_masks((rows, features))
    query = query_ref[...]
    allowed = []
    codes = []
    for at in range(count):
        code = bias_ref[:, at * width : (at + 1) * width]
        codes.append(code)
        allowed.append(code != MASKED)
    outs = []
    for head in range(2):
        mine = jnp.where(masks[head], query, jnp.zeros_like(query))
        scores = []
        for at in range(count):
            code = (codes[at] >> 16) if head == 0 else (codes[at] & 65535)
            score = contract_cols(mine, pair_ref[at, :width, :features])
            score = score + code.astype(F32) * (1.0 / STEPS)
            scores.append(jnp.where(allowed[at], score, -1e30))
        top = functools.reduce(jnp.maximum, scores)
        top = jnp.max(top, axis=1, keepdims=True)
        weights = [jnp.exp(score - top) for score in scores]
        total = functools.reduce(jnp.add, weights)
        inverse = 1.0 / jnp.sum(total, axis=1, keepdims=True)
        result = None
        for at in range(count):
            low = (weights[at] * inverse).astype(BF16)
            probs_ref[head, :, at * width : (at + 1) * width] = low
            part = jnp.dot(low, pair_ref[at, :width, features:], preferred_element_type=F32)
            result = part if result is None else result + part
        outs.append(result)
    exact = jnp.where(masks[0], outs[0], outs[1])
    exact_ref[...] = exact
    low = exact.astype(BF16)
    tiles = mine_ref.shape[0] // rows
    step = pl.program_id(0)
    here = pl.ds(pl.multiple_of(lax.rem(step, tiles) * rows, rows), rows)
    own = step // tiles == place_ref[0]

    @pl.when(own)
    def _():
        mine_ref[here, :] = low

    @pl.when(jnp.logical_not(own))
    def _():
        other_ref[here, :] = low


def attend(place, queries, pairs, bias, deps):
    rows, length = bias.shape
    both = pairs.shape[2]
    tile = 128
    features = both // 2
    slim = pl.BlockSpec((tile, features), lambda s: (s, 0))
    half = shape((rows // 2, features), BF16)
    return pl.pallas_call(
        attend_kernel,
        grid=(rows // tile,),
        in_specs=[SMEM, slim, pl.BlockSpec((tile, length), lambda s: (s, 0))]
        + whole(pairs)
        + [HBM] * len(deps),
        out_specs=[pl.BlockSpec((2, tile, length), lambda s: (0, s, 0)), slim] + whole(half, half),
        out_shape=[
            shape((2, rows, length), BF16),
            shape((rows, features), F32),
            half,
            half,
        ],
        compiler_params=params(),
        cost_estimate=cost(9),
        name="attend",
    )(place, queries, bias, pairs, *deps)


def out_weight(pair_ref):
    start = pair_ref.shape[1] - 2 * LANES
    parts = []
    for block in range(8):
        first = start + block // 4 * LANES
        parts.append(pair_ref[block % 4, first : first + LANES, :])
    return jnp.concatenate(parts, axis=0)


def branch_kernel(place_ref, mine_ref, got_ref, pair_ref, keep_ref, send_ref):
    parts = both_halves(mine_ref[...], got_ref[...], place_ref[0] == 0)
    attended = jnp.concatenate(parts, axis=1)
    result = contract_cols(attended, out_weight(pair_ref)).astype(BF16)
    keep_and_send(result, place_ref[3], keep_ref, send_ref)


def branch_part(place, mine, got, pairs, deps):
    half = shape((mine.shape[0] // 2, 8 * LANES), BF16)
    return simple(branch_kernel, "branch_part", [half, half], (mine, got, pairs), place, deps, 2)


def gelu_parts(gate):
    rate = 0.7978845608028654
    square = gate * gate
    slope = jnp.tanh(rate * gate * (1.0 + 0.044715 * square))
    half = 0.5 * (1.0 + slope)
    inner = rate * (1.0 + 3.0 * 0.044715 * square)
    return gate * half, half + 0.5 * gate * (1.0 - slope * slope) * inner


def piece_copies(place_ref, piece_refs, held, sems, hop, first):
    side, depth = place_ref[0], place_ref[1]
    height = held.shape[1]
    copies = []
    for far in range(2):
        for turn in range(4):
            block = (side + far * (1 - 2 * side)) * 4 + lax.rem(depth + turn, 4)
            lanes = pl.ds(pl.multiple_of(block * LANES, LANES), LANES)
            copies.append(
                pltpu.make_async_copy(
                    piece_refs[2 * hop + far].at[turn, pl.ds(first, height), :],
                    held.at[hop, :, lanes],
                    sems.at[hop, 4 * far + turn],
                )
            )
    return copies


def ffn_prepare_kernel(place_ref, dy_ref, *refs):
    piece_refs, (weight_ref, grad_ref, sems) = refs[:8], refs[8:]
    copies = [piece_copies(place_ref, piece_refs, weight_ref, sems, hop, 0) for hop in range(4)]
    units = weight_ref.shape[1] // 3
    for group in copies:
        for copy in group:
            copy.start()
    for hop in range(4):
        for copy in copies[hop]:
            copy.wait()
        grad_ref[hop] = contract_cols(weight_ref[hop, 2 * units :, :], dy_ref[...])


def ffn_prepare(place, dy, pieces):
    rows, model = dy.shape
    height = pieces[0].shape[1]
    out = [shape((4, height, model), BF16), shape((4, height // 3, rows), F32)]
    return pl.pallas_call(
        ffn_prepare_kernel,
        grid=(1,),
        in_specs=[SMEM] + whole(dy) + [HBM] * 8,
        out_specs=whole(*out),
        out_shape=out,
        scratch_shapes=[pltpu.SemaphoreType.DMA((4, 8))],
        compiler_params=params(),
        cost_estimate=cost(4),
        name="ffn_prepare",
    )(place, dy, *pieces)


def middle_of(tokens_ref, total_ref, got_ref, core):
    branch = jnp.concatenate(both_halves(total_ref[...], got_ref[...], core == 0), axis=0)
    return tokens_ref[...].astype(F32) + branch.astype(F32)


def rms_scale(values):
    return lax.rsqrt(jnp.mean(values * values, axis=1, keepdims=True) + EPS)


def ffn_kernel(
    place_ref, tokens_ref, total_ref, got_ref, gain_ref, hidden_grad_ref, weight_ref, normed_ref, parts_ref, keep_ref, send_ref, sums, turned
):
    units = weight_ref.shape[1] // 2
    step = pl.program_id(0)

    @pl.when(step == 0)
    def _():
        middle = middle_of(tokens_ref, total_ref, got_ref, place_ref[3])
        normed = (middle * rms_scale(middle) * gain_ref[1:2, :]).astype(BF16)
        normed_ref[...] = normed
        turned[...] = jnp.transpose(normed)
        sums[...] = jnp.zeros_like(sums)

    gates = jnp.dot(weight_ref[0], turned[...], preferred_element_type=F32)
    gate, upward = gates[:units], gates[units:]
    hidden_grad = hidden_grad_ref[0]
    value, slope = gelu_parts(gate)
    grads = jnp.concatenate([hidden_grad * upward * slope, hidden_grad * value], axis=0).astype(BF16)
    parts_ref[0, : 2 * units, :] = grads
    parts_ref[0, 2 * units :, :] = (value * upward).astype(BF16)
    sums[...] += contract_rows(grads, weight_ref[0])

    @pl.when(step == pl.num_programs(0) - 1)
    def _():
        keep_and_send(sums[...].astype(BF16), place_ref[3], keep_ref, send_ref)


def ffn_forward(place, tokens, total, got, gains, hidden_grad, weights):
    rows, model = tokens.shape
    hops, height, _ = weights.shape
    half = shape((rows // 2, model), BF16)
    out = [shape((rows, model), BF16), shape((hops, height, rows), BF16), half, half]

    def chunk(item):
        return pl.BlockSpec((1,) + item.shape[1:], lambda s: (s, 0, 0))

    return pl.pallas_call(
        ffn_kernel,
        grid=(hops,),
        in_specs=[SMEM]
        + whole(tokens, total, got, gains)
        + [chunk(hidden_grad), pl.BlockSpec((1, height // 3 * 2, model), lambda s: (s, 0, 0))],
        out_specs=whole(out[0]) + [chunk(out[1])] + whole(half, half),
        out_shape=out,
        scratch_shapes=[pltpu.VMEM((rows, model), F32), pltpu.VMEM((model, rows), BF16)],
        compiler_params=params(),
        cost_estimate=cost(5),
        name="ffn_forward",
    )(place, tokens, total, got, gains, hidden_grad, weights)


def ffn_back_kernel(place_ref, parts_ref, normed_ref, dy_ref, *refs):
    grad_ref = refs[-1]
    units = parts_ref.shape[1] // 3
    grad_ref[0, : 2 * units, :] = jnp.dot(
        parts_ref[0, : 2 * units, :], normed_ref[...], preferred_element_type=F32
    ).astype(BF16)
    grad_ref[0, 2 * units :, :] = jnp.dot(
        parts_ref[0, 2 * units :, :], dy_ref[...], preferred_element_type=F32
    ).astype(BF16)


def ffn_output_kernel(place_ref, parts_ref, weight_ref, *refs):
    keep_ref, send_ref, sums = refs[-3:]
    step = pl.program_id(0)
    part = contract_rows(parts_ref[0], weight_ref[0])

    @pl.when(step == 0)
    def _():
        sums[...] = part

    @pl.when(step > 0)
    def _():
        sums[...] += part

    @pl.when(step == pl.num_programs(0) - 1)
    def _():
        keep_and_send(sums[...].astype(BF16), place_ref[3], keep_ref, send_ref)


def ffn_output(place, parts, weights, deps):
    hops, height, rows = parts.shape
    model = weights.shape[2]
    half = shape((rows // 2, model), BF16)
    return pl.pallas_call(
        ffn_output_kernel,
        grid=(hops,),
        in_specs=[
            SMEM,
            pl.BlockSpec((1, height // 3, rows), lambda s: (s, 2, 0)),
            pl.BlockSpec((1, height // 3, model), lambda s: (s, 2, 0)),
        ]
        + [HBM] * len(deps),
        out_specs=whole(half, half),
        out_shape=[half, half],
        scratch_shapes=[pltpu.VMEM((rows, model), F32)],
        compiler_params=params(),
        cost_estimate=cost(3),
        name="ffn_output",
    )(place, parts, weights, *deps)


def norm_back(inputs, gain, normed_grad):
    scale = rms_scale(inputs)
    gain_grad = jnp.sum(normed_grad * inputs * scale, axis=0, keepdims=True)
    weighted = normed_grad * gain
    mean = jnp.mean(weighted * inputs, axis=1, keepdims=True)
    return scale * weighted - inputs * (scale * scale * scale) * mean, gain_grad


def middle_kernel(
    place_ref, tokens_ref, total_ref, got_ref, dy_ref, gain_ref, grad_ref, grad_got_ref, pair_ref, middle_ref, low_ref, two_ref, mine_ref, other_ref
):
    core = place_ref[3]
    middle = middle_of(tokens_ref, total_ref, got_ref, core)
    parts = both_halves(grad_ref[...], grad_got_ref[...], core == 0)
    normed_grad = jnp.concatenate(parts, axis=0).astype(F32)
    result, gain_grad = norm_back(middle, gain_ref[1:2, :], normed_grad)
    result = dy_ref[...].astype(F32) + result
    middle_ref[...] = result
    low = result.astype(BF16)
    low_ref[...] = low
    two_ref[...] = gain_grad
    attended = jnp.dot(low, out_weight(pair_ref), preferred_element_type=F32).astype(BF16)
    pair = attended.shape[1] // 2
    first = place_ref[0] == 0
    mine_ref[...] = jnp.where(first, attended[:, :pair], attended[:, pair:])
    other_ref[...] = jnp.where(first, attended[:, pair:], attended[:, :pair])


def middle_back(place, tokens, total, got, dy, gains, grad, grad_got, pairs):
    rows, model = tokens.shape
    half = shape((rows, pairs.shape[2] // 2), BF16)
    out = [shape((rows, model), F32), shape((rows, model), BF16), shape((1, model), F32), half, half]
    args = (tokens, total, got, dy, gains, grad, grad_got, pairs)
    return simple(middle_kernel, "middle_back", out, args, place, micros=3)


def tokens_kernel(place_ref, tokens_ref, gain_ref, grad_ref, grad_got_ref, middle_ref, out_ref):
    parts = both_halves(grad_ref[...], grad_got_ref[...], place_ref[3] == 0)
    normed_grad = jnp.concatenate(parts, axis=0).astype(F32)
    result, _ = norm_back(tokens_ref[...].astype(F32), gain_ref[0:1, :], normed_grad)
    out_ref[...] = middle_ref[...] + result


def tokens_back(place, tokens, gains, grad, grad_got, middle_grad):
    out = shape(tokens.shape, F32)
    return simple(
        tokens_kernel, "tokens_back", out, (tokens, gains, grad, grad_got, middle_grad), place, micros=2
    )


def mixed_kernel(place_ref, tokens_ref, total_ref, got_ref, out_total_ref, out_got_ref, out_ref):
    core = place_ref[3]
    middle = middle_of(tokens_ref, total_ref, got_ref, core)
    parts = both_halves(out_total_ref[...], out_got_ref[...], core == 0)
    out_ref[...] = (middle + jnp.concatenate(parts, axis=0).astype(F32)).astype(BF16)


HOPS = (0, 1, 3, 2)


def ffn_back(place, parts, normed, dy, deps):
    rows, model = normed.shape
    hops, height, _ = parts.shape

    def owner(step, place_ref):
        hop = jnp.where(step == 0, 0, jnp.where(step == 1, 1, jnp.where(step == 2, 3, 2)))
        return lax.rem(place_ref[2] - hop + 4, 4)

    def same(*arrays):
        return [pl.BlockSpec(item.shape, lambda s, p: (0, 0)) for item in arrays]

    return pl.pallas_call(
        ffn_back_kernel,
        grid_spec=pltpu.PrefetchScalarGridSpec(
            num_scalar_prefetch=1,
            grid=(hops,),
            in_specs=[pl.BlockSpec((1, height, rows), lambda s, p: (s, 0, 0))]
            + same(normed, dy)
            + [HBM] * len(deps),
            out_specs=pl.BlockSpec((1, height, model), lambda s, p: (owner(s, p), 0, 0)),
        ),
        out_shape=shape((hops, height, model), BF16),
        compiler_params=params(),
        cost_estimate=cost(4),
        name="ffn_back",
    )(place, parts, normed, dy, *deps)


def fold_kernel(place_ref, parts_ref, *refs):
    out_ref = refs[-1]
    for block in range(4):
        lanes = slice(block * LANES, (block + 1) * LANES)
        total = parts_ref[0, :, lanes].astype(F32)
        for at in range(1, parts_ref.shape[0]):
            total = total + parts_ref[at, :, lanes].astype(F32)
        out_ref[0, lax.rem(block - place_ref[1] + 4, 4)] = total.astype(BF16)


def fold_to_blocks(place, parts, deps):
    count, height, model = parts.shape
    return pl.pallas_call(
        fold_kernel,
        grid_spec=pltpu.PrefetchScalarGridSpec(
            num_scalar_prefetch=1,
            grid=(2,),
            in_specs=[pl.BlockSpec((count, height, model // 2), lambda s, p: (0, 0, s))]
            + [HBM] * len(deps),
            out_specs=pl.BlockSpec(
                (1, 4, height, LANES), lambda s, p: (jnp.where(s == p[0], 0, 1), 0, 0, 0)
            ),
        ),
        out_shape=shape((2, 4, height, LANES), BF16),
        compiler_params=params(),
        cost_estimate=cost(4),
        name="fold_to_blocks",
    )(place, parts, *deps)


def attend_back_kernel(place_ref, query_ref, mine_ref, got_ref, exact_ref, probs_ref, pair_ref, *refs):
    score_ref, pair_grad_refs = refs[-9], refs[-8:-4]
    query_grad_ref, sums, delta, grads = refs[-4:]
    _, rows, width = probs_ref.shape
    features = query_ref.shape[1]
    step = pl.program_id(0)
    masks = head_masks((rows, features))
    query = query_ref[...]

    @pl.when(step == 0)
    def _():
        sums[...] = jnp.zeros_like(sums)
        parts = both_halves(mine_ref[...], got_ref[...], place_ref[0] == 0)
        grads[...] = jnp.concatenate(parts, axis=0)
        product = grads[...].astype(F32) * exact_ref[...]
        for head in range(2):
            row = jnp.sum(jnp.where(masks[head], product, 0.0), axis=1, keepdims=True)
            delta[head] = jnp.broadcast_to(row, (rows, LANES))

    grad = grads[...]
    keys = pair_ref[0, :, :features]
    values = pair_ref[0, :, features:]
    parts = []
    key_grads = []
    value_grads = []
    for head in range(2):
        cols = slice(head * HEAD_DIM, (head + 1) * HEAD_DIM)
        mine = jnp.where(masks[head], grad, jnp.zeros_like(grad))
        probs = probs_ref[head]
        prob_grad = contract_cols(mine, values)
        offset = jnp.concatenate([delta[head]] * (width // LANES), axis=1)
        score_grad = (probs.astype(F32) * (prob_grad - offset)).astype(BF16)
        score_ref[head] = score_grad
        parts.append(jnp.dot(score_grad, keys, preferred_element_type=F32))
        key_grads.append(contract_rows(query[:, cols], score_grad).astype(BF16))
        value_grads.append(contract_rows(grad[:, cols], probs).astype(BF16))
    for at in range(4):

        @pl.when(step == at)
        def _():
            for spot, part in enumerate(key_grads + value_grads):
                pair_grad_refs[at][spot * HEAD_DIM : (spot + 1) * HEAD_DIM, :] = part

    sums[...] += jnp.where(masks[0], parts[0], parts[1])

    @pl.when(step == pl.num_programs(0) - 1)
    def _():
        query_grad_ref[...] = (sums[...] * HEAD_DIM ** (-0.5)).astype(BF16)


def attend_back(place, queries, mine, got, exact, pairs, probs, deps):
    _, rows, length = probs.shape
    features = queries.shape[1]
    width, both = rows, pairs.shape[2]

    def spot(step, place_ref):
        return lax.rem(place_ref[1] + step, 4)

    def same(*arrays):
        return [pl.BlockSpec(item.shape, lambda s, p: (0, 0)) for item in arrays]

    slab = pl.BlockSpec((2, rows, width), lambda s, p: (0, 0, spot(s, p)))
    pair_grads = [shape((both, width), BF16)] * 4
    query_grad = shape((rows, features), BF16)
    return pl.pallas_call(
        attend_back_kernel,
        grid_spec=pltpu.PrefetchScalarGridSpec(
            num_scalar_prefetch=1,
            grid=(4,),
            in_specs=same(queries, mine, got, exact)
            + [slab, pl.BlockSpec((1, width, both), lambda s, p: (spot(s, p), 0, 0))]
            + [HBM] * len(deps),
            out_specs=[slab] + same(*pair_grads, query_grad),
            scratch_shapes=[
                pltpu.VMEM((rows, features), F32),
                pltpu.VMEM((2, rows, LANES), F32),
                pltpu.VMEM((rows, features), BF16),
            ],
        ),
        out_shape=[shape((2, rows, length), BF16)] + pair_grads + [query_grad],
        compiler_params=params(),
        cost_estimate=cost(4),
        name="attend_back",
    )(place, queries, mine, got, exact, probs, pairs, *deps)


BOX_SPAN = 1024
SEQ_SPAN = 512
TILE = 512


def threshold_row(edge_list, far, lane):
    borders = [-far] + [1 - edge for edge in reversed(edge_list)] + [1] + list(edge_list)
    result = jnp.zeros(lane.shape, jnp.int32)
    for at, border in enumerate(borders):
        result = jnp.where(lane == at, border, result)
    return result


def table_grad_kernel(meta_ref, key_ref, score_ref, *refs):
    out_ref, sums_ref = refs[-2:]
    _, rows, length = score_ref.shape
    half = rows // 2
    step = pl.program_id(0)
    lane = lax.broadcasted_iota(jnp.int32, (1, LANES), 1)
    level = lax.broadcasted_iota(jnp.int32, (TILE, 1), 0)

    def add(place, key_row, mine, edges, top, offset, span):
        index = jnp.clip(mine + threshold_row(edges, 4096, lane), 0, top)
        column = index & (LANES - 1)
        block = (index - offset) >> 7
        reached = (key_ref[pl.ds(key_row, 1), :] >= level + offset).astype(F32).astype(BF16)
        for head in range(2):
            sums = contract_cols(score_ref[head, span, :], reached)
            picked = jnp.zeros(column.shape, F32)
            for at in range(TILE // LANES):
                found = lookup(sums[:, at * LANES : (at + 1) * LANES], column)
                picked = picked + jnp.where(block == at, found, 0.0)
            sums_ref[place, head : head + 1, :] += jnp.sum(picked, axis=0, keepdims=True)

    @pl.when(step == 0)
    def _():
        sums_ref[...] = jnp.zeros_like(sums_ref)

    @pl.when(step < 4)
    def _():
        axis = step // 2
        mine = meta_ref[1 + axis]
        add(1 + axis, 1 + axis, mine, BOX_EDGES, BOX_SPAN - 1, (step % 2) * TILE, slice(None))

    @pl.when(step >= 4)
    def _():
        part = step - 4
        span = pl.ds(pl.multiple_of(part * half, half), half)
        mine = lax.broadcasted_iota(jnp.int32, (half, LANES), 0) + SEQ_SPAN // 4
        add(0, 3 + part, mine, SEQ_EDGES, SEQ_SPAN - 1, 0, span)

    @pl.when(step == pl.num_programs(0) - 1)
    def _():
        lanes = lax.broadcasted_iota(jnp.int32, (8, LANES), 1)
        bucket = lanes & 31
        first = jnp.where(bucket < 16, 15 - bucket, bucket)
        result = jnp.zeros((8, LANES), F32)
        for axis in range(3):
            sums = sums_ref[axis]
            part = lookup(sums, first) - jnp.where(first == 31, 0.0, lookup(sums, first + 1))
            result = jnp.where((lanes >> 5) == axis, part, result)
        out_ref[...] = result


def table_grad_sums(meta, key_meta, score_grad, deps):
    _, rows, length = score_grad.shape
    return pl.pallas_call(
        table_grad_kernel,
        grid=(6,),
        in_specs=whole(meta, key_meta, score_grad) + [HBM] * len(deps),
        out_specs=pl.BlockSpec((8, LANES), lambda s: (0, 0)),
        out_shape=shape((8, LANES), F32),
        scratch_shapes=[pltpu.VMEM((3, 8, LANES), F32)],
        compiler_params=params(),
        cost_estimate=cost(8),
        name="table_grad",
    )(meta, key_meta, score_grad, *deps)


def weight_grads_kernel(
    place_ref, query_ref, normed_ref, early_ref, gain_ref, mine_ref, got_ref, low_ref, two_ref, table_ref, *refs
):
    pair_refs, (bundle_ref, small_ref, one_ref, keep_ref, send_ref) = refs[:4], refs[4:]
    side, core = place_ref[0], place_ref[3]
    attended = jnp.concatenate(both_halves(mine_ref[...], got_ref[...], side == 0), axis=1)
    grad_out = contract_rows(attended, low_ref[...]).astype(BF16)
    total = pair_refs[0][...].astype(F32)
    for ref in pair_refs[1:]:
        total = total + ref[...].astype(F32)
    low = total.astype(BF16)
    query = query_ref[...]
    normed = normed_ref[...]
    pair = query.shape[1]
    grad_query = contract_rows(query, normed).astype(BF16)
    grad_pair = jnp.dot(low, normed, preferred_element_type=F32).astype(BF16)
    bundle_ref[:pair, :] = grad_query
    bundle_ref[pair : 3 * pair, :] = grad_pair
    bundle_ref[3 * pair : 5 * pair, :] = grad_out
    triple = jnp.concatenate([query, jnp.transpose(low)], axis=1)
    row = lax.broadcasted_iota(jnp.int32, (SMALL, LANES), 0)
    lane = lax.broadcasted_iota(jnp.int32, (8, LANES), 1)
    table = table_ref[...]
    for block in range(8):
        lanes = slice(block * LANES, (block + 1) * LANES)
        partial = contract_cols(triple, early_ref[block, :LANES, :])
        sides = both_halves(*jnp.split(partial.astype(BF16), 2, axis=0), side == 0)
        half = sides[0].shape[0] // 2
        for far in range(2):
            first, second = sides[far][:half], sides[far][half:]
            keep_ref[far, :, lanes] = jnp.where(core == 0, first, second)
            send_ref[far, :, lanes] = jnp.where(core == 0, second, first)
        one = jnp.sum(partial * normed[:, lanes].astype(F32), axis=0, keepdims=True)
        one_ref[:, lanes] = jnp.where(row == 0, one / gain_ref[0:1, lanes], 0.0).astype(BF16)
        extra = jnp.where(row == 1, two_ref[:, lanes], 0.0)
        part = lookup(table, jnp.minimum(lane + 12 * block, LANES - 1))
        for head in range(2):
            extra = jnp.where(row == 2 + head + 2 * side, part[head : head + 1], extra)
        small_ref[:, lanes] = extra.astype(BF16)


def weight_grads(place, pair_parts, query, normed, early, gains, mine, got, low, two, table):
    rows, pair = query.shape
    args = (query, normed, early, gains, mine, got, low, two, table) + tuple(pair_parts)
    half = shape((2, rows // 4, normed.shape[1]), BF16)
    small = shape((SMALL, normed.shape[1]), BF16)
    out = [shape((BUNDLE, normed.shape[1]), BF16), small, small, half, half]
    return simple(weight_grads_kernel, "weight_grads", out, args, place, micros=4)


BUNDLE = 640


def fold_bundle_kernel(parts_ref, own_ref, a_ref, b_ref, c_ref, out_ref):
    height = parts_ref.shape[1]
    for half in range(2):
        total = parts_ref[4 * half].astype(F32)
        for block in range(4 * half + 1, 4 * half + 4):
            total = total + parts_ref[block].astype(F32)
        out_ref[half * height : (half + 1) * height, :] = total.astype(BF16)
    units = own_ref[0].astype(F32)
    for ref in (a_ref, b_ref, c_ref):
        units = units + ref[...].astype(F32)
    out_ref[2 * height :, :] = units.astype(BF16)


def fold_bundle(parts, own, others):
    out = shape((2 * parts.shape[1] + own.shape[1], LANES), BF16)
    return simple(fold_bundle_kernel, "fold_bundle", out, (parts, own) + tuple(others), micros=2)


def finish_kernel(place_ref, *refs):
    parts, outs, sides = refs[:4], refs[4:-1], refs[-1]
    pair = outs[0].shape[1] // 2
    height = sides.shape[1] // 4
    block = height + SMALL
    units = (parts[0].shape[0] - 2 * block) // 3
    small = jnp.zeros((SMALL, LANES), F32)
    for hop, part in zip(HOPS, parts):
        chunk = lax.rem(place_ref[2] - hop + 4, 4)
        here = pl.ds(pl.multiple_of(chunk * height, 16), height)
        for half in range(2):
            first = half * block
            sides[half, here, :] = part[first : first + height, :].astype(F32)
            small = small + part[first + height : first + block, :].astype(F32)
        here = pl.ds(pl.multiple_of(chunk * units, 16), units)
        for at, out_ref in enumerate(outs[4:7]):
            first = 2 * block + at * units
            out_ref[here, :] = part[first : first + units, :].astype(F32)
    for half in range(2):
        cols = slice(half * pair, (half + 1) * pair)
        for at in range(3):
            outs[at][:, cols] = jnp.transpose(sides[half, at * pair : (at + 1) * pair, :])
        rows = slice((3 + half) * pair, (4 + half) * pair)
        outs[3][:, cols] = jnp.transpose(sides[0, rows, :] + sides[1, rows, :])
    outs[7][...] = small


def finish(place, parts, pair):
    units = (parts[0].shape[0] - BUNDLE // 2 - 2 * SMALL) // 3
    out = [shape((LANES, 2 * pair), F32)] * 4 + [shape((4 * units, LANES), F32)] * 3
    out = out + [shape((SMALL, LANES), F32)]
    return pl.pallas_call(
        finish_kernel,
        grid=(1,),
        in_specs=[SMEM] + whole(*parts),
        out_specs=whole(*out),
        out_shape=out,
        scratch_shapes=[pltpu.VMEM((2, BUNDLE, LANES), F32)],
        compiler_params=params(),
        cost_estimate=cost(2),
        name="finish",
    )(place, *parts)


def spread_kernel(parts_ref, small_ref, one_ref, got_ref, out_ref):
    total = parts_ref[0].astype(F32)
    for at in range(1, 4):
        total = total + parts_ref[at].astype(F32)
    small = small_ref[...].astype(F32) + one_ref[...].astype(F32) + got_ref[...].astype(F32)
    total = jnp.concatenate([total.astype(BF16), small.astype(BF16)], axis=0)
    for block in range(8):
        out_ref[block] = total[:, block * LANES : (block + 1) * LANES]


def spread(parts, small, one, one_got, deps):
    out = shape((8, parts.shape[1] + SMALL, LANES), BF16)
    return simple(spread_kernel, "spread", out, (parts, small, one, one_got), deps=deps)


def swap(values, axis_name, count, bit):
    return lax.ppermute(values, axis_name, [(at, at ^ bit) for at in range(count)])


def swap_core(values):
    return swap(values, "mp", 4, 1)


def swap_chip(values):
    return swap(values, "mp", 4, 2)


def swap_side(values):
    return swap(values, "blk", 8, 4)


def turn_z(values, hop):
    return lax.ppermute(values, "blk", [(at, at // 4 * 4 + (at - hop) % 4) for at in range(8)])


def step_dp(values, hop):
    return lax.ppermute(values, "dp", [(at, (at + hop) % 4) for at in range(4)])


def turn_dp(values):
    return [step_dp(values, hop) for hop in (1, 3, 2)]


def turn_z(values, hop):
    return lax.ppermute(values, "blk", [(at, at // 4 * 4 + (at - hop) % 4) for at in range(8)])


def spread_gather(values, axis_name, count):
    wide = jnp.broadcast_to(values[None], (count,) + values.shape)
    return lax.all_to_all(wide, axis_name, 0, 0, tiled=False)


def sum_chips(values, core, meanwhile=()):
    return join_cores(values, after(swap(values, "mp", 4, 2), meanwhile), core)


def join_cores(values, got, core):
    total = (values.astype(F32) + got.astype(F32)).astype(BF16)
    got = swap(total, "mp", 4, 1)
    first = jnp.where(core == 0, total, got)
    second = jnp.where(core == 0, got, total)
    return jnp.concatenate([first, second], axis=0)


def pick(values, at, axis):
    return lax.dynamic_index_in_dim(values, at, axis, keepdims=False)


def sum_cores(values, core):
    rows, model = values.shape
    halves = values.reshape(2, rows // 2, model)
    got = swap(pick(halves, 1 - core, 0), "mp", 4, 1)
    return (pick(halves, core, 0).astype(F32) + got.astype(F32)).astype(BF16)


def shards(
    tokens,
    cotangent,
    seg_ids,
    token_boxes,
    norm1_gain,
    w_query,
    w_key,
    w_value,
    w_out_t,
    bias_table,
    norm2_gain,
    w_gate,
    w_up,
    w_down_t,
):
    rows = tokens.shape[0]
    pair = w_query.shape[1] // 2
    blk, mp, data = lax.axis_index("blk"), lax.axis_index("mp"), lax.axis_index("dp")
    place = jnp.stack([blk // 4, blk % 4, data, mp % 2]).astype(jnp.int32)

    tokens_other = swap_side(jnp.concatenate([tokens, unfold_rows(w_out_t)], axis=0))
    table = jnp.pad(bias_table.T, ((6, 6), (0, rows - bias_table.shape[0])))
    early, late = pack(
        place,
        (
            seg_ids.reshape(1, rows),
            token_boxes,
            norm1_gain.reshape(1, LANES),
            norm2_gain.reshape(1, LANES),
            table,
        ),
        (w_query, w_key, w_value),
        (w_gate.T, w_up.T, w_down_t.T),
    )
    early_all = lax.all_to_all(early, "blk", 0, 0, tiled=False)

    turned = [turn_z(late, hop) for hop in (1, 2, 3)]
    turned, tokens_other = lax.optimization_barrier((turned, tokens_other))
    near = stack([late] + turned)
    before_near, behind_near = step_dp(near, 1), step_dp(near, 3)
    normed_one, queries, own_pairs, gains, key_meta, meta, table = project(
        place, early_all, tokens, tokens_other, w_out_t, (near,)
    )
    own_pairs, before_near, behind_near = lax.optimization_barrier(
        (own_pairs, before_near, behind_near)
    )
    pairs = lax.all_to_all(
        own_pairs, "blk", 0, 0, axis_index_groups=[[0, 1, 2, 3], [4, 5, 6, 7]]
    )
    far = swap_side(near)
    after_near = step_dp(before_near, 1)
    bias = bias_scores(place, meta, key_meta, table, ())
    probs, attn_exact, attn_mine, attn_other = attend(
        place, queries, pairs, bias, (after_near, far)
    )
    before_far, behind_far = step_dp(far, 1), step_dp(far, 3)
    after_far = step_dp(behind_far, 3)

    attn_got = swap_side(attn_other)
    keep, send = branch_part(place, attn_mine, attn_got, pairs, (before_far, behind_far))
    pieces = [near, far, before_near, before_far, behind_near, behind_far, after_near, after_far]
    ffn_w, hidden_grad = ffn_prepare(place, cotangent, pieces)
    part = add(keep, swap_core(send))
    branch = add(part, swap_chip(part), (ffn_w,))
    branch_got = swap_core(branch)
    normed_two, parts, keep, send = ffn_forward(
        place, tokens, branch, branch_got, gains, hidden_grad, ffn_w
    )
    part = add(keep, swap_core(send))
    ffn_grads = ffn_back(place, parts, normed_two, cotangent, (part,))
    grad = add(part, swap_chip(part), (ffn_grads,))
    middle_grad, branch_low, gain_two_grad, grad_mine, grad_other = middle_back(
        place, tokens, branch, branch_got, cotangent, gains, grad, swap_core(grad), pairs
    )
    ffn_grads = lax.all_to_all(ffn_grads, "dp", 0, 0, tiled=False)
    keep, send = ffn_output(place, parts, ffn_w, (grad_other,))
    out_part = add(keep, swap_core(send))
    out_got = swap_chip(out_part)
    score_grad, *pair_grads, query_low = attend_back(
        place, queries, grad_mine, swap_side(grad_other), attn_exact, pairs, probs, (out_part,)
    )
    pair_parts = pair_grads[:1] + [turn_z(pair_grads[hop], -hop) for hop in (1, 2, 3)]
    table_grad = table_grad_sums(meta, key_meta, score_grad, (out_got,))
    bundle, small, one, keep, send = weight_grads(
        place,
        pair_parts,
        query_low,
        normed_one,
        early_all,
        gains,
        attn_mine,
        attn_got,
        branch_low,
        gain_two_grad,
        table_grad,
    )
    bundle = bundle.reshape(4, BUNDLE // 4, -1)
    bundle = lax.all_to_all(bundle, "dp", 0, 0, tiled=False)
    ffn_parts = fold_to_blocks(place, ffn_grads, (send,))
    ffn_near = add(ffn_parts[0], swap_side(ffn_parts[1]))
    one = add(one, swap_core(one))
    bundle = spread(bundle, small, one, swap_chip(one), (ffn_near,))
    bundle = lax.all_to_all(bundle, "blk", 0, 0, tiled=False)
    ffn_turned = [turn_z(ffn_near[hop], -hop) for hop in (1, 2, 3)]
    folded = fold_bundle(bundle, ffn_near, ffn_turned)
    grad_query, grad_key, grad_value, grad_out, *ffn_final, small = finish(
        place, [folded] + turn_dp(folded), pair
    )

    part = add(keep, swap_core(send))
    part = add(part[0], swap_side(part[1]))
    grad = add(part, swap_chip(part))
    tokens_grad = tokens_back(place, tokens, gains, grad, swap_core(grad), middle_grad)

    out_sum = add(out_part, out_got, (ffn_near,))
    mixed = simple(
        mixed_kernel,
        "mixed",
        shape(tokens.shape, BF16),
        (tokens, branch, branch_got, out_sum, swap_core(out_sum)),
        place,
    )

    return (
        mixed,
        tokens_grad,
        small[0],
        grad_query,
        grad_key,
        grad_value,
        grad_out,
        small[2:6, :12].T,
        small[1],
        ffn_final[0].T,
        ffn_final[1].T,
        ffn_final[2].T,
    )


def solution(mesh):
    rows = P(("dp", "blk"), None)
    weight = P("blk", "mp")
    in_specs = (
        rows,
        rows,
        P(("dp", "blk")),
        P(None, ("dp", "blk")),
        P("blk"),
        weight,
        weight,
        weight,
        weight,
        weight,
        P("blk"),
        weight,
        weight,
        weight,
    )
    out_specs = (
        rows,
        rows,
        P("blk"),
        weight,
        weight,
        weight,
        weight,
        weight,
        P("blk"),
        weight,
        weight,
        weight,
    )
    return jax.shard_map(shards, mesh=mesh, in_specs=in_specs, out_specs=out_specs, check_vma=False)
```

```python
import functools

import jax
import jax.numpy as jnp
from jax import lax
from jax.experimental import pallas as pl
from jax.experimental.pallas import tpu as pltpu
from jax.sharding import PartitionSpec as P

HEAD_DIM = 64
EPS = 1e-06
SEQ_EDGES = (1, 2, 3, 4, 5, 6, 7, 8, 12, 16, 23, 32, 46, 64, 91)
BOX_EDGES = (2, 4, 6, 8, 12, 16, 24, 32, 48, 64, 96, 128, 192, 256, 384)
BF16 = jnp.bfloat16
F32 = jnp.float32
LANES = 128
MIB = 2**20
VMEM_MIB = 32
PREP = 10
SMEM = pl.BlockSpec(memory_space=pltpu.SMEM)


def whole(*arrays):
    return [pl.BlockSpec(item.shape, lambda s, rank=len(item.shape): (0,) * rank) for item in arrays]


def shape(dims, kind):
    return jax.ShapeDtypeStruct(dims, kind)


HBM = pl.BlockSpec(memory_space=pl.ANY)


def simple(kernel, name, out, args, place=None, deps=(), micros=0.05, mib=VMEM_MIB):
    count = len(args) + (place is not None)

    def body(*refs):
        kernel(*refs[:count], *refs[count + len(deps) :])

    single = not isinstance(out, list)
    specs = whole(*([out] if single else out))
    return pl.pallas_call(
        body,
        grid=(1,),
        in_specs=[SMEM] * (place is not None) + whole(*args) + [HBM] * len(deps),
        out_specs=specs[0] if single else specs,
        out_shape=out,
        compiler_params=params(mib),
        cost_estimate=cost(micros),
        name=name,
    )(*([place] if place is not None else []), *args, *deps)


def add_kernel(a_ref, b_ref, out_ref):
    out_ref[...] = (a_ref[...].astype(F32) + b_ref[...].astype(F32)).astype(BF16)


def add(a, b, deps=()):
    return simple(add_kernel, "add", shape(a.shape, BF16), (a, b), deps=deps)


def stack_kernel(*refs):
    for at, ref in enumerate(refs[:-1]):
        refs[-1][at] = ref[...]


def stack(parts, deps=()):
    out = shape((len(parts),) + parts[0].shape, BF16)
    return simple(stack_kernel, "stack", out, parts, deps=deps)


def both_halves(own, got, first):
    return jnp.where(first, own, got), jnp.where(first, got, own)


def keep_and_send(values, core, keep_ref, send_ref):
    half = values.shape[0] // 2
    first, second = values[:half], values[half:]
    keep_ref[...] = jnp.where(core == 0, first, second)
    send_ref[...] = jnp.where(core == 0, second, first)


def params(mib=VMEM_MIB):
    return pltpu.CompilerParams(
        vmem_limit_bytes=mib * MIB, dimension_semantics=("arbitrary",)
    )


def cost(micros):
    return pl.CostEstimate(flops=int(micros * 1.1e9), bytes_accessed=int(micros * 1e5), transcendentals=0)


def contract_rows(left, right):
    return lax.dot_general(
        left, right, (((0,), (0,)), ((), ())), preferred_element_type=jnp.float32
    )


def contract_cols(left, right):
    return lax.dot_general(
        left, right, (((1,), (1,)), ((), ())), preferred_element_type=jnp.float32
    )


def count_edges(magnitude, edge_list):
    result = jnp.zeros(magnitude.shape, jnp.int32)
    for border in edge_list:
        result = result + (magnitude >= border).astype(jnp.int32)
    return result


def box_cell(offset):
    half = jnp.abs(offset) >> 1
    cell = jnp.where(half < 32, half, (half >> 4) + 30)
    return cell + jnp.where(offset > 0, 64, 0)


def cell_bucket(cell):
    low = cell & 63
    half = jnp.where(low < 32, low, (low - 30) << 4)
    return count_edges(half * 2, BOX_EDGES) + jnp.where(cell >= 64, 16, 0)


def lookup(table, index):
    return jnp.take_along_axis(table, index, axis=1, mode="promise_in_bounds")


SMALL = 16


def pack_kernel(
    place_ref, seg_hbm, box_hbm, one_hbm, two_hbm, table_hbm, query_hbm, key_hbm, value_hbm, gate_hbm, up_hbm, down_hbm, early_ref, late_ref, *rest
):
    refs, sems = rest[:-1], rest[-1]
    units = gate_hbm.shape[0] // 4
    mine = pl.ds(pl.multiple_of(place_ref[2] * units, 16), units)
    sources = [seg_hbm, box_hbm, one_hbm, two_hbm, table_hbm, query_hbm, key_hbm, value_hbm]
    copies = [pltpu.make_async_copy(src, dst, sems.at[at]) for at, (src, dst) in enumerate(zip(sources, refs))]
    for at, src in enumerate((gate_hbm, up_hbm, down_hbm)):
        spot = late_ref.at[at * units : (at + 1) * units, :]
        copies.append(pltpu.make_async_copy(src.at[mine, :], spot, sems.at[len(sources) + at]))
    for copy in copies:
        copy.start()
    for copy in copies:
        copy.wait()
    seg_ref, box_ref, one_ref, two_ref, table_ref, query_ref, key_ref, value_ref = refs
    width = seg_ref.shape[1]
    pair = query_ref.shape[1] // 2
    row = lax.broadcasted_iota(jnp.int32, (SMALL, width), 0)
    boxes = box_ref[...]
    centre_x = boxes[0:1] + boxes[2:3]
    centre_y = boxes[1:2] + boxes[3:4]
    gains = jnp.concatenate([one_ref[...], two_ref[...]], axis=1).astype(F32)
    small = table_ref[...].astype(F32)
    for at, values in enumerate(
        (seg_ref[...], centre_x >> 8, centre_x & 255, centre_y >> 8, centre_y & 255, gains)
    ):
        small = jnp.where(row == at, values.astype(F32), small)
    small = small.astype(BF16)
    small = jnp.concatenate([small, jnp.zeros((SMALL, 3 * pair - width), BF16)], axis=1)
    for block in range(early_ref.shape[0]):
        half = block // 4
        cols = slice(half * pair, (half + 1) * pair)
        for at, ref in enumerate((query_ref, key_ref, value_ref)):
            early_ref[block, :LANES, at * pair : (at + 1) * pair] = ref[:, cols]
        early_ref[block, LANES:, :] = small


def pack(place, small, weights, late):
    pair = weights[0].shape[1] // 2
    args = small + weights
    out = [
        shape((8, LANES + SMALL, 3 * pair), BF16),
        shape((3 * late[0].shape[0] // 4, LANES), BF16),
    ]
    return pl.pallas_call(
        pack_kernel,
        grid=(1,),
        in_specs=[SMEM] + [HBM] * (len(args) + 3),
        out_specs=whole(*out),
        out_shape=out,
        scratch_shapes=[pltpu.VMEM(item.shape, item.dtype) for item in args]
        + [pltpu.SemaphoreType.DMA((len(args) + 3,))],
        compiler_params=params(64),
        cost_estimate=cost(0.05),
        name="pack",
    )(place, *args, *late)


def unfold_rows(values):
    return jnp.concatenate(jnp.split(values, 4, axis=0), axis=1)


def fold_rows(values):
    return jnp.concatenate(jnp.split(values, 4, axis=1), axis=0)


def scale_tokens_kernel(place_ref, own_ref, other_ref, out_w_ref, scaled_ref, wide_ref):
    rows = own_ref.shape[0]
    side = place_ref[0]
    for ref, half in ((own_ref, side), (other_ref, 1 - side)):
        inputs = ref[:rows, :].astype(F32)
        here = pl.ds(pl.multiple_of(half * rows, rows), rows)
        scaled_ref[here, :] = inputs * rms_scale(inputs)
    for values, half in ((out_w_ref[...], side), (fold_rows(other_ref[rows:, :]), 1 - side)):
        wide_ref[pl.ds(pl.multiple_of(half * LANES, LANES), LANES), :] = values


def scale_tokens(place, own, other, out_w):
    rows, model = own.shape
    out = [shape((2 * rows, model), F32), shape((2 * LANES, out_w.shape[1]), BF16)]
    return simple(scale_tokens_kernel, "scale_tokens", out, (own, other, out_w), place, micros=PREP)


def project_kernel(
    place_ref, early_ref, scaled_ref, out_w_ref, normed_ref, query_ref, pair_ref, gain_ref, key_ref, meta_ref, table_ref
):
    rows = scaled_ref.shape[0] // 2
    pair = query_ref.shape[1]
    side, depth = place_ref[0], place_ref[1]
    small = [early_ref[block, LANES:, :rows].astype(F32) for block in range(8)]
    for at in range(2):
        lanes = slice(at * LANES, (at + 1) * LANES)
        gain = jnp.concatenate([part[5:6, lanes] for part in small], axis=1)
        gain_ref[at : at + 1, :] = gain
        if at == 0:
            gain_one = gain

    for copy in range(4):
        pair_ref[copy, 2 * rows :, :] = out_w_ref[...]
    weight = jnp.concatenate([early_ref[block, :LANES, :] for block in range(8)], axis=0)
    normed = (scaled_ref[...] * gain_one).astype(BF16)
    normed_ref[...] = normed
    result = jnp.dot(normed, weight, preferred_element_type=F32).astype(BF16)
    query_ref[...] = result[:, :pair] * jnp.asarray(HEAD_DIM ** (-0.5), BF16)
    for copy in range(4):
        pair_ref[copy, : 2 * rows, :] = result[:, pair:]

    time = lax.broadcasted_iota(jnp.int32, (1, rows), 1)
    for block in range(8):
        part = small[block]
        at = (block % 4) * 2 + block // 4
        there = slice(at * rows, (at + 1) * rows)
        key_ref[0:1, there] = part[0:1].astype(jnp.int32)
        key_ref[1:2, there] = (part[1:2] * 256.0 + part[2:3]).astype(jnp.int32)
        key_ref[2:3, there] = (part[3:4] * 256.0 + part[4:5]).astype(jnp.int32)
        for half in range(2):
            ahead = (block - depth - 4 * half) * rows + SEQ_SPAN // 4
            key_ref[3 + half : 4 + half, there] = jnp.clip(time + ahead, 0, SEQ_SPAN - 1)
        key_ref[5:8, there] = jnp.zeros((3, rows), jnp.int32)

    for half in range(2):
        part = early_ref[depth + 4 * half, LANES:, :rows].astype(F32)
        columns = jnp.transpose(part)
        seg = columns[:, 0:1]
        centre_x = columns[:, 1:2] * 256.0 + columns[:, 2:3]
        centre_y = columns[:, 3:4] * 256.0 + columns[:, 4:5]
        for at, values in enumerate((seg, centre_x, centre_y)):
            wide = jnp.broadcast_to(values.astype(jnp.int32), (rows, LANES))
            meta_ref[at, half * rows : (half + 1) * rows, :] = wide

    lane = lax.broadcasted_iota(jnp.int32, (8, LANES), 1)
    table = jnp.zeros((8, LANES), F32)
    for block in range(8):
        entries = jnp.where(side == 0, small[block][6:8, :LANES], small[block][8:10, :LANES])
        entries = jnp.concatenate([entries, jnp.zeros((6, LANES), F32)], axis=0)
        index = jnp.clip(lane - 12 * block, 0, LANES - 1)
        found = lookup(entries, index)
        table = jnp.where((lane >= 12 * block) & (lane < 12 * block + 12), found, table)
    table_ref[...] = table


def project(place, early, scaled, out_w, deps):
    rows, model = scaled.shape[0] // 2, scaled.shape[1]
    pair = early.shape[2] // 3
    out = [
        shape((2 * rows, model), BF16),
        shape((2 * rows, pair), BF16),
        shape((4, 2 * rows + 2 * LANES, 2 * pair), BF16),
        shape((2, model), F32),
        shape((8, 8 * rows), jnp.int32),
        shape((3, 2 * rows, LANES), jnp.int32),
        shape((8, LANES), F32),
    ]
    return simple(
        project_kernel, "project", out, (early, scaled, out_w), place, deps, 0.05, 64
    )


STEPS = 3600.0
SHIFT = 10800.0
MASKED = -(2**31)


def bias_kernel(place_ref, meta_ref, key_ref, table_ref, *refs):
    bias_ref = refs[-1]
    chunk, length = bias_ref.shape
    width = TOKENS_BLOCK
    step = pl.program_id(0)
    half = step // (2 * width // chunk // 2)
    first_row = lax.rem(step * chunk, width)
    query_block = place_ref[1] + 4 * half
    lane = lax.broadcasted_iota(jnp.int32, (8, LANES), 1)
    buckets = cell_bucket(lane)
    table = table_ref[...]

    def packed(index):
        found = lookup(table, index)
        high = jnp.round(found[0:1, :] * STEPS).astype(jnp.int32)
        low = jnp.round(found[1:2, :] * STEPS + SHIFT).astype(jnp.int32)
        return (high << 16) + low

    def spread(values):
        return jnp.broadcast_to(values, (chunk, LANES))

    hor = packed(buckets + 32)
    ver = spread(packed(buckets + 64))
    seq_count = count_edges(jnp.abs(lane - 64), SEQ_EDGES) + jnp.where(lane > 64, 16, 0)
    seq = spread(packed(seq_count))
    behind, middle, beyond = [packed(jnp.full((8, LANES), at, jnp.int32)) for at in (15, 30, 31)]

    def key_block(at):
        return at // 2 + 4 * lax.rem(at, 2)

    def block_of_keys(at, with_near):
        ahead = key_block(at) * width - query_block * width - first_row
        far = spread(hor if with_near else hor + jnp.where(ahead > 0, beyond, behind))
        for column in range(width // LANES):
            there = pl.ds(pl.multiple_of(at * width + column * LANES, LANES), LANES)
            keys = key_ref[:, there]
            total = lookup(far, box_cell(keys[1:2, :] - meta_ref[1]))
            total = total + lookup(ver, box_cell(keys[2:3, :] - meta_ref[2]))
            if with_near:
                row = lax.broadcasted_iota(jnp.int32, (chunk, LANES), 0)
                col = lax.broadcasted_iota(jnp.int32, (chunk, LANES), 1)
                offset = col - row + (ahead + column * LANES)
                found = lookup(seq, jnp.clip(offset + 64, 0, LANES - 1))
                found = jnp.where(offset >= 64, middle, found)
                found = jnp.where(offset >= 91, beyond, found)
                total = total + jnp.where(offset <= -91, behind, found)
            bias_ref[:, there] = jnp.where(keys[0:1, :] == meta_ref[0], total, MASKED)

    def body(at, carry):
        near = jnp.abs(key_block(at) - query_block) <= 1
        pl.when(near)(functools.partial(block_of_keys, at, True))
        pl.when(jnp.logical_not(near))(functools.partial(block_of_keys, at, False))
        return carry

    lax.fori_loop(0, length // width, body, 0)


TOKENS_BLOCK = 256


def bias_scores(place, meta, key_meta, table, deps):
    rows = meta.shape[1]
    length = key_meta.shape[1]
    chunk = 128
    return pl.pallas_call(
        bias_kernel,
        grid=(rows // chunk,),
        in_specs=[
            pl.BlockSpec(memory_space=pltpu.SMEM),
            pl.BlockSpec((3, chunk, LANES), lambda s: (0, s, 0)),
            pl.BlockSpec((8, length), lambda s: (0, 0)),
            pl.BlockSpec((8, LANES), lambda s: (0, 0)),
        ]
        + [HBM] * len(deps),
        out_specs=pl.BlockSpec((chunk, length), lambda s: (s, 0)),
        out_shape=jax.ShapeDtypeStruct((rows, length), jnp.int32),
        compiler_params=params(64),
        cost_estimate=cost(10),
        name="bias_scores",
    )(place, meta, key_meta, table, *deps)


def head_masks(shape):
    lane = lax.broadcasted_iota(jnp.int32, shape, 1)
    return lane < HEAD_DIM, lane >= HEAD_DIM


def attend_kernel(place_ref, query_ref, bias_ref, pair_ref, *refs):
    probs_ref, exact_ref, mine_ref, other_ref = refs[-4:]
    count, _, both = pair_ref.shape
    width = bias_ref.shape[1] // count
    features = both // 2
    rows = query_ref.shape[0]
    masks = head_masks((rows, features))
    query = query_ref[...]
    allowed = []
    codes = []
    for at in range(count):
        code = bias_ref[:, at * width : (at + 1) * width]
        codes.append(code)
        allowed.append(code != MASKED)
    outs = []
    for head in range(2):
        mine = jnp.where(masks[head], query, jnp.zeros_like(query))
        scores = []
        for at in range(count):
            code = (codes[at] >> 16) if head == 0 else (codes[at] & 65535)
            score = contract_cols(mine, pair_ref[at, :width, :features])
            score = score + code.astype(F32) * (1.0 / STEPS)
            scores.append(jnp.where(allowed[at], score, -1e30))
        top = functools.reduce(jnp.maximum, scores)
        top = jnp.max(top, axis=1, keepdims=True)
        weights = [jnp.exp(score - top) for score in scores]
        total = functools.reduce(jnp.add, weights)
        inverse = 1.0 / jnp.sum(total, axis=1, keepdims=True)
        result = None
        for at in range(count):
            low = (weights[at] * inverse).astype(BF16)
            probs_ref[head, :, at * width : (at + 1) * width] = low
            part = jnp.dot(low, pair_ref[at, :width, features:], preferred_element_type=F32)
            result = part if result is None else result + part
        outs.append(result)
    exact = jnp.where(masks[0], outs[0], outs[1])
    exact_ref[...] = exact
    low = exact.astype(BF16)
    tiles = mine_ref.shape[0] // rows
    step = pl.program_id(0)
    here = pl.ds(pl.multiple_of(lax.rem(step, tiles) * rows, rows), rows)
    own = step // tiles == place_ref[0]

    @pl.when(own)
    def _():
        mine_ref[here, :] = low

    @pl.when(jnp.logical_not(own))
    def _():
        other_ref[here, :] = low


def attend(place, queries, pairs, bias, deps):
    rows, length = bias.shape
    both = pairs.shape[2]
    tile = 128
    features = both // 2
    slim = pl.BlockSpec((tile, features), lambda s: (s, 0))
    half = shape((rows // 2, features), BF16)
    return pl.pallas_call(
        attend_kernel,
        grid=(rows // tile,),
        in_specs=[SMEM, slim, pl.BlockSpec((tile, length), lambda s: (s, 0))]
        + whole(pairs)
        + [HBM] * len(deps),
        out_specs=[pl.BlockSpec((2, tile, length), lambda s: (0, s, 0)), slim] + whole(half, half),
        out_shape=[
            shape((2, rows, length), BF16),
            shape((rows, features), F32),
            half,
            half,
        ],
        compiler_params=params(64),
        cost_estimate=cost(9),
        name="attend",
    )(place, queries, bias, pairs, *deps)


def out_weight(pair_ref):
    start = pair_ref.shape[1] - 2 * LANES
    parts = []
    for block in range(8):
        first = start + block // 4 * LANES
        parts.append(pair_ref[block % 4, first : first + LANES, :])
    return jnp.concatenate(parts, axis=0)


def branch_kernel(place_ref, mine_ref, got_ref, pair_ref, keep_ref, send_ref):
    parts = both_halves(mine_ref[...], got_ref[...], place_ref[0] == 0)
    attended = jnp.concatenate(parts, axis=1)
    result = contract_cols(attended, out_weight(pair_ref)).astype(BF16)
    keep_and_send(result, place_ref[3], keep_ref, send_ref)


def branch_part(place, mine, got, pairs, deps):
    half = shape((mine.shape[0] // 2, 8 * LANES), BF16)
    return simple(branch_kernel, "branch_part", [half, half], (mine, got, pairs), place, deps, 2)


def gelu_parts(gate):
    rate = 0.7978845608028654
    square = gate * gate
    slope = jnp.tanh(rate * gate * (1.0 + 0.044715 * square))
    half = 0.5 * (1.0 + slope)
    inner = rate * (1.0 + 3.0 * 0.044715 * square)
    return gate * half, half + 0.5 * gate * (1.0 - slope * slope) * inner


def piece_copies(place_ref, piece_refs, held, sems, hop, first):
    side, depth = place_ref[0], place_ref[1]
    height = held.shape[1]
    copies = []
    for far in range(2):
        for turn in range(4):
            block = (side + far * (1 - 2 * side)) * 4 + lax.rem(depth + turn, 4)
            lanes = pl.ds(pl.multiple_of(block * LANES, LANES), LANES)
            copies.append(
                pltpu.make_async_copy(
                    piece_refs[2 * hop + far].at[turn, pl.ds(first, height), :],
                    held.at[hop, :, lanes],
                    sems.at[hop, 4 * far + turn],
                )
            )
    return copies


def ffn_prepare_kernel(place_ref, dy_ref, *refs):
    piece_refs, (weight_ref, grad_ref, sems) = refs[:8], refs[8:]
    copies = [piece_copies(place_ref, piece_refs, weight_ref, sems, hop, 0) for hop in range(4)]
    units = weight_ref.shape[1] // 3
    for group in copies:
        for copy in group:
            copy.start()
    for hop in range(4):
        for copy in copies[hop]:
            copy.wait()
        grad_ref[hop] = contract_cols(weight_ref[hop, 2 * units :, :], dy_ref[...])


def ffn_prepare(place, dy, pieces):
    rows, model = dy.shape
    height = pieces[0].shape[1]
    out = [shape((4, height, model), BF16), shape((4, height // 3, rows), F32)]
    return pl.pallas_call(
        ffn_prepare_kernel,
        grid=(1,),
        in_specs=[SMEM] + whole(dy) + [HBM] * 8,
        out_specs=whole(*out),
        out_shape=out,
        scratch_shapes=[pltpu.SemaphoreType.DMA((4, 8))],
        compiler_params=params(),
        cost_estimate=cost(4),
        name="ffn_prepare",
    )(place, dy, *pieces)


def middle_of(tokens_ref, total_ref, got_ref, core):
    branch = jnp.concatenate(both_halves(total_ref[...], got_ref[...], core == 0), axis=0)
    return tokens_ref[...].astype(F32) + branch.astype(F32)


def rms_scale(values):
    return lax.rsqrt(jnp.mean(values * values, axis=1, keepdims=True) + EPS)


def ffn_kernel(
    place_ref, tokens_ref, total_ref, got_ref, gain_ref, hidden_grad_ref, weight_ref, normed_ref, parts_ref, keep_ref, send_ref, sums, turned
):
    units = weight_ref.shape[1] // 2
    step = pl.program_id(0)

    @pl.when(step == 0)
    def _():
        middle = middle_of(tokens_ref, total_ref, got_ref, place_ref[3])
        normed = (middle * rms_scale(middle) * gain_ref[1:2, :]).astype(BF16)
        normed_ref[...] = normed
        turned[...] = jnp.transpose(normed)
        sums[...] = jnp.zeros_like(sums)

    gates = jnp.dot(weight_ref[0], turned[...], preferred_element_type=F32)
    gate, upward = gates[:units], gates[units:]
    hidden_grad = hidden_grad_ref[0]
    value, slope = gelu_parts(gate)
    grads = jnp.concatenate([hidden_grad * upward * slope, hidden_grad * value], axis=0).astype(BF16)
    parts_ref[0, : 2 * units, :] = grads
    parts_ref[0, 2 * units :, :] = (value * upward).astype(BF16)
    sums[...] += contract_rows(grads, weight_ref[0])

    @pl.when(step == pl.num_programs(0) - 1)
    def _():
        keep_and_send(sums[...].astype(BF16), place_ref[3], keep_ref, send_ref)


def ffn_forward(place, tokens, total, got, gains, hidden_grad, weights):
    rows, model = tokens.shape
    hops, height, _ = weights.shape
    half = shape((rows // 2, model), BF16)
    out = [shape((rows, model), BF16), shape((hops, height, rows), BF16), half, half]

    def chunk(item):
        return pl.BlockSpec((1,) + item.shape[1:], lambda s: (s, 0, 0))

    return pl.pallas_call(
        ffn_kernel,
        grid=(hops,),
        in_specs=[SMEM]
        + whole(tokens, total, got, gains)
        + [chunk(hidden_grad), pl.BlockSpec((1, height // 3 * 2, model), lambda s: (s, 0, 0))],
        out_specs=whole(out[0]) + [chunk(out[1])] + whole(half, half),
        out_shape=out,
        scratch_shapes=[pltpu.VMEM((rows, model), F32), pltpu.VMEM((model, rows), BF16)],
        compiler_params=params(),
        cost_estimate=cost(5),
        name="ffn_forward",
    )(place, tokens, total, got, gains, hidden_grad, weights)


def ffn_back_kernel(place_ref, parts_ref, normed_ref, dy_ref, *refs):
    grad_ref = refs[-1]
    units = parts_ref.shape[1] // 3
    grad_ref[0, : 2 * units, :] = jnp.dot(
        parts_ref[0, : 2 * units, :], normed_ref[...], preferred_element_type=F32
    ).astype(BF16)
    grad_ref[0, 2 * units :, :] = jnp.dot(
        parts_ref[0, 2 * units :, :], dy_ref[...], preferred_element_type=F32
    ).astype(BF16)


def ffn_output_kernel(place_ref, parts_ref, weight_ref, *refs):
    keep_ref, send_ref, sums = refs[-3:]
    step = pl.program_id(0)
    part = contract_rows(parts_ref[0], weight_ref[0])

    @pl.when(step == 0)
    def _():
        sums[...] = part

    @pl.when(step > 0)
    def _():
        sums[...] += part

    @pl.when(step == pl.num_programs(0) - 1)
    def _():
        keep_and_send(sums[...].astype(BF16), place_ref[3], keep_ref, send_ref)


def ffn_output(place, parts, weights, deps):
    hops, height, rows = parts.shape
    model = weights.shape[2]
    half = shape((rows // 2, model), BF16)
    return pl.pallas_call(
        ffn_output_kernel,
        grid=(hops,),
        in_specs=[
            SMEM,
            pl.BlockSpec((1, height // 3, rows), lambda s: (s, 2, 0)),
            pl.BlockSpec((1, height // 3, model), lambda s: (s, 2, 0)),
        ]
        + [HBM] * len(deps),
        out_specs=whole(half, half),
        out_shape=[half, half],
        scratch_shapes=[pltpu.VMEM((rows, model), F32)],
        compiler_params=params(),
        cost_estimate=cost(3),
        name="ffn_output",
    )(place, parts, weights, *deps)


def norm_back(inputs, gain, normed_grad):
    scale = rms_scale(inputs)
    gain_grad = jnp.sum(normed_grad * inputs * scale, axis=0, keepdims=True)
    weighted = normed_grad * gain
    mean = jnp.mean(weighted * inputs, axis=1, keepdims=True)
    return scale * weighted - inputs * (scale * scale * scale) * mean, gain_grad


def middle_kernel(
    place_ref, tokens_ref, total_ref, got_ref, dy_ref, gain_ref, grad_ref, grad_got_ref, pair_ref, middle_ref, low_ref, two_ref, mine_ref, other_ref
):
    core = place_ref[3]
    middle = middle_of(tokens_ref, total_ref, got_ref, core)
    parts = both_halves(grad_ref[...], grad_got_ref[...], core == 0)
    normed_grad = jnp.concatenate(parts, axis=0).astype(F32)
    result, gain_grad = norm_back(middle, gain_ref[1:2, :], normed_grad)
    result = dy_ref[...].astype(F32) + result
    middle_ref[...] = result
    low = result.astype(BF16)
    low_ref[...] = low
    two_ref[...] = gain_grad
    attended = jnp.dot(low, out_weight(pair_ref), preferred_element_type=F32).astype(BF16)
    pair = attended.shape[1] // 2
    first = place_ref[0] == 0
    mine_ref[...] = jnp.where(first, attended[:, :pair], attended[:, pair:])
    other_ref[...] = jnp.where(first, attended[:, pair:], attended[:, :pair])


def middle_back(place, tokens, total, got, dy, gains, grad, grad_got, pairs):
    rows, model = tokens.shape
    half = shape((rows, pairs.shape[2] // 2), BF16)
    out = [shape((rows, model), F32), shape((rows, model), BF16), shape((1, model), F32), half, half]
    args = (tokens, total, got, dy, gains, grad, grad_got, pairs)
    return simple(middle_kernel, "middle_back", out, args, place, micros=3)


def tokens_kernel(place_ref, tokens_ref, gain_ref, grad_ref, grad_got_ref, middle_ref, out_ref):
    parts = both_halves(grad_ref[...], grad_got_ref[...], place_ref[3] == 0)
    normed_grad = jnp.concatenate(parts, axis=0).astype(F32)
    result, _ = norm_back(tokens_ref[...].astype(F32), gain_ref[0:1, :], normed_grad)
    out_ref[...] = middle_ref[...] + result


def tokens_back(place, tokens, gains, grad, grad_got, middle_grad):
    out = shape(tokens.shape, F32)
    return simple(
        tokens_kernel, "tokens_back", out, (tokens, gains, grad, grad_got, middle_grad), place, micros=2
    )


def mixed_kernel(place_ref, tokens_ref, total_ref, got_ref, out_total_ref, out_got_ref, out_ref):
    core = place_ref[3]
    middle = middle_of(tokens_ref, total_ref, got_ref, core)
    parts = both_halves(out_total_ref[...], out_got_ref[...], core == 0)
    out_ref[...] = (middle + jnp.concatenate(parts, axis=0).astype(F32)).astype(BF16)


HOPS = (0, 1, 3, 2)


def ffn_back(place, parts, normed, dy, deps):
    rows, model = normed.shape
    hops, height, _ = parts.shape

    def owner(step, place_ref):
        hop = jnp.where(step == 0, 0, jnp.where(step == 1, 1, jnp.where(step == 2, 3, 2)))
        return lax.rem(place_ref[2] - hop + 4, 4)

    def same(*arrays):
        return [pl.BlockSpec(item.shape, lambda s, p: (0, 0)) for item in arrays]

    return pl.pallas_call(
        ffn_back_kernel,
        grid_spec=pltpu.PrefetchScalarGridSpec(
            num_scalar_prefetch=1,
            grid=(hops,),
            in_specs=[pl.BlockSpec((1, height, rows), lambda s, p: (s, 0, 0))]
            + same(normed, dy)
            + [HBM] * len(deps),
            out_specs=pl.BlockSpec((1, height, model), lambda s, p: (owner(s, p), 0, 0)),
        ),
        out_shape=shape((hops, height, model), BF16),
        compiler_params=params(),
        cost_estimate=cost(4),
        name="ffn_back",
    )(place, parts, normed, dy, *deps)


def fold_kernel(place_ref, parts_ref, *refs):
    out_ref = refs[-1]
    for block in range(4):
        lanes = slice(block * LANES, (block + 1) * LANES)
        total = parts_ref[0, :, lanes].astype(F32)
        for at in range(1, parts_ref.shape[0]):
            total = total + parts_ref[at, :, lanes].astype(F32)
        out_ref[0, lax.rem(block - place_ref[1] + 4, 4)] = total.astype(BF16)


def fold_to_blocks(place, parts, deps):
    count, height, model = parts.shape
    return pl.pallas_call(
        fold_kernel,
        grid_spec=pltpu.PrefetchScalarGridSpec(
            num_scalar_prefetch=1,
            grid=(2,),
            in_specs=[pl.BlockSpec((count, height, model // 2), lambda s, p: (0, 0, s))]
            + [HBM] * len(deps),
            out_specs=pl.BlockSpec(
                (1, 4, height, LANES), lambda s, p: (jnp.where(s == p[0], 0, 1), 0, 0, 0)
            ),
        ),
        out_shape=shape((2, 4, height, LANES), BF16),
        compiler_params=params(),
        cost_estimate=cost(4),
        name="fold_to_blocks",
    )(place, parts, *deps)


def attend_back_kernel(place_ref, query_ref, mine_ref, got_ref, exact_ref, probs_ref, pair_ref, *refs):
    score_ref, pair_grad_refs = refs[-9], refs[-8:-4]
    query_grad_ref, sums, delta, grads = refs[-4:]
    _, rows, width = probs_ref.shape
    features = query_ref.shape[1]
    step = pl.program_id(0)
    masks = head_masks((rows, features))
    query = query_ref[...]

    @pl.when(step == 0)
    def _():
        sums[...] = jnp.zeros_like(sums)
        parts = both_halves(mine_ref[...], got_ref[...], place_ref[0] == 0)
        grads[...] = jnp.concatenate(parts, axis=0)
        product = grads[...].astype(F32) * exact_ref[...]
        for head in range(2):
            row = jnp.sum(jnp.where(masks[head], product, 0.0), axis=1, keepdims=True)
            delta[head] = jnp.broadcast_to(row, (rows, LANES))

    grad = grads[...]
    keys = pair_ref[0, :, :features]
    values = pair_ref[0, :, features:]
    parts = []
    key_grads = []
    value_grads = []
    for head in range(2):
        cols = slice(head * HEAD_DIM, (head + 1) * HEAD_DIM)
        mine = jnp.where(masks[head], grad, jnp.zeros_like(grad))
        probs = probs_ref[head]
        prob_grad = contract_cols(mine, values)
        offset = jnp.concatenate([delta[head]] * (width // LANES), axis=1)
        score_grad = (probs.astype(F32) * (prob_grad - offset)).astype(BF16)
        score_ref[head] = score_grad
        parts.append(jnp.dot(score_grad, keys, preferred_element_type=F32))
        key_grads.append(contract_rows(query[:, cols], score_grad).astype(BF16))
        value_grads.append(contract_rows(grad[:, cols], probs).astype(BF16))
    for at in range(4):

        @pl.when(step == at)
        def _():
            for spot, part in enumerate(key_grads + value_grads):
                pair_grad_refs[at][spot * HEAD_DIM : (spot + 1) * HEAD_DIM, :] = part

    sums[...] += jnp.where(masks[0], parts[0], parts[1])

    @pl.when(step == pl.num_programs(0) - 1)
    def _():
        query_grad_ref[...] = (sums[...] * HEAD_DIM ** (-0.5)).astype(BF16)


def attend_back(place, queries, mine, got, exact, pairs, probs, deps):
    _, rows, length = probs.shape
    features = queries.shape[1]
    width, both = rows, pairs.shape[2]

    def spot(step, place_ref):
        return lax.rem(place_ref[1] + step, 4)

    def same(*arrays):
        return [pl.BlockSpec(item.shape, lambda s, p: (0, 0)) for item in arrays]

    slab = pl.BlockSpec((2, rows, width), lambda s, p: (0, 0, spot(s, p)))
    pair_grads = [shape((both, width), BF16)] * 4
    query_grad = shape((rows, features), BF16)
    return pl.pallas_call(
        attend_back_kernel,
        grid_spec=pltpu.PrefetchScalarGridSpec(
            num_scalar_prefetch=1,
            grid=(4,),
            in_specs=same(queries, mine, got, exact)
            + [slab, pl.BlockSpec((1, width, both), lambda s, p: (spot(s, p), 0, 0))]
            + [HBM] * len(deps),
            out_specs=[slab] + same(*pair_grads, query_grad),
            scratch_shapes=[
                pltpu.VMEM((rows, features), F32),
                pltpu.VMEM((2, rows, LANES), F32),
                pltpu.VMEM((rows, features), BF16),
            ],
        ),
        out_shape=[shape((2, rows, length), BF16)] + pair_grads + [query_grad],
        compiler_params=params(),
        cost_estimate=cost(5),
        name="attend_back",
    )(place, queries, mine, got, exact, probs, pairs, *deps)


BOX_SPAN = 1024
SEQ_SPAN = 512
TILE = 512


def threshold_row(edge_list, far, lane):
    borders = [-far] + [1 - edge for edge in reversed(edge_list)] + [1] + list(edge_list)
    result = jnp.zeros(lane.shape, jnp.int32)
    for at, border in enumerate(borders):
        result = jnp.where(lane == at, border, result)
    return result


def table_grad_kernel(meta_ref, key_ref, score_ref, *refs):
    out_ref, sums_ref = refs[-2:]
    _, rows, length = score_ref.shape
    half = rows // 2
    step = pl.program_id(0)
    lane = lax.broadcasted_iota(jnp.int32, (1, LANES), 1)
    level = lax.broadcasted_iota(jnp.int32, (TILE, 1), 0)

    def add(place, key_row, mine, edges, top, offset, span):
        index = jnp.clip(mine + threshold_row(edges, 4096, lane), 0, top)
        column = index & (LANES - 1)
        block = (index - offset) >> 7
        reached = (key_ref[pl.ds(key_row, 1), :] >= level + offset).astype(F32).astype(BF16)
        for head in range(2):
            sums = contract_cols(score_ref[head, span, :], reached)
            picked = jnp.zeros(column.shape, F32)
            for at in range(TILE // LANES):
                found = lookup(sums[:, at * LANES : (at + 1) * LANES], column)
                picked = picked + jnp.where(block == at, found, 0.0)
            sums_ref[place, head : head + 1, :] += jnp.sum(picked, axis=0, keepdims=True)

    @pl.when(step == 0)
    def _():
        sums_ref[...] = jnp.zeros_like(sums_ref)

    @pl.when(step < 4)
    def _():
        axis = step // 2
        mine = meta_ref[1 + axis]
        add(1 + axis, 1 + axis, mine, BOX_EDGES, BOX_SPAN - 1, (step % 2) * TILE, slice(None))

    @pl.when(step >= 4)
    def _():
        part = step - 4
        span = pl.ds(pl.multiple_of(part * half, half), half)
        mine = lax.broadcasted_iota(jnp.int32, (half, LANES), 0) + SEQ_SPAN // 4
        add(0, 3 + part, mine, SEQ_EDGES, SEQ_SPAN - 1, 0, span)

    @pl.when(step == pl.num_programs(0) - 1)
    def _():
        lanes = lax.broadcasted_iota(jnp.int32, (8, LANES), 1)
        bucket = lanes & 31
        first = jnp.where(bucket < 16, 15 - bucket, bucket)
        result = jnp.zeros((8, LANES), F32)
        for axis in range(3):
            sums = sums_ref[axis]
            part = lookup(sums, first) - jnp.where(first == 31, 0.0, lookup(sums, first + 1))
            result = jnp.where((lanes >> 5) == axis, part, result)
        out_ref[...] = result


def table_grad_sums(meta, key_meta, score_grad, deps):
    _, rows, length = score_grad.shape
    return pl.pallas_call(
        table_grad_kernel,
        grid=(6,),
        in_specs=whole(meta, key_meta, score_grad) + [HBM] * len(deps),
        out_specs=pl.BlockSpec((8, LANES), lambda s: (0, 0)),
        out_shape=shape((8, LANES), F32),
        scratch_shapes=[pltpu.VMEM((3, 8, LANES), F32)],
        compiler_params=params(),
        cost_estimate=cost(11),
        name="table_grad",
    )(meta, key_meta, score_grad, *deps)


def weight_grads_kernel(
    place_ref, query_ref, normed_ref, early_ref, gain_ref, mine_ref, got_ref, low_ref, two_ref, table_ref, *refs
):
    pair_refs, (bundle_ref, small_ref, one_ref, keep_ref, send_ref) = refs[:4], refs[4:]
    side, core = place_ref[0], place_ref[3]
    attended = jnp.concatenate(both_halves(mine_ref[...], got_ref[...], side == 0), axis=1)
    grad_out = contract_rows(attended, low_ref[...]).astype(BF16)
    total = pair_refs[0][...].astype(F32)
    for ref in pair_refs[1:]:
        total = total + ref[...].astype(F32)
    low = total.astype(BF16)
    query = query_ref[...]
    normed = normed_ref[...]
    pair = query.shape[1]
    grad_query = contract_rows(query, normed).astype(BF16)
    grad_pair = jnp.dot(low, normed, preferred_element_type=F32).astype(BF16)
    bundle_ref[:pair, :] = grad_query
    bundle_ref[pair : 3 * pair, :] = grad_pair
    bundle_ref[3 * pair : 5 * pair, :] = grad_out
    triple = jnp.concatenate([query, jnp.transpose(low)], axis=1)
    row = lax.broadcasted_iota(jnp.int32, (SMALL, LANES), 0)
    lane = lax.broadcasted_iota(jnp.int32, (8, LANES), 1)
    table = table_ref[...]
    for block in range(8):
        lanes = slice(block * LANES, (block + 1) * LANES)
        partial = contract_cols(triple, early_ref[block, :LANES, :])
        sides = both_halves(*jnp.split(partial.astype(BF16), 2, axis=0), side == 0)
        half = sides[0].shape[0] // 2
        for far in range(2):
            first, second = sides[far][:half], sides[far][half:]
            keep_ref[far, :, lanes] = jnp.where(core == 0, first, second)
            send_ref[far, :, lanes] = jnp.where(core == 0, second, first)
        one = jnp.sum(partial * normed[:, lanes].astype(F32), axis=0, keepdims=True)
        one_ref[:, lanes] = jnp.where(row == 0, one / gain_ref[0:1, lanes], 0.0).astype(BF16)
        extra = jnp.where(row == 1, two_ref[:, lanes], 0.0)
        part = lookup(table, jnp.minimum(lane + 12 * block, LANES - 1))
        for head in range(2):
            extra = jnp.where(row == 2 + head + 2 * side, part[head : head + 1], extra)
        small_ref[:, lanes] = extra.astype(BF16)


def weight_grads(place, pair_parts, query, normed, early, gains, mine, got, low, two, table):
    rows, pair = query.shape
    args = (query, normed, early, gains, mine, got, low, two, table) + tuple(pair_parts)
    half = shape((2, rows // 4, normed.shape[1]), BF16)
    small = shape((SMALL, normed.shape[1]), BF16)
    out = [shape((BUNDLE, normed.shape[1]), BF16), small, small, half, half]
    return simple(weight_grads_kernel, "weight_grads", out, args, place, micros=4)


BUNDLE = 640


def fold_bundle_kernel(parts_ref, own_ref, a_ref, b_ref, c_ref, out_ref):
    height = parts_ref.shape[1]
    for half in range(2):
        total = parts_ref[4 * half].astype(F32)
        for block in range(4 * half + 1, 4 * half + 4):
            total = total + parts_ref[block].astype(F32)
        out_ref[half * height : (half + 1) * height, :] = total.astype(BF16)
    units = own_ref[0].astype(F32)
    for ref in (a_ref, b_ref, c_ref):
        units = units + ref[...].astype(F32)
    out_ref[2 * height :, :] = units.astype(BF16)


def fold_bundle(parts, own, others):
    out = shape((2 * parts.shape[1] + own.shape[1], LANES), BF16)
    return simple(fold_bundle_kernel, "fold_bundle", out, (parts, own) + tuple(others), micros=2)


def finish_kernel(place_ref, *refs):
    parts, outs, sides = refs[:4], refs[4:-1], refs[-1]
    pair = outs[0].shape[1] // 2
    height = sides.shape[1] // 4
    block = height + SMALL
    units = (parts[0].shape[0] - 2 * block) // 3
    small = jnp.zeros((SMALL, LANES), F32)
    for hop, part in zip(HOPS, parts):
        chunk = lax.rem(place_ref[2] - hop + 4, 4)
        here = pl.ds(pl.multiple_of(chunk * height, 16), height)
        for half in range(2):
            first = half * block
            sides[half, here, :] = part[first : first + height, :].astype(F32)
            small = small + part[first + height : first + block, :].astype(F32)
        here = pl.ds(pl.multiple_of(chunk * units, 16), units)
        for at, out_ref in enumerate(outs[4:7]):
            first = 2 * block + at * units
            out_ref[here, :] = part[first : first + units, :].astype(F32)
    for half in range(2):
        cols = slice(half * pair, (half + 1) * pair)
        for at in range(3):
            outs[at][:, cols] = jnp.transpose(sides[half, at * pair : (at + 1) * pair, :])
        rows = slice((3 + half) * pair, (4 + half) * pair)
        outs[3][:, cols] = jnp.transpose(sides[0, rows, :] + sides[1, rows, :])
    outs[7][...] = small


def finish(place, parts, pair):
    units = (parts[0].shape[0] - BUNDLE // 2 - 2 * SMALL) // 3
    out = [shape((LANES, 2 * pair), F32)] * 4 + [shape((4 * units, LANES), F32)] * 3
    out = out + [shape((SMALL, LANES), F32)]
    return pl.pallas_call(
        finish_kernel,
        grid=(1,),
        in_specs=[SMEM] + whole(*parts),
        out_specs=whole(*out),
        out_shape=out,
        scratch_shapes=[pltpu.VMEM((2, BUNDLE, LANES), F32)],
        compiler_params=params(),
        cost_estimate=cost(2),
        name="finish",
    )(place, *parts)


def spread_kernel(parts_ref, small_ref, one_ref, got_ref, out_ref):
    total = parts_ref[0].astype(F32)
    for at in range(1, 4):
        total = total + parts_ref[at].astype(F32)
    small = small_ref[...].astype(F32) + one_ref[...].astype(F32) + got_ref[...].astype(F32)
    total = jnp.concatenate([total.astype(BF16), small.astype(BF16)], axis=0)
    for block in range(8):
        out_ref[block] = total[:, block * LANES : (block + 1) * LANES]


def spread(parts, small, one, one_got, deps):
    out = shape((8, parts.shape[1] + SMALL, LANES), BF16)
    return simple(spread_kernel, "spread", out, (parts, small, one, one_got), deps=deps)


def swap(values, axis_name, count, bit):
    return lax.ppermute(values, axis_name, [(at, at ^ bit) for at in range(count)])


def swap_core(values):
    return swap(values, "mp", 4, 1)


def swap_chip(values):
    return swap(values, "mp", 4, 2)


def swap_side(values):
    return swap(values, "blk", 8, 4)


def turn_z(values, hop):
    return lax.ppermute(values, "blk", [(at, at // 4 * 4 + (at - hop) % 4) for at in range(8)])


def step_dp(values, hop):
    return lax.ppermute(values, "dp", [(at, (at + hop) % 4) for at in range(4)])


def turn_dp(values):
    return [step_dp(values, hop) for hop in (1, 3, 2)]


def turn_z(values, hop):
    return lax.ppermute(values, "blk", [(at, at // 4 * 4 + (at - hop) % 4) for at in range(8)])


def spread_gather(values, axis_name, count):
    wide = jnp.broadcast_to(values[None], (count,) + values.shape)
    return lax.all_to_all(wide, axis_name, 0, 0, tiled=False)


def sum_chips(values, core, meanwhile=()):
    return join_cores(values, after(swap(values, "mp", 4, 2), meanwhile), core)


def join_cores(values, got, core):
    total = (values.astype(F32) + got.astype(F32)).astype(BF16)
    got = swap(total, "mp", 4, 1)
    first = jnp.where(core == 0, total, got)
    second = jnp.where(core == 0, got, total)
    return jnp.concatenate([first, second], axis=0)


def pick(values, at, axis):
    return lax.dynamic_index_in_dim(values, at, axis, keepdims=False)


def sum_cores(values, core):
    rows, model = values.shape
    halves = values.reshape(2, rows // 2, model)
    got = swap(pick(halves, 1 - core, 0), "mp", 4, 1)
    return (pick(halves, core, 0).astype(F32) + got.astype(F32)).astype(BF16)


def shards(
    tokens,
    cotangent,
    seg_ids,
    token_boxes,
    norm1_gain,
    w_query,
    w_key,
    w_value,
    w_out_t,
    bias_table,
    norm2_gain,
    w_gate,
    w_up,
    w_down_t,
):
    rows = tokens.shape[0]
    pair = w_query.shape[1] // 2
    blk, mp, data = lax.axis_index("blk"), lax.axis_index("mp"), lax.axis_index("dp")
    place = jnp.stack([blk // 4, blk % 4, data, mp % 2]).astype(jnp.int32)

    tokens_other = swap_side(jnp.concatenate([tokens, unfold_rows(w_out_t)], axis=0))
    table = jnp.pad(bias_table.T, ((6, 6), (0, rows - bias_table.shape[0])))
    early, late = pack(
        place,
        (
            seg_ids.reshape(1, rows),
            token_boxes,
            norm1_gain.reshape(1, LANES),
            norm2_gain.reshape(1, LANES),
            table,
        ),
        (w_query, w_key, w_value),
        (w_gate.T, w_up.T, w_down_t.T),
    )
    early_all = lax.all_to_all(early, "blk", 0, 0, tiled=False)

    turned = [turn_z(late, hop) for hop in (1, 2, 3)]
    scaled, out_w_both = scale_tokens(place, tokens, tokens_other, w_out_t)
    near = stack([late] + turned, (scaled,))
    before_near, behind_near = step_dp(near, 1), step_dp(near, 3)
    normed_one, queries, own_pairs, gains, key_meta, meta, table = project(
        place, early_all, scaled, out_w_both, ()
    )
    pairs = lax.all_to_all(
        own_pairs, "blk", 0, 0, axis_index_groups=[[0, 1, 2, 3], [4, 5, 6, 7]]
    )
    far = swap_side(near)
    after_near = step_dp(before_near, 1)
    bias = bias_scores(place, meta, key_meta, table, (before_near, behind_near))
    probs, attn_exact, attn_mine, attn_other = attend(
        place, queries, pairs, bias, (far,)
    )
    before_far, behind_far = step_dp(far, 1), step_dp(far, 3)
    after_far = step_dp(behind_far, 3)

    attn_got = swap_side(attn_other)
    keep, send = branch_part(place, attn_mine, attn_got, pairs, (before_far, behind_far, after_near))
    pieces = [near, far, before_near, before_far, behind_near, behind_far, after_near, after_far]
    ffn_w, hidden_grad = ffn_prepare(place, cotangent, pieces)
    part = add(keep, swap_core(send))
    branch = add(part, swap_chip(part), (ffn_w,))
    branch_got = swap_core(branch)
    normed_two, parts, keep, send = ffn_forward(
        place, tokens, branch, branch_got, gains, hidden_grad, ffn_w
    )
    part = add(keep, swap_core(send))
    ffn_grads = ffn_back(place, parts, normed_two, cotangent, (part,))
    grad = add(part, swap_chip(part), (ffn_grads,))
    middle_grad, branch_low, gain_two_grad, grad_mine, grad_other = middle_back(
        place, tokens, branch, branch_got, cotangent, gains, grad, swap_core(grad), pairs
    )
    ffn_grads = lax.all_to_all(ffn_grads, "dp", 0, 0, tiled=False)
    keep, send = ffn_output(place, parts, ffn_w, (grad_other,))
    out_part = add(keep, swap_core(send))
    out_got = swap_chip(out_part)
    score_grad, *pair_grads, query_low = attend_back(
        place, queries, grad_mine, swap_side(grad_other), attn_exact, pairs, probs, (out_part,)
    )
    pair_parts = pair_grads[:1] + [turn_z(pair_grads[hop], -hop) for hop in (1, 2, 3)]
    table_grad = table_grad_sums(meta, key_meta, score_grad, (out_got,))
    bundle, small, one, keep, send = weight_grads(
        place,
        pair_parts,
        query_low,
        normed_one,
        early_all,
        gains,
        attn_mine,
        attn_got,
        branch_low,
        gain_two_grad,
        table_grad,
    )
    bundle = bundle.reshape(4, BUNDLE // 4, -1)
    bundle = lax.all_to_all(bundle, "dp", 0, 0, tiled=False)
    ffn_parts = fold_to_blocks(place, ffn_grads, (send,))
    ffn_near = add(ffn_parts[0], swap_side(ffn_parts[1]))
    one = add(one, swap_core(one))
    bundle = spread(bundle, small, one, swap_chip(one), (ffn_near,))
    bundle = lax.all_to_all(bundle, "blk", 0, 0, tiled=False)
    ffn_turned = [turn_z(ffn_near[hop], -hop) for hop in (1, 2, 3)]
    folded = fold_bundle(bundle, ffn_near, ffn_turned)
    grad_query, grad_key, grad_value, grad_out, *ffn_final, small = finish(
        place, [folded] + turn_dp(folded), pair
    )

    part = add(keep, swap_core(send), (ffn_near,))
    part = add(part[0], swap_side(part[1]))
    grad = add(part, swap_chip(part))
    tokens_grad = tokens_back(place, tokens, gains, grad, swap_core(grad), middle_grad)

    out_sum = add(out_part, out_got, (ffn_near,))
    mixed = simple(
        mixed_kernel,
        "mixed",
        shape(tokens.shape, BF16),
        (tokens, branch, branch_got, out_sum, swap_core(out_sum)),
        place,
    )

    return (
        mixed,
        tokens_grad,
        small[0],
        grad_query,
        grad_key,
        grad_value,
        grad_out,
        small[2:6, :12].T,
        small[1],
        ffn_final[0].T,
        ffn_final[1].T,
        ffn_final[2].T,
    )


def solution(mesh):
    rows = P(("dp", "blk"), None)
    weight = P("blk", "mp")
    in_specs = (
        rows,
        rows,
        P(("dp", "blk")),
        P(None, ("dp", "blk")),
        P("blk"),
        weight,
        weight,
        weight,
        weight,
        weight,
        P("blk"),
        weight,
        weight,
        weight,
    )
    out_specs = (
        rows,
        rows,
        P("blk"),
        weight,
        weight,
        weight,
        weight,
        weight,
        P("blk"),
        weight,
        weight,
        weight,
    )
    return jax.shard_map(shards, mesh=mesh, in_specs=in_specs, out_specs=out_specs, check_vma=False)
```

```python
import functools

import jax
import jax.numpy as jnp
from jax import lax
from jax.experimental import pallas as pl
from jax.experimental.pallas import tpu as pltpu
from jax.sharding import PartitionSpec as P

HEAD_DIM = 64
EPS = 1e-06
SEQ_EDGES = (1, 2, 3, 4, 5, 6, 7, 8, 12, 16, 23, 32, 46, 64, 91)
BOX_EDGES = (2, 4, 6, 8, 12, 16, 24, 32, 48, 64, 96, 128, 192, 256, 384)
BF16 = jnp.bfloat16
F32 = jnp.float32
LANES = 128
MIB = 2**20
VMEM_MIB = 32
PREP = 10
SMEM = pl.BlockSpec(memory_space=pltpu.SMEM)


def whole(*arrays):
    return [pl.BlockSpec(item.shape, lambda s, rank=len(item.shape): (0,) * rank) for item in arrays]


def shape(dims, kind):
    return jax.ShapeDtypeStruct(dims, kind)


HBM = pl.BlockSpec(memory_space=pl.ANY)


def simple(kernel, name, out, args, place=None, deps=(), micros=0.05, mib=VMEM_MIB):
    count = len(args) + (place is not None)

    def body(*refs):
        kernel(*refs[:count], *refs[count + len(deps) :])

    single = not isinstance(out, list)
    specs = whole(*([out] if single else out))
    return pl.pallas_call(
        body,
        grid=(1,),
        in_specs=[SMEM] * (place is not None) + whole(*args) + [HBM] * len(deps),
        out_specs=specs[0] if single else specs,
        out_shape=out,
        compiler_params=params(mib),
        cost_estimate=cost(micros),
        name=name,
    )(*([place] if place is not None else []), *args, *deps)


def add_kernel(a_ref, b_ref, out_ref):
    out_ref[...] = (a_ref[...].astype(F32) + b_ref[...].astype(F32)).astype(BF16)


def add(a, b, deps=()):
    return simple(add_kernel, "add", shape(a.shape, BF16), (a, b), deps=deps)


def stack_kernel(*refs):
    for at, ref in enumerate(refs[:-1]):
        refs[-1][at] = ref[...]


def stack(parts, deps=()):
    out = shape((len(parts),) + parts[0].shape, BF16)
    return simple(stack_kernel, "stack", out, parts, deps=deps)


def both_halves(own, got, first):
    return jnp.where(first, own, got), jnp.where(first, got, own)


def keep_and_send(values, core, keep_ref, send_ref):
    half = values.shape[0] // 2
    first, second = values[:half], values[half:]
    keep_ref[...] = jnp.where(core == 0, first, second)
    send_ref[...] = jnp.where(core == 0, second, first)


def params(mib=VMEM_MIB):
    return pltpu.CompilerParams(
        vmem_limit_bytes=mib * MIB, dimension_semantics=("arbitrary",)
    )


def cost(micros):
    return pl.CostEstimate(flops=int(micros * 1.1e9), bytes_accessed=int(micros * 1e5), transcendentals=0)


def contract_rows(left, right):
    return lax.dot_general(
        left, right, (((0,), (0,)), ((), ())), preferred_element_type=jnp.float32
    )


def contract_cols(left, right):
    return lax.dot_general(
        left, right, (((1,), (1,)), ((), ())), preferred_element_type=jnp.float32
    )


def count_edges(magnitude, edge_list):
    result = jnp.zeros(magnitude.shape, jnp.int32)
    for border in edge_list:
        result = result + (magnitude >= border).astype(jnp.int32)
    return result


def box_cell(offset):
    half = jnp.abs(offset) >> 1
    cell = jnp.where(half < 32, half, (half >> 4) + 30)
    return cell + jnp.where(offset > 0, 64, 0)


def cell_bucket(cell):
    low = cell & 63
    half = jnp.where(low < 32, low, (low - 30) << 4)
    return count_edges(half * 2, BOX_EDGES) + jnp.where(cell >= 64, 16, 0)


def lookup(table, index):
    return jnp.take_along_axis(table, index, axis=1, mode="promise_in_bounds")


SMALL = 16


def pack_kernel(
    place_ref, seg_hbm, box_hbm, one_hbm, two_hbm, table_hbm, query_hbm, key_hbm, value_hbm, gate_hbm, up_hbm, down_hbm, early_ref, late_ref, *rest
):
    refs, sems = rest[:-1], rest[-1]
    units = gate_hbm.shape[0] // 4
    mine = pl.ds(pl.multiple_of(place_ref[2] * units, 16), units)
    sources = [seg_hbm, box_hbm, one_hbm, two_hbm, table_hbm, query_hbm, key_hbm, value_hbm]
    copies = [pltpu.make_async_copy(src, dst, sems.at[at]) for at, (src, dst) in enumerate(zip(sources, refs))]
    for at, src in enumerate((gate_hbm, up_hbm, down_hbm)):
        spot = late_ref.at[at * units : (at + 1) * units, :]
        copies.append(pltpu.make_async_copy(src.at[mine, :], spot, sems.at[len(sources) + at]))
    for copy in copies:
        copy.start()
    for copy in copies:
        copy.wait()
    seg_ref, box_ref, one_ref, two_ref, table_ref, query_ref, key_ref, value_ref = refs
    width = seg_ref.shape[1]
    pair = query_ref.shape[1] // 2
    row = lax.broadcasted_iota(jnp.int32, (SMALL, width), 0)
    boxes = box_ref[...]
    centre_x = boxes[0:1] + boxes[2:3]
    centre_y = boxes[1:2] + boxes[3:4]
    gains = jnp.concatenate([one_ref[...], two_ref[...]], axis=1).astype(F32)
    small = table_ref[...].astype(F32)
    for at, values in enumerate(
        (seg_ref[...], centre_x >> 8, centre_x & 255, centre_y >> 8, centre_y & 255, gains)
    ):
        small = jnp.where(row == at, values.astype(F32), small)
    small = small.astype(BF16)
    small = jnp.concatenate([small, jnp.zeros((SMALL, 3 * pair - width), BF16)], axis=1)
    for block in range(early_ref.shape[0]):
        half = block // 4
        cols = slice(half * pair, (half + 1) * pair)
        for at, ref in enumerate((query_ref, key_ref, value_ref)):
            early_ref[block, :LANES, at * pair : (at + 1) * pair] = ref[:, cols]
        early_ref[block, LANES:, :] = small


def pack(place, small, weights, late):
    pair = weights[0].shape[1] // 2
    args = small + weights
    out = [
        shape((8, LANES + SMALL, 3 * pair), BF16),
        shape((3 * late[0].shape[0] // 4, LANES), BF16),
    ]
    return pl.pallas_call(
        pack_kernel,
        grid=(1,),
        in_specs=[SMEM] + [HBM] * (len(args) + 3),
        out_specs=whole(*out),
        out_shape=out,
        scratch_shapes=[pltpu.VMEM(item.shape, item.dtype) for item in args]
        + [pltpu.SemaphoreType.DMA((len(args) + 3,))],
        compiler_params=params(64),
        cost_estimate=cost(0.05),
        name="pack",
    )(place, *args, *late)


def unfold_rows(values):
    return jnp.concatenate(jnp.split(values, 4, axis=0), axis=1)


def fold_rows(values):
    return jnp.concatenate(jnp.split(values, 4, axis=1), axis=0)


def scale_tokens_kernel(place_ref, own_ref, other_ref, out_w_ref, scaled_ref, wide_ref):
    rows = own_ref.shape[0]
    side = place_ref[0]
    for ref, half in ((own_ref, side), (other_ref, 1 - side)):
        inputs = ref[:rows, :].astype(F32)
        here = pl.ds(pl.multiple_of(half * rows, rows), rows)
        scaled_ref[here, :] = inputs * rms_scale(inputs)
    for values, half in ((out_w_ref[...], side), (fold_rows(other_ref[rows:, :]), 1 - side)):
        wide_ref[pl.ds(pl.multiple_of(half * LANES, LANES), LANES), :] = values


def scale_tokens(place, own, other, out_w):
    rows, model = own.shape
    out = [shape((2 * rows, model), F32), shape((2 * LANES, out_w.shape[1]), BF16)]
    return simple(scale_tokens_kernel, "scale_tokens", out, (own, other, out_w), place, micros=PREP)


def project_kernel(
    place_ref, early_ref, scaled_ref, out_w_ref, normed_ref, query_ref, pair_ref, gain_ref, key_ref, meta_ref, table_ref
):
    rows = scaled_ref.shape[0] // 2
    pair = query_ref.shape[1]
    side, depth = place_ref[0], place_ref[1]
    small = [early_ref[block, LANES:, :rows].astype(F32) for block in range(8)]
    for at in range(2):
        lanes = slice(at * LANES, (at + 1) * LANES)
        gain = jnp.concatenate([part[5:6, lanes] for part in small], axis=1)
        gain_ref[at : at + 1, :] = gain
        if at == 0:
            gain_one = gain

    for copy in range(4):
        pair_ref[copy, 2 * rows :, :] = out_w_ref[...]
    weight = jnp.concatenate([early_ref[block, :LANES, :] for block in range(8)], axis=0)
    normed = (scaled_ref[...] * gain_one).astype(BF16)
    normed_ref[...] = normed
    result = jnp.dot(normed, weight, preferred_element_type=F32).astype(BF16)
    query_ref[...] = result[:, :pair] * jnp.asarray(HEAD_DIM ** (-0.5), BF16)
    for copy in range(4):
        pair_ref[copy, : 2 * rows, :] = result[:, pair:]

    time = lax.broadcasted_iota(jnp.int32, (1, rows), 1)
    for block in range(8):
        part = small[block]
        at = (block % 4) * 2 + block // 4
        there = slice(at * rows, (at + 1) * rows)
        key_ref[0:1, there] = part[0:1].astype(jnp.int32)
        key_ref[1:2, there] = (part[1:2] * 256.0 + part[2:3]).astype(jnp.int32)
        key_ref[2:3, there] = (part[3:4] * 256.0 + part[4:5]).astype(jnp.int32)
        for half in range(2):
            ahead = (block - depth - 4 * half) * rows + SEQ_SPAN // 4
            key_ref[3 + half : 4 + half, there] = jnp.clip(time + ahead, 0, SEQ_SPAN - 1)
        key_ref[5:8, there] = jnp.zeros((3, rows), jnp.int32)

    for half in range(2):
        part = early_ref[depth + 4 * half, LANES:, :rows].astype(F32)
        columns = jnp.transpose(part)
        seg = columns[:, 0:1]
        centre_x = columns[:, 1:2] * 256.0 + columns[:, 2:3]
        centre_y = columns[:, 3:4] * 256.0 + columns[:, 4:5]
        for at, values in enumerate((seg, centre_x, centre_y)):
            wide = jnp.broadcast_to(values.astype(jnp.int32), (rows, LANES))
            meta_ref[at, half * rows : (half + 1) * rows, :] = wide

    lane = lax.broadcasted_iota(jnp.int32, (8, LANES), 1)
    table = jnp.zeros((8, LANES), F32)
    for block in range(8):
        entries = jnp.where(side == 0, small[block][6:8, :LANES], small[block][8:10, :LANES])
        entries = jnp.concatenate([entries, jnp.zeros((6, LANES), F32)], axis=0)
        index = jnp.clip(lane - 12 * block, 0, LANES - 1)
        found = lookup(entries, index)
        table = jnp.where((lane >= 12 * block) & (lane < 12 * block + 12), found, table)
    table_ref[...] = table


def project(place, early, scaled, out_w, deps):
    rows, model = scaled.shape[0] // 2, scaled.shape[1]
    pair = early.shape[2] // 3
    out = [
        shape((2 * rows, model), BF16),
        shape((2 * rows, pair), BF16),
        shape((4, 2 * rows + 2 * LANES, 2 * pair), BF16),
        shape((2, model), F32),
        shape((8, 8 * rows), jnp.int32),
        shape((3, 2 * rows, LANES), jnp.int32),
        shape((8, LANES), F32),
    ]
    return simple(
        project_kernel, "project", out, (early, scaled, out_w), place, deps, 0.05, 64
    )


STEPS = 3600.0
SHIFT = 10800.0
MASKED = -(2**31)


def bias_kernel(place_ref, meta_ref, key_ref, table_ref, *refs):
    bias_ref = refs[-1]
    chunk, length = bias_ref.shape
    width = TOKENS_BLOCK
    step = pl.program_id(0)
    half = step // (2 * width // chunk // 2)
    first_row = lax.rem(step * chunk, width)
    query_block = place_ref[1] + 4 * half
    lane = lax.broadcasted_iota(jnp.int32, (8, LANES), 1)
    buckets = cell_bucket(lane)
    table = table_ref[...]

    def packed(index):
        found = lookup(table, index)
        high = jnp.round(found[0:1, :] * STEPS).astype(jnp.int32)
        low = jnp.round(found[1:2, :] * STEPS + SHIFT).astype(jnp.int32)
        return (high << 16) + low

    def spread(values):
        return jnp.broadcast_to(values, (chunk, LANES))

    hor = packed(buckets + 32)
    ver = spread(packed(buckets + 64))
    seq_count = count_edges(jnp.abs(lane - 64), SEQ_EDGES) + jnp.where(lane > 64, 16, 0)
    seq = spread(packed(seq_count))
    behind, middle, beyond = [packed(jnp.full((8, LANES), at, jnp.int32)) for at in (15, 30, 31)]

    def key_block(at):
        return at // 2 + 4 * lax.rem(at, 2)

    def block_of_keys(at, with_near):
        ahead = key_block(at) * width - query_block * width - first_row
        far = spread(hor if with_near else hor + jnp.where(ahead > 0, beyond, behind))
        for column in range(width // LANES):
            there = pl.ds(pl.multiple_of(at * width + column * LANES, LANES), LANES)
            keys = key_ref[:, there]
            total = lookup(far, box_cell(keys[1:2, :] - meta_ref[1]))
            total = total + lookup(ver, box_cell(keys[2:3, :] - meta_ref[2]))
            if with_near:
                row = lax.broadcasted_iota(jnp.int32, (chunk, LANES), 0)
                col = lax.broadcasted_iota(jnp.int32, (chunk, LANES), 1)
                offset = col - row + (ahead + column * LANES)
                found = lookup(seq, jnp.clip(offset + 64, 0, LANES - 1))
                found = jnp.where(offset >= 64, middle, found)
                found = jnp.where(offset >= 91, beyond, found)
                total = total + jnp.where(offset <= -91, behind, found)
            bias_ref[:, there] = jnp.where(keys[0:1, :] == meta_ref[0], total, MASKED)

    def body(at, carry):
        near = jnp.abs(key_block(at) - query_block) <= 1
        pl.when(near)(functools.partial(block_of_keys, at, True))
        pl.when(jnp.logical_not(near))(functools.partial(block_of_keys, at, False))
        return carry

    lax.fori_loop(0, length // width, body, 0)


TOKENS_BLOCK = 256


def bias_scores(place, meta, key_meta, table, deps):
    rows = meta.shape[1]
    length = key_meta.shape[1]
    chunk = 128
    return pl.pallas_call(
        bias_kernel,
        grid=(rows // chunk,),
        in_specs=[
            pl.BlockSpec(memory_space=pltpu.SMEM),
            pl.BlockSpec((3, chunk, LANES), lambda s: (0, s, 0)),
            pl.BlockSpec((8, length), lambda s: (0, 0)),
            pl.BlockSpec((8, LANES), lambda s: (0, 0)),
        ]
        + [HBM] * len(deps),
        out_specs=pl.BlockSpec((chunk, length), lambda s: (s, 0)),
        out_shape=jax.ShapeDtypeStruct((rows, length), jnp.int32),
        compiler_params=params(64),
        cost_estimate=cost(10),
        name="bias_scores",
    )(place, meta, key_meta, table, *deps)


def head_masks(shape):
    lane = lax.broadcasted_iota(jnp.int32, shape, 1)
    return lane < HEAD_DIM, lane >= HEAD_DIM


def attend_kernel(place_ref, query_ref, bias_ref, pair_ref, *refs):
    probs_ref, exact_ref, mine_ref, other_ref = refs[-4:]
    count, _, both = pair_ref.shape
    width = bias_ref.shape[1] // count
    features = both // 2
    rows = query_ref.shape[0]
    masks = head_masks((rows, features))
    query = query_ref[...]
    allowed = []
    codes = []
    for at in range(count):
        code = bias_ref[:, at * width : (at + 1) * width]
        codes.append(code)
        allowed.append(code != MASKED)
    outs = []
    for head in range(2):
        mine = jnp.where(masks[head], query, jnp.zeros_like(query))
        scores = []
        for at in range(count):
            code = (codes[at] >> 16) if head == 0 else (codes[at] & 65535)
            score = contract_cols(mine, pair_ref[at, :width, :features])
            score = score + code.astype(F32) * (1.0 / STEPS)
            scores.append(jnp.where(allowed[at], score, -1e30))
        top = functools.reduce(jnp.maximum, scores)
        top = jnp.max(top, axis=1, keepdims=True)
        weights = [jnp.exp(score - top) for score in scores]
        total = functools.reduce(jnp.add, weights)
        inverse = 1.0 / jnp.sum(total, axis=1, keepdims=True)
        result = None
        for at in range(count):
            low = (weights[at] * inverse).astype(BF16)
            probs_ref[head, :, at * width : (at + 1) * width] = low
            part = jnp.dot(low, pair_ref[at, :width, features:], preferred_element_type=F32)
            result = part if result is None else result + part
        outs.append(result)
    exact = jnp.where(masks[0], outs[0], outs[1])
    exact_ref[...] = exact
    low = exact.astype(BF16)
    tiles = mine_ref.shape[0] // rows
    step = pl.program_id(0)
    here = pl.ds(pl.multiple_of(lax.rem(step, tiles) * rows, rows), rows)
    own = step // tiles == place_ref[0]

    @pl.when(own)
    def _():
        mine_ref[here, :] = low

    @pl.when(jnp.logical_not(own))
    def _():
        other_ref[here, :] = low


def attend(place, queries, pairs, bias, deps):
    rows, length = bias.shape
    both = pairs.shape[2]
    tile = 128
    features = both // 2
    slim = pl.BlockSpec((tile, features), lambda s: (s, 0))
    half = shape((rows // 2, features), BF16)
    return pl.pallas_call(
        attend_kernel,
        grid=(rows // tile,),
        in_specs=[SMEM, slim, pl.BlockSpec((tile, length), lambda s: (s, 0))]
        + whole(pairs)
        + [HBM] * len(deps),
        out_specs=[pl.BlockSpec((2, tile, length), lambda s: (0, s, 0)), slim] + whole(half, half),
        out_shape=[
            shape((2, rows, length), BF16),
            shape((rows, features), F32),
            half,
            half,
        ],
        compiler_params=params(64),
        cost_estimate=cost(9),
        name="attend",
    )(place, queries, bias, pairs, *deps)


def out_weight(pair_ref):
    start = pair_ref.shape[1] - 2 * LANES
    parts = []
    for block in range(8):
        first = start + block // 4 * LANES
        parts.append(pair_ref[block % 4, first : first + LANES, :])
    return jnp.concatenate(parts, axis=0)


def branch_kernel(place_ref, mine_ref, got_ref, pair_ref, keep_ref, send_ref):
    parts = both_halves(mine_ref[...], got_ref[...], place_ref[0] == 0)
    attended = jnp.concatenate(parts, axis=1)
    result = contract_cols(attended, out_weight(pair_ref)).astype(BF16)
    keep_and_send(result, place_ref[3], keep_ref, send_ref)


def branch_part(place, mine, got, pairs, deps):
    half = shape((mine.shape[0] // 2, 8 * LANES), BF16)
    return simple(branch_kernel, "branch_part", [half, half], (mine, got, pairs), place, deps, 2)


def gelu_parts(gate):
    rate = 0.7978845608028654
    square = gate * gate
    slope = jnp.tanh(rate * gate * (1.0 + 0.044715 * square))
    half = 0.5 * (1.0 + slope)
    inner = rate * (1.0 + 3.0 * 0.044715 * square)
    return gate * half, half + 0.5 * gate * (1.0 - slope * slope) * inner


def piece_copies(place_ref, piece_refs, held, sems, hop, first):
    side, depth = place_ref[0], place_ref[1]
    height = held.shape[1]
    copies = []
    for far in range(2):
        for turn in range(4):
            block = (side + far * (1 - 2 * side)) * 4 + lax.rem(depth + turn, 4)
            lanes = pl.ds(pl.multiple_of(block * LANES, LANES), LANES)
            copies.append(
                pltpu.make_async_copy(
                    piece_refs[2 * hop + far].at[turn, pl.ds(first, height), :],
                    held.at[hop, :, lanes],
                    sems.at[hop, 4 * far + turn],
                )
            )
    return copies


def ffn_prepare_kernel(place_ref, dy_ref, *refs):
    piece_refs, (weight_ref, down_ref, grad_ref, sems, down_sems) = refs[:8], refs[8:]
    units = down_ref.shape[1]
    copies = [piece_copies(place_ref, piece_refs, down_ref, down_sems, hop, 2 * units) for hop in range(4)]
    late = [piece_copies(place_ref, piece_refs, weight_ref, sems, hop, 0) for hop in range(4)]
    for group in copies + late:
        for copy in group:
            copy.start()
    for hop in range(4):
        for copy in copies[hop]:
            copy.wait()
        grad_ref[hop] = contract_cols(down_ref[hop], dy_ref[...])
    for group in late:
        for copy in group:
            copy.wait()


def ffn_prepare(place, dy, pieces):
    rows, model = dy.shape
    units = pieces[0].shape[1] // 3
    out = [
        shape((4, 2 * units, model), BF16),
        shape((4, units, model), BF16),
        shape((4, units, rows), F32),
    ]
    return pl.pallas_call(
        ffn_prepare_kernel,
        grid=(1,),
        in_specs=[SMEM] + whole(dy) + [HBM] * 8,
        out_specs=whole(*out),
        out_shape=out,
        scratch_shapes=[pltpu.SemaphoreType.DMA((4, 8)), pltpu.SemaphoreType.DMA((4, 8))],
        compiler_params=params(),
        cost_estimate=cost(4),
        name="ffn_prepare",
    )(place, dy, *pieces)


def middle_of(tokens_ref, total_ref, got_ref, core):
    branch = jnp.concatenate(both_halves(total_ref[...], got_ref[...], core == 0), axis=0)
    return tokens_ref[...].astype(F32) + branch.astype(F32)


def rms_scale(values):
    return lax.rsqrt(jnp.mean(values * values, axis=1, keepdims=True) + EPS)


def ffn_kernel(
    place_ref, tokens_ref, total_ref, got_ref, gain_ref, hidden_grad_ref, weight_ref, normed_ref, parts_ref, keep_ref, send_ref, sums, turned
):
    units = weight_ref.shape[1] // 2
    step = pl.program_id(0)

    @pl.when(step == 0)
    def _():
        middle = middle_of(tokens_ref, total_ref, got_ref, place_ref[3])
        normed = (middle * rms_scale(middle) * gain_ref[1:2, :]).astype(BF16)
        normed_ref[...] = normed
        turned[...] = jnp.transpose(normed)
        sums[...] = jnp.zeros_like(sums)

    gates = jnp.dot(weight_ref[0], turned[...], preferred_element_type=F32)
    gate, upward = gates[:units], gates[units:]
    hidden_grad = hidden_grad_ref[0]
    value, slope = gelu_parts(gate)
    grads = jnp.concatenate([hidden_grad * upward * slope, hidden_grad * value], axis=0).astype(BF16)
    parts_ref[0, : 2 * units, :] = grads
    parts_ref[0, 2 * units :, :] = (value * upward).astype(BF16)
    sums[...] += contract_rows(grads, weight_ref[0])

    @pl.when(step == pl.num_programs(0) - 1)
    def _():
        keep_and_send(sums[...].astype(BF16), place_ref[3], keep_ref, send_ref)


def ffn_forward(place, tokens, total, got, gains, hidden_grad, weights):
    rows, model = tokens.shape
    hops, height, _ = weights.shape
    half = shape((rows // 2, model), BF16)
    parts = shape((hops, height // 2 * 3, rows), BF16)
    out = [shape((rows, model), BF16), parts, half, half]

    def chunk(item):
        return pl.BlockSpec((1,) + item.shape[1:], lambda s: (s, 0, 0))

    return pl.pallas_call(
        ffn_kernel,
        grid=(hops,),
        in_specs=[SMEM]
        + whole(tokens, total, got, gains)
        + [chunk(hidden_grad), chunk(weights)],
        out_specs=whole(out[0]) + [chunk(out[1])] + whole(half, half),
        out_shape=out,
        scratch_shapes=[pltpu.VMEM((rows, model), F32), pltpu.VMEM((model, rows), BF16)],
        compiler_params=params(),
        cost_estimate=cost(5),
        name="ffn_forward",
    )(place, tokens, total, got, gains, hidden_grad, weights)


def ffn_back_kernel(place_ref, parts_ref, normed_ref, dy_ref, *refs):
    grad_ref = refs[-1]
    units = parts_ref.shape[1] // 3
    grad_ref[0, : 2 * units, :] = jnp.dot(
        parts_ref[0, : 2 * units, :], normed_ref[...], preferred_element_type=F32
    ).astype(BF16)
    grad_ref[0, 2 * units :, :] = jnp.dot(
        parts_ref[0, 2 * units :, :], dy_ref[...], preferred_element_type=F32
    ).astype(BF16)


def ffn_output_kernel(place_ref, parts_ref, weight_ref, *refs):
    keep_ref, send_ref, sums = refs[-3:]
    step = pl.program_id(0)
    part = contract_rows(parts_ref[0], weight_ref[0])

    @pl.when(step == 0)
    def _():
        sums[...] = part

    @pl.when(step > 0)
    def _():
        sums[...] += part

    @pl.when(step == pl.num_programs(0) - 1)
    def _():
        keep_and_send(sums[...].astype(BF16), place_ref[3], keep_ref, send_ref)


def ffn_output(place, parts, weights, deps):
    hops, height, rows = parts.shape
    model = weights.shape[2]
    half = shape((rows // 2, model), BF16)
    return pl.pallas_call(
        ffn_output_kernel,
        grid=(hops,),
        in_specs=[
            SMEM,
            pl.BlockSpec((1, height // 3, rows), lambda s: (s, 2, 0)),
            pl.BlockSpec((1, height // 3, model), lambda s: (s, 0, 0)),
        ]
        + [HBM] * len(deps),
        out_specs=whole(half, half),
        out_shape=[half, half],
        scratch_shapes=[pltpu.VMEM((rows, model), F32)],
        compiler_params=params(),
        cost_estimate=cost(3),
        name="ffn_output",
    )(place, parts, weights, *deps)


def norm_back(inputs, gain, normed_grad):
    scale = rms_scale(inputs)
    gain_grad = jnp.sum(normed_grad * inputs * scale, axis=0, keepdims=True)
    weighted = normed_grad * gain
    mean = jnp.mean(weighted * inputs, axis=1, keepdims=True)
    return scale * weighted - inputs * (scale * scale * scale) * mean, gain_grad


def middle_kernel(
    place_ref, tokens_ref, total_ref, got_ref, dy_ref, gain_ref, grad_ref, grad_got_ref, pair_ref, middle_ref, low_ref, two_ref, mine_ref, other_ref
):
    core = place_ref[3]
    middle = middle_of(tokens_ref, total_ref, got_ref, core)
    parts = both_halves(grad_ref[...], grad_got_ref[...], core == 0)
    normed_grad = jnp.concatenate(parts, axis=0).astype(F32)
    result, gain_grad = norm_back(middle, gain_ref[1:2, :], normed_grad)
    result = dy_ref[...].astype(F32) + result
    middle_ref[...] = result
    low = result.astype(BF16)
    low_ref[...] = low
    two_ref[...] = gain_grad
    attended = jnp.dot(low, out_weight(pair_ref), preferred_element_type=F32).astype(BF16)
    pair = attended.shape[1] // 2
    first = place_ref[0] == 0
    mine_ref[...] = jnp.where(first, attended[:, :pair], attended[:, pair:])
    other_ref[...] = jnp.where(first, attended[:, pair:], attended[:, :pair])


def middle_back(place, tokens, total, got, dy, gains, grad, grad_got, pairs):
    rows, model = tokens.shape
    half = shape((rows, pairs.shape[2] // 2), BF16)
    out = [shape((rows, model), F32), shape((rows, model), BF16), shape((1, model), F32), half, half]
    args = (tokens, total, got, dy, gains, grad, grad_got, pairs)
    return simple(middle_kernel, "middle_back", out, args, place, micros=3)


def tokens_kernel(place_ref, tokens_ref, gain_ref, grad_ref, grad_got_ref, middle_ref, out_ref):
    parts = both_halves(grad_ref[...], grad_got_ref[...], place_ref[3] == 0)
    normed_grad = jnp.concatenate(parts, axis=0).astype(F32)
    result, _ = norm_back(tokens_ref[...].astype(F32), gain_ref[0:1, :], normed_grad)
    out_ref[...] = middle_ref[...] + result


def tokens_back(place, tokens, gains, grad, grad_got, middle_grad):
    out = shape(tokens.shape, F32)
    return simple(
        tokens_kernel, "tokens_back", out, (tokens, gains, grad, grad_got, middle_grad), place, micros=2
    )


def mixed_kernel(place_ref, tokens_ref, total_ref, got_ref, out_total_ref, out_got_ref, out_ref):
    core = place_ref[3]
    middle = middle_of(tokens_ref, total_ref, got_ref, core)
    parts = both_halves(out_total_ref[...], out_got_ref[...], core == 0)
    out_ref[...] = (middle + jnp.concatenate(parts, axis=0).astype(F32)).astype(BF16)


HOPS = (0, 1, 3, 2)


def ffn_back(place, parts, normed, dy, deps):
    rows, model = normed.shape
    hops, height, _ = parts.shape

    def owner(step, place_ref):
        hop = jnp.where(step == 0, 0, jnp.where(step == 1, 1, jnp.where(step == 2, 3, 2)))
        return lax.rem(place_ref[2] - hop + 4, 4)

    def same(*arrays):
        return [pl.BlockSpec(item.shape, lambda s, p: (0, 0)) for item in arrays]

    return pl.pallas_call(
        ffn_back_kernel,
        grid_spec=pltpu.PrefetchScalarGridSpec(
            num_scalar_prefetch=1,
            grid=(hops,),
            in_specs=[pl.BlockSpec((1, height, rows), lambda s, p: (s, 0, 0))]
            + same(normed, dy)
            + [HBM] * len(deps),
            out_specs=pl.BlockSpec((1, height, model), lambda s, p: (owner(s, p), 0, 0)),
        ),
        out_shape=shape((hops, height, model), BF16),
        compiler_params=params(),
        cost_estimate=cost(4),
        name="ffn_back",
    )(place, parts, normed, dy, *deps)


def fold_kernel(place_ref, parts_ref, *refs):
    out_ref = refs[-1]
    for block in range(4):
        lanes = slice(block * LANES, (block + 1) * LANES)
        total = parts_ref[0, :, lanes].astype(F32)
        for at in range(1, parts_ref.shape[0]):
            total = total + parts_ref[at, :, lanes].astype(F32)
        out_ref[0, lax.rem(block - place_ref[1] + 4, 4)] = total.astype(BF16)


def fold_to_blocks(place, parts, deps):
    count, height, model = parts.shape
    return pl.pallas_call(
        fold_kernel,
        grid_spec=pltpu.PrefetchScalarGridSpec(
            num_scalar_prefetch=1,
            grid=(2,),
            in_specs=[pl.BlockSpec((count, height, model // 2), lambda s, p: (0, 0, s))]
            + [HBM] * len(deps),
            out_specs=pl.BlockSpec(
                (1, 4, height, LANES), lambda s, p: (jnp.where(s == p[0], 0, 1), 0, 0, 0)
            ),
        ),
        out_shape=shape((2, 4, height, LANES), BF16),
        compiler_params=params(),
        cost_estimate=cost(4),
        name="fold_to_blocks",
    )(place, parts, *deps)


def attend_back_kernel(place_ref, query_ref, mine_ref, got_ref, exact_ref, probs_ref, pair_ref, *refs):
    score_ref, pair_grad_refs = refs[-9], refs[-8:-4]
    query_grad_ref, sums, delta, grads = refs[-4:]
    _, rows, width = probs_ref.shape
    features = query_ref.shape[1]
    step = pl.program_id(0)
    masks = head_masks((rows, features))
    query = query_ref[...]

    @pl.when(step == 0)
    def _():
        sums[...] = jnp.zeros_like(sums)
        parts = both_halves(mine_ref[...], got_ref[...], place_ref[0] == 0)
        grads[...] = jnp.concatenate(parts, axis=0)
        product = grads[...].astype(F32) * exact_ref[...]
        for head in range(2):
            row = jnp.sum(jnp.where(masks[head], product, 0.0), axis=1, keepdims=True)
            delta[head] = jnp.broadcast_to(row, (rows, LANES))

    grad = grads[...]
    keys = pair_ref[0, :, :features]
    values = pair_ref[0, :, features:]
    parts = []
    key_grads = []
    value_grads = []
    for head in range(2):
        cols = slice(head * HEAD_DIM, (head + 1) * HEAD_DIM)
        mine = jnp.where(masks[head], grad, jnp.zeros_like(grad))
        probs = probs_ref[head]
        prob_grad = contract_cols(mine, values)
        offset = jnp.concatenate([delta[head]] * (width // LANES), axis=1)
        score_grad = (probs.astype(F32) * (prob_grad - offset)).astype(BF16)
        score_ref[head] = score_grad
        parts.append(jnp.dot(score_grad, keys, preferred_element_type=F32))
        key_grads.append(contract_rows(query[:, cols], score_grad).astype(BF16))
        value_grads.append(contract_rows(grad[:, cols], probs).astype(BF16))
    for at in range(4):

        @pl.when(step == at)
        def _():
            for spot, part in enumerate(key_grads + value_grads):
                pair_grad_refs[at][spot * HEAD_DIM : (spot + 1) * HEAD_DIM, :] = part

    sums[...] += jnp.where(masks[0], parts[0], parts[1])

    @pl.when(step == pl.num_programs(0) - 1)
    def _():
        query_grad_ref[...] = (sums[...] * HEAD_DIM ** (-0.5)).astype(BF16)


def attend_back(place, queries, mine, got, exact, pairs, probs, deps):
    _, rows, length = probs.shape
    features = queries.shape[1]
    width, both = rows, pairs.shape[2]

    def spot(step, place_ref):
        return lax.rem(place_ref[1] + step, 4)

    def same(*arrays):
        return [pl.BlockSpec(item.shape, lambda s, p: (0, 0)) for item in arrays]

    slab = pl.BlockSpec((2, rows, width), lambda s, p: (0, 0, spot(s, p)))
    pair_grads = [shape((both, width), BF16)] * 4
    query_grad = shape((rows, features), BF16)
    return pl.pallas_call(
        attend_back_kernel,
        grid_spec=pltpu.PrefetchScalarGridSpec(
            num_scalar_prefetch=1,
            grid=(4,),
            in_specs=same(queries, mine, got, exact)
            + [slab, pl.BlockSpec((1, width, both), lambda s, p: (spot(s, p), 0, 0))]
            + [HBM] * len(deps),
            out_specs=[slab] + same(*pair_grads, query_grad),
            scratch_shapes=[
                pltpu.VMEM((rows, features), F32),
                pltpu.VMEM((2, rows, LANES), F32),
                pltpu.VMEM((rows, features), BF16),
            ],
        ),
        out_shape=[shape((2, rows, length), BF16)] + pair_grads + [query_grad],
        compiler_params=params(),
        cost_estimate=cost(5),
        name="attend_back",
    )(place, queries, mine, got, exact, probs, pairs, *deps)


BOX_SPAN = 1024
SEQ_SPAN = 512
TILE = 512


def threshold_row(edge_list, far, lane):
    borders = [-far] + [1 - edge for edge in reversed(edge_list)] + [1] + list(edge_list)
    result = jnp.zeros(lane.shape, jnp.int32)
    for at, border in enumerate(borders):
        result = jnp.where(lane == at, border, result)
    return result


def table_grad_kernel(meta_ref, key_ref, score_ref, *refs):
    out_ref, sums_ref = refs[-2:]
    _, rows, length = score_ref.shape
    half = rows // 2
    step = pl.program_id(0)
    lane = lax.broadcasted_iota(jnp.int32, (1, LANES), 1)
    level = lax.broadcasted_iota(jnp.int32, (TILE, 1), 0)

    def add(place, key_row, mine, edges, top, offset, span):
        index = jnp.clip(mine + threshold_row(edges, 4096, lane), 0, top)
        column = index & (LANES - 1)
        block = (index - offset) >> 7
        reached = (key_ref[pl.ds(key_row, 1), :] >= level + offset).astype(F32).astype(BF16)
        for head in range(2):
            sums = contract_cols(score_ref[head, span, :], reached)
            picked = jnp.zeros(column.shape, F32)
            for at in range(TILE // LANES):
                found = lookup(sums[:, at * LANES : (at + 1) * LANES], column)
                picked = picked + jnp.where(block == at, found, 0.0)
            sums_ref[place, head : head + 1, :] += jnp.sum(picked, axis=0, keepdims=True)

    @pl.when(step == 0)
    def _():
        sums_ref[...] = jnp.zeros_like(sums_ref)

    @pl.when(step < 4)
    def _():
        axis = step // 2
        mine = meta_ref[1 + axis]
        add(1 + axis, 1 + axis, mine, BOX_EDGES, BOX_SPAN - 1, (step % 2) * TILE, slice(None))

    @pl.when(step >= 4)
    def _():
        part = step - 4
        span = pl.ds(pl.multiple_of(part * half, half), half)
        mine = lax.broadcasted_iota(jnp.int32, (half, LANES), 0) + SEQ_SPAN // 4
        add(0, 3 + part, mine, SEQ_EDGES, SEQ_SPAN - 1, 0, span)

    @pl.when(step == pl.num_programs(0) - 1)
    def _():
        lanes = lax.broadcasted_iota(jnp.int32, (8, LANES), 1)
        bucket = lanes & 31
        first = jnp.where(bucket < 16, 15 - bucket, bucket)
        result = jnp.zeros((8, LANES), F32)
        for axis in range(3):
            sums = sums_ref[axis]
            part = lookup(sums, first) - jnp.where(first == 31, 0.0, lookup(sums, first + 1))
            result = jnp.where((lanes >> 5) == axis, part, result)
        out_ref[...] = result


def table_grad_sums(meta, key_meta, score_grad, deps):
    _, rows, length = score_grad.shape
    return pl.pallas_call(
        table_grad_kernel,
        grid=(6,),
        in_specs=whole(meta, key_meta, score_grad) + [HBM] * len(deps),
        out_specs=pl.BlockSpec((8, LANES), lambda s: (0, 0)),
        out_shape=shape((8, LANES), F32),
        scratch_shapes=[pltpu.VMEM((3, 8, LANES), F32)],
        compiler_params=params(),
        cost_estimate=cost(11),
        name="table_grad",
    )(meta, key_meta, score_grad, *deps)


def weight_grads_kernel(
    place_ref, query_ref, normed_ref, early_ref, gain_ref, mine_ref, got_ref, low_ref, two_ref, table_ref, *refs
):
    pair_refs, (bundle_ref, small_ref, one_ref, keep_ref, send_ref) = refs[:4], refs[4:]
    side, core = place_ref[0], place_ref[3]
    attended = jnp.concatenate(both_halves(mine_ref[...], got_ref[...], side == 0), axis=1)
    grad_out = contract_rows(attended, low_ref[...]).astype(BF16)
    total = pair_refs[0][...].astype(F32)
    for ref in pair_refs[1:]:
        total = total + ref[...].astype(F32)
    low = total.astype(BF16)
    query = query_ref[...]
    normed = normed_ref[...]
    pair = query.shape[1]
    grad_query = contract_rows(query, normed).astype(BF16)
    grad_pair = jnp.dot(low, normed, preferred_element_type=F32).astype(BF16)
    bundle_ref[:pair, :] = grad_query
    bundle_ref[pair : 3 * pair, :] = grad_pair
    bundle_ref[3 * pair : 5 * pair, :] = grad_out
    triple = jnp.concatenate([query, jnp.transpose(low)], axis=1)
    row = lax.broadcasted_iota(jnp.int32, (SMALL, LANES), 0)
    lane = lax.broadcasted_iota(jnp.int32, (8, LANES), 1)
    table = table_ref[...]
    for block in range(8):
        lanes = slice(block * LANES, (block + 1) * LANES)
        partial = contract_cols(triple, early_ref[block, :LANES, :])
        sides = both_halves(*jnp.split(partial.astype(BF16), 2, axis=0), side == 0)
        half = sides[0].shape[0] // 2
        for far in range(2):
            first, second = sides[far][:half], sides[far][half:]
            keep_ref[far, :, lanes] = jnp.where(core == 0, first, second)
            send_ref[far, :, lanes] = jnp.where(core == 0, second, first)
        one = jnp.sum(partial * normed[:, lanes].astype(F32), axis=0, keepdims=True)
        one_ref[:, lanes] = jnp.where(row == 0, one / gain_ref[0:1, lanes], 0.0).astype(BF16)
        extra = jnp.where(row == 1, two_ref[:, lanes], 0.0)
        part = lookup(table, jnp.minimum(lane + 12 * block, LANES - 1))
        for head in range(2):
            extra = jnp.where(row == 2 + head + 2 * side, part[head : head + 1], extra)
        small_ref[:, lanes] = extra.astype(BF16)


def weight_grads(place, pair_parts, query, normed, early, gains, mine, got, low, two, table):
    rows, pair = query.shape
    args = (query, normed, early, gains, mine, got, low, two, table) + tuple(pair_parts)
    half = shape((2, rows // 4, normed.shape[1]), BF16)
    small = shape((SMALL, normed.shape[1]), BF16)
    out = [shape((BUNDLE, normed.shape[1]), BF16), small, small, half, half]
    return simple(weight_grads_kernel, "weight_grads", out, args, place, micros=4)


BUNDLE = 640


def fold_bundle_kernel(parts_ref, own_ref, a_ref, b_ref, c_ref, out_ref):
    height = parts_ref.shape[1]
    for half in range(2):
        total = parts_ref[4 * half].astype(F32)
        for block in range(4 * half + 1, 4 * half + 4):
            total = total + parts_ref[block].astype(F32)
        out_ref[half * height : (half + 1) * height, :] = total.astype(BF16)
    units = own_ref[0].astype(F32)
    for ref in (a_ref, b_ref, c_ref):
        units = units + ref[...].astype(F32)
    out_ref[2 * height :, :] = units.astype(BF16)


def fold_bundle(parts, own, others):
    out = shape((2 * parts.shape[1] + own.shape[1], LANES), BF16)
    return simple(fold_bundle_kernel, "fold_bundle", out, (parts, own) + tuple(others), micros=2)


def finish_kernel(place_ref, *refs):
    parts, outs, sides = refs[:4], refs[4:-1], refs[-1]
    pair = outs[0].shape[1] // 2
    height = sides.shape[1] // 4
    block = height + SMALL
    units = (parts[0].shape[0] - 2 * block) // 3
    small = jnp.zeros((SMALL, LANES), F32)
    for hop, part in zip(HOPS, parts):
        chunk = lax.rem(place_ref[2] - hop + 4, 4)
        here = pl.ds(pl.multiple_of(chunk * height, 16), height)
        for half in range(2):
            first = half * block
            sides[half, here, :] = part[first : first + height, :].astype(F32)
            small = small + part[first + height : first + block, :].astype(F32)
        here = pl.ds(pl.multiple_of(chunk * units, 16), units)
        for at, out_ref in enumerate(outs[4:7]):
            first = 2 * block + at * units
            out_ref[here, :] = part[first : first + units, :].astype(F32)
    for half in range(2):
        cols = slice(half * pair, (half + 1) * pair)
        for at in range(3):
            outs[at][:, cols] = jnp.transpose(sides[half, at * pair : (at + 1) * pair, :])
        rows = slice((3 + half) * pair, (4 + half) * pair)
        outs[3][:, cols] = jnp.transpose(sides[0, rows, :] + sides[1, rows, :])
    outs[7][...] = small


def finish(place, parts, pair):
    units = (parts[0].shape[0] - BUNDLE // 2 - 2 * SMALL) // 3
    out = [shape((LANES, 2 * pair), F32)] * 4 + [shape((4 * units, LANES), F32)] * 3
    out = out + [shape((SMALL, LANES), F32)]
    return pl.pallas_call(
        finish_kernel,
        grid=(1,),
        in_specs=[SMEM] + whole(*parts),
        out_specs=whole(*out),
        out_shape=out,
        scratch_shapes=[pltpu.VMEM((2, BUNDLE, LANES), F32)],
        compiler_params=params(),
        cost_estimate=cost(2),
        name="finish",
    )(place, *parts)


def spread_kernel(parts_ref, small_ref, one_ref, got_ref, out_ref):
    total = parts_ref[0].astype(F32)
    for at in range(1, 4):
        total = total + parts_ref[at].astype(F32)
    small = small_ref[...].astype(F32) + one_ref[...].astype(F32) + got_ref[...].astype(F32)
    total = jnp.concatenate([total.astype(BF16), small.astype(BF16)], axis=0)
    for block in range(8):
        out_ref[block] = total[:, block * LANES : (block + 1) * LANES]


def spread(parts, small, one, one_got, deps):
    out = shape((8, parts.shape[1] + SMALL, LANES), BF16)
    return simple(spread_kernel, "spread", out, (parts, small, one, one_got), deps=deps)


def swap(values, axis_name, count, bit):
    return lax.ppermute(values, axis_name, [(at, at ^ bit) for at in range(count)])


def swap_core(values):
    return swap(values, "mp", 4, 1)


def swap_chip(values):
    return swap(values, "mp", 4, 2)


def swap_side(values):
    return swap(values, "blk", 8, 4)


def turn_z(values, hop):
    return lax.ppermute(values, "blk", [(at, at // 4 * 4 + (at - hop) % 4) for at in range(8)])


def step_dp(values, hop):
    return lax.ppermute(values, "dp", [(at, (at + hop) % 4) for at in range(4)])


def turn_dp(values):
    return [step_dp(values, hop) for hop in (1, 3, 2)]


def turn_z(values, hop):
    return lax.ppermute(values, "blk", [(at, at // 4 * 4 + (at - hop) % 4) for at in range(8)])


def spread_gather(values, axis_name, count):
    wide = jnp.broadcast_to(values[None], (count,) + values.shape)
    return lax.all_to_all(wide, axis_name, 0, 0, tiled=False)


def sum_chips(values, core, meanwhile=()):
    return join_cores(values, after(swap(values, "mp", 4, 2), meanwhile), core)


def join_cores(values, got, core):
    total = (values.astype(F32) + got.astype(F32)).astype(BF16)
    got = swap(total, "mp", 4, 1)
    first = jnp.where(core == 0, total, got)
    second = jnp.where(core == 0, got, total)
    return jnp.concatenate([first, second], axis=0)


def pick(values, at, axis):
    return lax.dynamic_index_in_dim(values, at, axis, keepdims=False)


def sum_cores(values, core):
    rows, model = values.shape
    halves = values.reshape(2, rows // 2, model)
    got = swap(pick(halves, 1 - core, 0), "mp", 4, 1)
    return (pick(halves, core, 0).astype(F32) + got.astype(F32)).astype(BF16)


def shards(
    tokens,
    cotangent,
    seg_ids,
    token_boxes,
    norm1_gain,
    w_query,
    w_key,
    w_value,
    w_out_t,
    bias_table,
    norm2_gain,
    w_gate,
    w_up,
    w_down_t,
):
    rows = tokens.shape[0]
    pair = w_query.shape[1] // 2
    blk, mp, data = lax.axis_index("blk"), lax.axis_index("mp"), lax.axis_index("dp")
    place = jnp.stack([blk // 4, blk % 4, data, mp % 2]).astype(jnp.int32)

    tokens_other = swap_side(jnp.concatenate([tokens, unfold_rows(w_out_t)], axis=0))
    table = jnp.pad(bias_table.T, ((6, 6), (0, rows - bias_table.shape[0])))
    early, late = pack(
        place,
        (
            seg_ids.reshape(1, rows),
            token_boxes,
            norm1_gain.reshape(1, LANES),
            norm2_gain.reshape(1, LANES),
            table,
        ),
        (w_query, w_key, w_value),
        (w_gate.T, w_up.T, w_down_t.T),
    )
    early_all = lax.all_to_all(early, "blk", 0, 0, tiled=False)

    turned = [turn_z(late, hop) for hop in (1, 2, 3)]
    scaled, out_w_both = scale_tokens(place, tokens, tokens_other, w_out_t)
    near = stack([late] + turned, (scaled,))
    before_near, behind_near = step_dp(near, 1), step_dp(near, 3)
    normed_one, queries, own_pairs, gains, key_meta, meta, table = project(
        place, early_all, scaled, out_w_both, ()
    )
    pairs = lax.all_to_all(
        own_pairs, "blk", 0, 0, axis_index_groups=[[0, 1, 2, 3], [4, 5, 6, 7]]
    )
    far = swap_side(near)
    after_near = step_dp(before_near, 1)
    bias = bias_scores(place, meta, key_meta, table, (before_near, behind_near))
    probs, attn_exact, attn_mine, attn_other = attend(
        place, queries, pairs, bias, (far,)
    )
    before_far, behind_far = step_dp(far, 1), step_dp(far, 3)
    after_far = step_dp(behind_far, 3)

    attn_got = swap_side(attn_other)
    keep, send = branch_part(place, attn_mine, attn_got, pairs, (before_far, behind_far, after_near))
    pieces = [near, far, before_near, before_far, behind_near, behind_far, after_near, after_far]
    ffn_w, down_w, hidden_grad = ffn_prepare(place, cotangent, pieces)
    part = add(keep, swap_core(send))
    branch = add(part, swap_chip(part), (ffn_w,))
    branch_got = swap_core(branch)
    normed_two, parts, keep, send = ffn_forward(
        place, tokens, branch, branch_got, gains, hidden_grad, ffn_w
    )
    part = add(keep, swap_core(send))
    ffn_grads = ffn_back(place, parts, normed_two, cotangent, (part,))
    grad = add(part, swap_chip(part), (ffn_grads,))
    middle_grad, branch_low, gain_two_grad, grad_mine, grad_other = middle_back(
        place, tokens, branch, branch_got, cotangent, gains, grad, swap_core(grad), pairs
    )
    ffn_grads = lax.all_to_all(ffn_grads, "dp", 0, 0, tiled=False)
    keep, send = ffn_output(place, parts, down_w, (grad_other,))
    out_part = add(keep, swap_core(send))
    out_got = swap_chip(out_part)
    score_grad, *pair_grads, query_low = attend_back(
        place, queries, grad_mine, swap_side(grad_other), attn_exact, pairs, probs, (out_part,)
    )
    pair_parts = pair_grads[:1] + [turn_z(pair_grads[hop], -hop) for hop in (1, 2, 3)]
    table_grad = table_grad_sums(meta, key_meta, score_grad, (out_got,))
    bundle, small, one, keep, send = weight_grads(
        place,
        pair_parts,
        query_low,
        normed_one,
        early_all,
        gains,
        attn_mine,
        attn_got,
        branch_low,
        gain_two_grad,
        table_grad,
    )
    bundle = bundle.reshape(4, BUNDLE // 4, -1)
    bundle = lax.all_to_all(bundle, "dp", 0, 0, tiled=False)
    ffn_parts = fold_to_blocks(place, ffn_grads, (send,))
    ffn_near = add(ffn_parts[0], swap_side(ffn_parts[1]))
    one = add(one, swap_core(one))
    bundle = spread(bundle, small, one, swap_chip(one), (ffn_near,))
    bundle = lax.all_to_all(bundle, "blk", 0, 0, tiled=False)
    ffn_turned = [turn_z(ffn_near[hop], -hop) for hop in (1, 2, 3)]
    folded = fold_bundle(bundle, ffn_near, ffn_turned)
    grad_query, grad_key, grad_value, grad_out, *ffn_final, small = finish(
        place, [folded] + turn_dp(folded), pair
    )

    part = add(keep, swap_core(send), (ffn_near,))
    part = add(part[0], swap_side(part[1]))
    grad = add(part, swap_chip(part))
    tokens_grad = tokens_back(place, tokens, gains, grad, swap_core(grad), middle_grad)

    out_sum = add(out_part, out_got, (ffn_near,))
    mixed = simple(
        mixed_kernel,
        "mixed",
        shape(tokens.shape, BF16),
        (tokens, branch, branch_got, out_sum, swap_core(out_sum)),
        place,
    )

    return (
        mixed,
        tokens_grad,
        small[0],
        grad_query,
        grad_key,
        grad_value,
        grad_out,
        small[2:6, :12].T,
        small[1],
        ffn_final[0].T,
        ffn_final[1].T,
        ffn_final[2].T,
    )


def solution(mesh):
    rows = P(("dp", "blk"), None)
    weight = P("blk", "mp")
    in_specs = (
        rows,
        rows,
        P(("dp", "blk")),
        P(None, ("dp", "blk")),
        P("blk"),
        weight,
        weight,
        weight,
        weight,
        weight,
        P("blk"),
        weight,
        weight,
        weight,
    )
    out_specs = (
        rows,
        rows,
        P("blk"),
        weight,
        weight,
        weight,
        weight,
        weight,
        P("blk"),
        weight,
        weight,
        weight,
    )
    return jax.shard_map(shards, mesh=mesh, in_specs=in_specs, out_specs=out_specs, check_vma=False)
```

```python
import functools

import jax
import jax.numpy as jnp
from jax import lax
from jax.experimental import pallas as pl
from jax.experimental.pallas import tpu as pltpu
from jax.sharding import PartitionSpec as P

HEAD_DIM = 64
EPS = 1e-06
SEQ_EDGES = (1, 2, 3, 4, 5, 6, 7, 8, 12, 16, 23, 32, 46, 64, 91)
BOX_EDGES = (2, 4, 6, 8, 12, 16, 24, 32, 48, 64, 96, 128, 192, 256, 384)
BF16 = jnp.bfloat16
F32 = jnp.float32
LANES = 128
MIB = 2**20
VMEM_MIB = 32
PREP = 10
SMEM = pl.BlockSpec(memory_space=pltpu.SMEM)


def whole(*arrays):
    return [pl.BlockSpec(item.shape, lambda s, rank=len(item.shape): (0,) * rank) for item in arrays]


def shape(dims, kind):
    return jax.ShapeDtypeStruct(dims, kind)


HBM = pl.BlockSpec(memory_space=pl.ANY)


def simple(kernel, name, out, args, place=None, deps=(), micros=0.05, mib=VMEM_MIB):
    count = len(args) + (place is not None)

    def body(*refs):
        kernel(*refs[:count], *refs[count + len(deps) :])

    single = not isinstance(out, list)
    specs = whole(*([out] if single else out))
    return pl.pallas_call(
        body,
        grid=(1,),
        in_specs=[SMEM] * (place is not None) + whole(*args) + [HBM] * len(deps),
        out_specs=specs[0] if single else specs,
        out_shape=out,
        compiler_params=params(mib),
        cost_estimate=cost(micros),
        name=name,
    )(*([place] if place is not None else []), *args, *deps)


def add_kernel(a_ref, b_ref, out_ref):
    out_ref[...] = (a_ref[...].astype(F32) + b_ref[...].astype(F32)).astype(BF16)


def add(a, b, deps=()):
    return simple(add_kernel, "add", shape(a.shape, BF16), (a, b), deps=deps)


def stack_kernel(*refs):
    for at, ref in enumerate(refs[:-1]):
        refs[-1][at] = ref[...]


def stack(parts, deps=()):
    out = shape((len(parts),) + parts[0].shape, BF16)
    return simple(stack_kernel, "stack", out, parts, deps=deps)


def both_halves(own, got, first):
    return jnp.where(first, own, got), jnp.where(first, got, own)


def keep_and_send(values, core, keep_ref, send_ref):
    half = values.shape[0] // 2
    first, second = values[:half], values[half:]
    keep_ref[...] = jnp.where(core == 0, first, second)
    send_ref[...] = jnp.where(core == 0, second, first)


def params(mib=VMEM_MIB):
    return pltpu.CompilerParams(
        vmem_limit_bytes=mib * MIB, dimension_semantics=("arbitrary",)
    )


def cost(micros):
    return pl.CostEstimate(flops=int(micros * 1.1e9), bytes_accessed=int(micros * 1e5), transcendentals=0)


def contract_rows(left, right):
    return lax.dot_general(
        left, right, (((0,), (0,)), ((), ())), preferred_element_type=jnp.float32
    )


def contract_cols(left, right):
    return lax.dot_general(
        left, right, (((1,), (1,)), ((), ())), preferred_element_type=jnp.float32
    )


def count_edges(magnitude, edge_list):
    result = jnp.zeros(magnitude.shape, jnp.int32)
    for border in edge_list:
        result = result + (magnitude >= border).astype(jnp.int32)
    return result


def box_cell(offset):
    half = jnp.abs(offset) >> 1
    cell = jnp.where(half < 32, half, (half >> 4) + 30)
    return cell + jnp.where(offset > 0, 64, 0)


def cell_bucket(cell):
    low = cell & 63
    half = jnp.where(low < 32, low, (low - 30) << 4)
    return count_edges(half * 2, BOX_EDGES) + jnp.where(cell >= 64, 16, 0)


def lookup(table, index):
    return jnp.take_along_axis(table, index, axis=1, mode="promise_in_bounds")


SMALL = 16


def pack_kernel(
    place_ref, seg_hbm, box_hbm, one_hbm, two_hbm, table_hbm, query_hbm, key_hbm, value_hbm, gate_hbm, up_hbm, down_hbm, early_ref, late_ref, *rest
):
    refs, sems = rest[:-1], rest[-1]
    units = gate_hbm.shape[0] // 4
    mine = pl.ds(pl.multiple_of(place_ref[2] * units, 16), units)
    sources = [seg_hbm, box_hbm, one_hbm, two_hbm, table_hbm, query_hbm, key_hbm, value_hbm]
    copies = [pltpu.make_async_copy(src, dst, sems.at[at]) for at, (src, dst) in enumerate(zip(sources, refs))]
    for at, src in enumerate((gate_hbm, up_hbm, down_hbm)):
        spot = late_ref.at[at * units : (at + 1) * units, :]
        copies.append(pltpu.make_async_copy(src.at[mine, :], spot, sems.at[len(sources) + at]))
    for copy in copies:
        copy.start()
    for copy in copies:
        copy.wait()
    seg_ref, box_ref, one_ref, two_ref, table_ref, query_ref, key_ref, value_ref = refs
    width = seg_ref.shape[1]
    pair = query_ref.shape[1] // 2
    row = lax.broadcasted_iota(jnp.int32, (SMALL, width), 0)
    boxes = box_ref[...]
    centre_x = boxes[0:1] + boxes[2:3]
    centre_y = boxes[1:2] + boxes[3:4]
    gains = jnp.concatenate([one_ref[...], two_ref[...]], axis=1).astype(F32)
    small = table_ref[...].astype(F32)
    for at, values in enumerate(
        (seg_ref[...], centre_x >> 8, centre_x & 255, centre_y >> 8, centre_y & 255, gains)
    ):
        small = jnp.where(row == at, values.astype(F32), small)
    small = small.astype(BF16)
    small = jnp.concatenate([small, jnp.zeros((SMALL, 3 * pair - width), BF16)], axis=1)
    for block in range(early_ref.shape[0]):
        half = block // 4
        cols = slice(half * pair, (half + 1) * pair)
        for at, ref in enumerate((query_ref, key_ref, value_ref)):
            early_ref[block, :LANES, at * pair : (at + 1) * pair] = ref[:, cols]
        early_ref[block, LANES:, :] = small


def pack(place, small, weights, late):
    pair = weights[0].shape[1] // 2
    args = small + weights
    out = [
        shape((8, LANES + SMALL, 3 * pair), BF16),
        shape((3 * late[0].shape[0] // 4, LANES), BF16),
    ]
    return pl.pallas_call(
        pack_kernel,
        grid=(1,),
        in_specs=[SMEM] + [HBM] * (len(args) + 3),
        out_specs=whole(*out),
        out_shape=out,
        scratch_shapes=[pltpu.VMEM(item.shape, item.dtype) for item in args]
        + [pltpu.SemaphoreType.DMA((len(args) + 3,))],
        compiler_params=params(64),
        cost_estimate=cost(0.05),
        name="pack",
    )(place, *args, *late)


def unfold_rows(values):
    return jnp.concatenate(jnp.split(values, 4, axis=0), axis=1)


def fold_rows(values):
    return jnp.concatenate(jnp.split(values, 4, axis=1), axis=0)


def scale_tokens_kernel(place_ref, own_ref, other_ref, out_w_ref, scaled_ref, wide_ref):
    rows = own_ref.shape[0]
    side = place_ref[0]
    for ref, half in ((own_ref, side), (other_ref, 1 - side)):
        inputs = ref[:rows, :].astype(F32)
        here = pl.ds(pl.multiple_of(half * rows, rows), rows)
        scaled_ref[here, :] = inputs * rms_scale(inputs)
    for values, half in ((out_w_ref[...], side), (fold_rows(other_ref[rows:, :]), 1 - side)):
        wide_ref[pl.ds(pl.multiple_of(half * LANES, LANES), LANES), :] = values


def scale_tokens(place, own, other, out_w):
    rows, model = own.shape
    out = [shape((2 * rows, model), F32), shape((2 * LANES, out_w.shape[1]), BF16)]
    return simple(scale_tokens_kernel, "scale_tokens", out, (own, other, out_w), place, micros=PREP)


def project_kernel(
    place_ref, early_ref, scaled_ref, out_w_ref, normed_ref, query_ref, pair_ref, gain_ref, key_ref, meta_ref, table_ref
):
    rows = scaled_ref.shape[0] // 2
    pair = query_ref.shape[1]
    side, depth = place_ref[0], place_ref[1]
    small = [early_ref[block, LANES:, :rows].astype(F32) for block in range(8)]
    for at in range(2):
        lanes = slice(at * LANES, (at + 1) * LANES)
        gain = jnp.concatenate([part[5:6, lanes] for part in small], axis=1)
        gain_ref[at : at + 1, :] = gain
        if at == 0:
            gain_one = gain

    for copy in range(4):
        pair_ref[copy, 2 * rows :, :] = out_w_ref[...]
    weight = jnp.concatenate([early_ref[block, :LANES, :] for block in range(8)], axis=0)
    normed = (scaled_ref[...] * gain_one).astype(BF16)
    normed_ref[...] = normed
    result = jnp.dot(normed, weight, preferred_element_type=F32).astype(BF16)
    query_ref[...] = result[:, :pair] * jnp.asarray(HEAD_DIM ** (-0.5), BF16)
    for copy in range(4):
        pair_ref[copy, : 2 * rows, :] = result[:, pair:]

    time = lax.broadcasted_iota(jnp.int32, (1, rows), 1)
    for block in range(8):
        part = small[block]
        at = (block % 4) * 2 + block // 4
        there = slice(at * rows, (at + 1) * rows)
        key_ref[0:1, there] = part[0:1].astype(jnp.int32)
        key_ref[1:2, there] = (part[1:2] * 256.0 + part[2:3]).astype(jnp.int32)
        key_ref[2:3, there] = (part[3:4] * 256.0 + part[4:5]).astype(jnp.int32)
        for half in range(2):
            ahead = (block - depth - 4 * half) * rows + SEQ_SPAN // 4
            key_ref[3 + half : 4 + half, there] = jnp.clip(time + ahead, 0, SEQ_SPAN - 1)
        key_ref[5:8, there] = jnp.zeros((3, rows), jnp.int32)

    for half in range(2):
        part = early_ref[depth + 4 * half, LANES:, :rows].astype(F32)
        columns = jnp.transpose(part)
        seg = columns[:, 0:1]
        centre_x = columns[:, 1:2] * 256.0 + columns[:, 2:3]
        centre_y = columns[:, 3:4] * 256.0 + columns[:, 4:5]
        for at, values in enumerate((seg, centre_x, centre_y)):
            wide = jnp.broadcast_to(values.astype(jnp.int32), (rows, LANES))
            meta_ref[at, half * rows : (half + 1) * rows, :] = wide

    lane = lax.broadcasted_iota(jnp.int32, (8, LANES), 1)
    table = jnp.zeros((8, LANES), F32)
    for block in range(8):
        entries = jnp.where(side == 0, small[block][6:8, :LANES], small[block][8:10, :LANES])
        entries = jnp.concatenate([entries, jnp.zeros((6, LANES), F32)], axis=0)
        index = jnp.clip(lane - 12 * block, 0, LANES - 1)
        found = lookup(entries, index)
        table = jnp.where((lane >= 12 * block) & (lane < 12 * block + 12), found, table)
    table_ref[...] = table


def project(place, early, scaled, out_w, deps):
    rows, model = scaled.shape[0] // 2, scaled.shape[1]
    pair = early.shape[2] // 3
    out = [
        shape((2 * rows, model), BF16),
        shape((2 * rows, pair), BF16),
        shape((4, 2 * rows + 2 * LANES, 2 * pair), BF16),
        shape((2, model), F32),
        shape((8, 8 * rows), jnp.int32),
        shape((3, 2 * rows, LANES), jnp.int32),
        shape((8, LANES), F32),
    ]
    return simple(
        project_kernel, "project", out, (early, scaled, out_w), place, deps, 0.05, 64
    )


STEPS = 3600.0
SHIFT = 10800.0
MASKED = -(2**31)


def bias_kernel(place_ref, meta_ref, key_ref, table_ref, *refs):
    bias_ref = refs[-1]
    chunk, length = bias_ref.shape
    width = TOKENS_BLOCK
    step = pl.program_id(0)
    half = step // (2 * width // chunk // 2)
    first_row = lax.rem(step * chunk, width)
    query_block = place_ref[1] + 4 * half
    lane = lax.broadcasted_iota(jnp.int32, (8, LANES), 1)
    buckets = cell_bucket(lane)
    table = table_ref[...]

    def packed(index):
        found = lookup(table, index)
        high = jnp.round(found[0:1, :] * STEPS).astype(jnp.int32)
        low = jnp.round(found[1:2, :] * STEPS + SHIFT).astype(jnp.int32)
        return (high << 16) + low

    def spread(values):
        return jnp.broadcast_to(values, (chunk, LANES))

    hor = packed(buckets + 32)
    ver = spread(packed(buckets + 64))
    seq_count = count_edges(jnp.abs(lane - 64), SEQ_EDGES) + jnp.where(lane > 64, 16, 0)
    seq = spread(packed(seq_count))
    behind, middle, beyond = [packed(jnp.full((8, LANES), at, jnp.int32)) for at in (15, 30, 31)]

    def key_block(at):
        return at // 2 + 4 * lax.rem(at, 2)

    def block_of_keys(at, with_near):
        ahead = key_block(at) * width - query_block * width - first_row
        far = spread(hor if with_near else hor + jnp.where(ahead > 0, beyond, behind))
        for column in range(width // LANES):
            there = pl.ds(pl.multiple_of(at * width + column * LANES, LANES), LANES)
            keys = key_ref[:, there]
            total = lookup(far, box_cell(keys[1:2, :] - meta_ref[1]))
            total = total + lookup(ver, box_cell(keys[2:3, :] - meta_ref[2]))
            if with_near:
                row = lax.broadcasted_iota(jnp.int32, (chunk, LANES), 0)
                col = lax.broadcasted_iota(jnp.int32, (chunk, LANES), 1)
                offset = col - row + (ahead + column * LANES)
                found = lookup(seq, jnp.clip(offset + 64, 0, LANES - 1))
                found = jnp.where(offset >= 64, middle, found)
                found = jnp.where(offset >= 91, beyond, found)
                total = total + jnp.where(offset <= -91, behind, found)
            bias_ref[:, there] = jnp.where(keys[0:1, :] == meta_ref[0], total, MASKED)

    def body(at, carry):
        near = jnp.abs(key_block(at) - query_block) <= 1
        pl.when(near)(functools.partial(block_of_keys, at, True))
        pl.when(jnp.logical_not(near))(functools.partial(block_of_keys, at, False))
        return carry

    lax.fori_loop(0, length // width, body, 0)


TOKENS_BLOCK = 256


def bias_scores(place, meta, key_meta, table, deps):
    rows = meta.shape[1]
    length = key_meta.shape[1]
    chunk = 128
    return pl.pallas_call(
        bias_kernel,
        grid=(rows // chunk,),
        in_specs=[
            pl.BlockSpec(memory_space=pltpu.SMEM),
            pl.BlockSpec((3, chunk, LANES), lambda s: (0, s, 0)),
            pl.BlockSpec((8, length), lambda s: (0, 0)),
            pl.BlockSpec((8, LANES), lambda s: (0, 0)),
        ]
        + [HBM] * len(deps),
        out_specs=pl.BlockSpec((chunk, length), lambda s: (s, 0)),
        out_shape=jax.ShapeDtypeStruct((rows, length), jnp.int32),
        compiler_params=params(64),
        cost_estimate=cost(10),
        name="bias_scores",
    )(place, meta, key_meta, table, *deps)


def head_masks(shape):
    lane = lax.broadcasted_iota(jnp.int32, shape, 1)
    return lane < HEAD_DIM, lane >= HEAD_DIM


def attend_kernel(place_ref, query_ref, bias_ref, pair_ref, *refs):
    probs_ref, exact_ref, mine_ref, other_ref = refs[-4:]
    count, _, both = pair_ref.shape
    width = bias_ref.shape[1] // count
    features = both // 2
    rows = query_ref.shape[0]
    masks = head_masks((rows, features))
    query = query_ref[...]
    allowed = []
    codes = []
    for at in range(count):
        code = bias_ref[:, at * width : (at + 1) * width]
        codes.append(code)
        allowed.append(code != MASKED)
    outs = []
    for head in range(2):
        mine = jnp.where(masks[head], query, jnp.zeros_like(query))
        scores = []
        for at in range(count):
            code = (codes[at] >> 16) if head == 0 else (codes[at] & 65535)
            score = contract_cols(mine, pair_ref[at, :width, :features])
            score = score + code.astype(F32) * (1.0 / STEPS)
            scores.append(jnp.where(allowed[at], score, -1e30))
        top = functools.reduce(jnp.maximum, scores)
        top = jnp.max(top, axis=1, keepdims=True)
        weights = [jnp.exp(score - top) for score in scores]
        total = functools.reduce(jnp.add, weights)
        inverse = 1.0 / jnp.sum(total, axis=1, keepdims=True)
        result = None
        for at in range(count):
            low = (weights[at] * inverse).astype(BF16)
            probs_ref[head, :, at * width : (at + 1) * width] = low
            part = jnp.dot(low, pair_ref[at, :width, features:], preferred_element_type=F32)
            result = part if result is None else result + part
        outs.append(result)
    exact = jnp.where(masks[0], outs[0], outs[1])
    exact_ref[...] = exact
    low = exact.astype(BF16)
    tiles = mine_ref.shape[0] // rows
    step = pl.program_id(0)
    here = pl.ds(pl.multiple_of(lax.rem(step, tiles) * rows, rows), rows)
    own = step // tiles == place_ref[0]

    @pl.when(own)
    def _():
        mine_ref[here, :] = low

    @pl.when(jnp.logical_not(own))
    def _():
        other_ref[here, :] = low


def attend(place, queries, pairs, bias, deps):
    rows, length = bias.shape
    both = pairs.shape[2]
    tile = 128
    features = both // 2
    slim = pl.BlockSpec((tile, features), lambda s: (s, 0))
    half = shape((rows // 2, features), BF16)
    return pl.pallas_call(
        attend_kernel,
        grid=(rows // tile,),
        in_specs=[SMEM, slim, pl.BlockSpec((tile, length), lambda s: (s, 0))]
        + whole(pairs)
        + [HBM] * len(deps),
        out_specs=[pl.BlockSpec((2, tile, length), lambda s: (0, s, 0)), slim] + whole(half, half),
        out_shape=[
            shape((2, rows, length), BF16),
            shape((rows, features), F32),
            half,
            half,
        ],
        compiler_params=params(64),
        cost_estimate=cost(9),
        name="attend",
    )(place, queries, bias, pairs, *deps)


def out_weight(pair_ref):
    start = pair_ref.shape[1] - 2 * LANES
    parts = []
    for block in range(8):
        first = start + block // 4 * LANES
        parts.append(pair_ref[block % 4, first : first + LANES, :])
    return jnp.concatenate(parts, axis=0)


def branch_kernel(place_ref, mine_ref, got_ref, pair_ref, keep_ref, send_ref):
    parts = both_halves(mine_ref[...], got_ref[...], place_ref[0] == 0)
    attended = jnp.concatenate(parts, axis=1)
    result = contract_cols(attended, out_weight(pair_ref)).astype(BF16)
    keep_and_send(result, place_ref[3], keep_ref, send_ref)


def branch_part(place, mine, got, pairs, deps):
    half = shape((mine.shape[0] // 2, 8 * LANES), BF16)
    return simple(branch_kernel, "branch_part", [half, half], (mine, got, pairs), place, deps, 2)


def gelu_parts(gate):
    rate = 0.7978845608028654
    square = gate * gate
    slope = jnp.tanh(rate * gate * (1.0 + 0.044715 * square))
    half = 0.5 * (1.0 + slope)
    inner = rate * (1.0 + 3.0 * 0.044715 * square)
    return gate * half, half + 0.5 * gate * (1.0 - slope * slope) * inner


def piece_copies(place_ref, piece_refs, held, sems, hop, first):
    side, depth = place_ref[0], place_ref[1]
    height = held.shape[1]
    copies = []
    for far in range(2):
        for turn in range(4):
            block = (side + far * (1 - 2 * side)) * 4 + lax.rem(depth + turn, 4)
            lanes = pl.ds(pl.multiple_of(block * LANES, LANES), LANES)
            copies.append(
                pltpu.make_async_copy(
                    piece_refs[2 * hop + far].at[turn, pl.ds(first, height), :],
                    held.at[hop, :, lanes],
                    sems.at[hop, 4 * far + turn],
                )
            )
    return copies


def ffn_prepare_kernel(place_ref, dy_ref, *refs):
    piece_refs, (weight_ref, down_ref, grad_ref, sems, down_sems) = refs[:8], refs[8:]
    units = down_ref.shape[1]
    copies = [piece_copies(place_ref, piece_refs, down_ref, down_sems, hop, 2 * units) for hop in range(4)]
    late = [piece_copies(place_ref, piece_refs, weight_ref, sems, hop, 0) for hop in range(4)]
    for group in copies + late:
        for copy in group:
            copy.start()
    for hop in range(4):
        for copy in copies[hop]:
            copy.wait()
        grad_ref[hop] = contract_cols(down_ref[hop], dy_ref[...])
    for group in late:
        for copy in group:
            copy.wait()


def ffn_prepare(place, dy, pieces):
    rows, model = dy.shape
    units = pieces[0].shape[1] // 3
    out = [
        shape((4, 2 * units, model), BF16),
        shape((4, units, model), BF16),
        shape((4, units, rows), F32),
    ]
    return pl.pallas_call(
        ffn_prepare_kernel,
        grid=(1,),
        in_specs=[SMEM] + whole(dy) + [HBM] * 8,
        out_specs=whole(*out),
        out_shape=out,
        scratch_shapes=[pltpu.SemaphoreType.DMA((4, 8)), pltpu.SemaphoreType.DMA((4, 8))],
        compiler_params=params(),
        cost_estimate=cost(4),
        name="ffn_prepare",
    )(place, dy, *pieces)


def middle_of(tokens_ref, total_ref, got_ref, core):
    branch = jnp.concatenate(both_halves(total_ref[...], got_ref[...], core == 0), axis=0)
    return tokens_ref[...].astype(F32) + branch.astype(F32)


def rms_scale(values):
    return lax.rsqrt(jnp.mean(values * values, axis=1, keepdims=True) + EPS)


def ffn_kernel(
    place_ref, tokens_ref, total_ref, got_ref, gain_ref, hidden_grad_ref, weight_ref, normed_ref, parts_ref, keep_ref, send_ref, sums, turned
):
    units = weight_ref.shape[1] // 2
    step = pl.program_id(0)

    @pl.when(step == 0)
    def _():
        middle = middle_of(tokens_ref, total_ref, got_ref, place_ref[3])
        normed = (middle * rms_scale(middle) * gain_ref[1:2, :]).astype(BF16)
        normed_ref[...] = normed
        turned[...] = jnp.transpose(normed)
        sums[...] = jnp.zeros_like(sums)

    for hop in range(weight_ref.shape[0]):
        gates = jnp.dot(weight_ref[hop], turned[...], preferred_element_type=F32)
        gate, upward = gates[:units], gates[units:]
        hidden_grad = hidden_grad_ref[hop]
        value, slope = gelu_parts(gate)
        grads = jnp.concatenate([hidden_grad * upward * slope, hidden_grad * value], axis=0)
        grads = grads.astype(BF16)
        parts_ref[hop, : 2 * units, :] = grads
        parts_ref[hop, 2 * units :, :] = (value * upward).astype(BF16)
        sums[...] += contract_rows(grads, weight_ref[hop])

    @pl.when(step == pl.num_programs(0) - 1)
    def _():
        keep_and_send(sums[...].astype(BF16), place_ref[3], keep_ref, send_ref)


def ffn_forward(place, tokens, total, got, gains, hidden_grad, weights):
    rows, model = tokens.shape
    hops, height, _ = weights.shape
    half = shape((rows // 2, model), BF16)
    parts = shape((hops, height // 2 * 3, rows), BF16)
    out = [shape((rows, model), BF16), parts, half, half]

    def chunk(item):
        return pl.BlockSpec((2,) + item.shape[1:], lambda s: (s, 0, 0))

    return pl.pallas_call(
        ffn_kernel,
        grid=(hops // 2,),
        in_specs=[SMEM]
        + whole(tokens, total, got, gains)
        + [chunk(hidden_grad), chunk(weights)],
        out_specs=whole(out[0]) + [chunk(out[1])] + whole(half, half),
        out_shape=out,
        scratch_shapes=[pltpu.VMEM((rows, model), F32), pltpu.VMEM((model, rows), BF16)],
        compiler_params=params(),
        cost_estimate=cost(5),
        name="ffn_forward",
    )(place, tokens, total, got, gains, hidden_grad, weights)


def ffn_back_kernel(place_ref, parts_ref, normed_ref, dy_ref, *refs):
    grad_ref = refs[-1]
    units = parts_ref.shape[1] // 3
    grad_ref[0, : 2 * units, :] = jnp.dot(
        parts_ref[0, : 2 * units, :], normed_ref[...], preferred_element_type=F32
    ).astype(BF16)
    grad_ref[0, 2 * units :, :] = jnp.dot(
        parts_ref[0, 2 * units :, :], dy_ref[...], preferred_element_type=F32
    ).astype(BF16)


def ffn_output_kernel(place_ref, parts_ref, weight_ref, *refs):
    keep_ref, send_ref, sums = refs[-3:]
    step = pl.program_id(0)
    part = contract_rows(parts_ref[0], weight_ref[0]) + contract_rows(parts_ref[1], weight_ref[1])

    @pl.when(step == 0)
    def _():
        sums[...] = part

    @pl.when(step > 0)
    def _():
        sums[...] += part

    @pl.when(step == pl.num_programs(0) - 1)
    def _():
        keep_and_send(sums[...].astype(BF16), place_ref[3], keep_ref, send_ref)


def ffn_output(place, parts, weights, deps):
    hops, height, rows = parts.shape
    model = weights.shape[2]
    half = shape((rows // 2, model), BF16)
    return pl.pallas_call(
        ffn_output_kernel,
        grid=(hops // 2,),
        in_specs=[
            SMEM,
            pl.BlockSpec((2, height // 3, rows), lambda s: (s, 2, 0)),
            pl.BlockSpec((2, height // 3, model), lambda s: (s, 0, 0)),
        ]
        + [HBM] * len(deps),
        out_specs=whole(half, half),
        out_shape=[half, half],
        scratch_shapes=[pltpu.VMEM((rows, model), F32)],
        compiler_params=params(),
        cost_estimate=cost(3),
        name="ffn_output",
    )(place, parts, weights, *deps)


def norm_back(inputs, gain, normed_grad):
    scale = rms_scale(inputs)
    gain_grad = jnp.sum(normed_grad * inputs * scale, axis=0, keepdims=True)
    weighted = normed_grad * gain
    mean = jnp.mean(weighted * inputs, axis=1, keepdims=True)
    return scale * weighted - inputs * (scale * scale * scale) * mean, gain_grad


def middle_kernel(
    place_ref, tokens_ref, total_ref, got_ref, dy_ref, gain_ref, grad_ref, grad_got_ref, pair_ref, middle_ref, low_ref, two_ref, mine_ref, other_ref
):
    core = place_ref[3]
    middle = middle_of(tokens_ref, total_ref, got_ref, core)
    parts = both_halves(grad_ref[...], grad_got_ref[...], core == 0)
    normed_grad = jnp.concatenate(parts, axis=0).astype(F32)
    result, gain_grad = norm_back(middle, gain_ref[1:2, :], normed_grad)
    result = dy_ref[...].astype(F32) + result
    middle_ref[...] = result
    low = result.astype(BF16)
    low_ref[...] = low
    two_ref[...] = gain_grad
    attended = jnp.dot(low, out_weight(pair_ref), preferred_element_type=F32).astype(BF16)
    pair = attended.shape[1] // 2
    first = place_ref[0] == 0
    mine_ref[...] = jnp.where(first, attended[:, :pair], attended[:, pair:])
    other_ref[...] = jnp.where(first, attended[:, pair:], attended[:, :pair])


def middle_back(place, tokens, total, got, dy, gains, grad, grad_got, pairs):
    rows, model = tokens.shape
    half = shape((rows, pairs.shape[2] // 2), BF16)
    out = [shape((rows, model), F32), shape((rows, model), BF16), shape((1, model), F32), half, half]
    args = (tokens, total, got, dy, gains, grad, grad_got, pairs)
    return simple(middle_kernel, "middle_back", out, args, place, micros=3)


def tokens_kernel(place_ref, tokens_ref, gain_ref, grad_ref, grad_got_ref, middle_ref, out_ref):
    parts = both_halves(grad_ref[...], grad_got_ref[...], place_ref[3] == 0)
    normed_grad = jnp.concatenate(parts, axis=0).astype(F32)
    result, _ = norm_back(tokens_ref[...].astype(F32), gain_ref[0:1, :], normed_grad)
    out_ref[...] = middle_ref[...] + result


def tokens_back(place, tokens, gains, grad, grad_got, middle_grad):
    out = shape(tokens.shape, F32)
    return simple(
        tokens_kernel, "tokens_back", out, (tokens, gains, grad, grad_got, middle_grad), place, micros=2
    )


def mixed_kernel(place_ref, tokens_ref, total_ref, got_ref, out_total_ref, out_got_ref, out_ref):
    core = place_ref[3]
    middle = middle_of(tokens_ref, total_ref, got_ref, core)
    parts = both_halves(out_total_ref[...], out_got_ref[...], core == 0)
    out_ref[...] = (middle + jnp.concatenate(parts, axis=0).astype(F32)).astype(BF16)


HOPS = (0, 1, 3, 2)


def ffn_back(place, parts, normed, dy, deps):
    rows, model = normed.shape
    hops, height, _ = parts.shape

    def owner(step, place_ref):
        hop = jnp.where(step == 0, 0, jnp.where(step == 1, 1, jnp.where(step == 2, 3, 2)))
        return lax.rem(place_ref[2] - hop + 4, 4)

    def same(*arrays):
        return [pl.BlockSpec(item.shape, lambda s, p: (0, 0)) for item in arrays]

    return pl.pallas_call(
        ffn_back_kernel,
        grid_spec=pltpu.PrefetchScalarGridSpec(
            num_scalar_prefetch=1,
            grid=(hops,),
            in_specs=[pl.BlockSpec((1, height, rows), lambda s, p: (s, 0, 0))]
            + same(normed, dy)
            + [HBM] * len(deps),
            out_specs=pl.BlockSpec((1, height, model), lambda s, p: (owner(s, p), 0, 0)),
        ),
        out_shape=shape((hops, height, model), BF16),
        compiler_params=params(),
        cost_estimate=cost(4),
        name="ffn_back",
    )(place, parts, normed, dy, *deps)


def fold_kernel(place_ref, parts_ref, *refs):
    out_ref = refs[-1]
    for block in range(4):
        lanes = slice(block * LANES, (block + 1) * LANES)
        total = parts_ref[0, :, lanes].astype(F32)
        for at in range(1, parts_ref.shape[0]):
            total = total + parts_ref[at, :, lanes].astype(F32)
        out_ref[0, lax.rem(block - place_ref[1] + 4, 4)] = total.astype(BF16)


def fold_to_blocks(place, parts, deps):
    count, height, model = parts.shape
    return pl.pallas_call(
        fold_kernel,
        grid_spec=pltpu.PrefetchScalarGridSpec(
            num_scalar_prefetch=1,
            grid=(2,),
            in_specs=[pl.BlockSpec((count, height, model // 2), lambda s, p: (0, 0, s))]
            + [HBM] * len(deps),
            out_specs=pl.BlockSpec(
                (1, 4, height, LANES), lambda s, p: (jnp.where(s == p[0], 0, 1), 0, 0, 0)
            ),
        ),
        out_shape=shape((2, 4, height, LANES), BF16),
        compiler_params=params(),
        cost_estimate=cost(4),
        name="fold_to_blocks",
    )(place, parts, *deps)


def attend_back_kernel(place_ref, query_ref, mine_ref, got_ref, exact_ref, probs_ref, pair_ref, *refs):
    score_ref, pair_grad_refs = refs[-9], refs[-8:-4]
    query_grad_ref, sums, delta, grads = refs[-4:]
    _, rows, width = probs_ref.shape
    features = query_ref.shape[1]
    step = pl.program_id(0)
    masks = head_masks((rows, features))
    query = query_ref[...]

    @pl.when(step == 0)
    def _():
        sums[...] = jnp.zeros_like(sums)
        parts = both_halves(mine_ref[...], got_ref[...], place_ref[0] == 0)
        grads[...] = jnp.concatenate(parts, axis=0)
        product = grads[...].astype(F32) * exact_ref[...]
        for head in range(2):
            row = jnp.sum(jnp.where(masks[head], product, 0.0), axis=1, keepdims=True)
            delta[head] = jnp.broadcast_to(row, (rows, LANES))

    grad = grads[...]
    keys = pair_ref[0, :, :features]
    values = pair_ref[0, :, features:]
    parts = []
    key_grads = []
    value_grads = []
    for head in range(2):
        cols = slice(head * HEAD_DIM, (head + 1) * HEAD_DIM)
        mine = jnp.where(masks[head], grad, jnp.zeros_like(grad))
        probs = probs_ref[head]
        prob_grad = contract_cols(mine, values)
        offset = jnp.concatenate([delta[head]] * (width // LANES), axis=1)
        score_grad = (probs.astype(F32) * (prob_grad - offset)).astype(BF16)
        score_ref[head] = score_grad
        parts.append(jnp.dot(score_grad, keys, preferred_element_type=F32))
        key_grads.append(contract_rows(query[:, cols], score_grad).astype(BF16))
        value_grads.append(contract_rows(grad[:, cols], probs).astype(BF16))
    for at in range(4):

        @pl.when(step == at)
        def _():
            for spot, part in enumerate(key_grads + value_grads):
                pair_grad_refs[at][spot * HEAD_DIM : (spot + 1) * HEAD_DIM, :] = part

    sums[...] += jnp.where(masks[0], parts[0], parts[1])

    @pl.when(step == pl.num_programs(0) - 1)
    def _():
        query_grad_ref[...] = (sums[...] * HEAD_DIM ** (-0.5)).astype(BF16)


def attend_back(place, queries, mine, got, exact, pairs, probs, deps):
    _, rows, length = probs.shape
    features = queries.shape[1]
    width, both = rows, pairs.shape[2]

    def spot(step, place_ref):
        return lax.rem(place_ref[1] + step, 4)

    def same(*arrays):
        return [pl.BlockSpec(item.shape, lambda s, p: (0, 0)) for item in arrays]

    slab = pl.BlockSpec((2, rows, width), lambda s, p: (0, 0, spot(s, p)))
    pair_grads = [shape((both, width), BF16)] * 4
    query_grad = shape((rows, features), BF16)
    return pl.pallas_call(
        attend_back_kernel,
        grid_spec=pltpu.PrefetchScalarGridSpec(
            num_scalar_prefetch=1,
            grid=(4,),
            in_specs=same(queries, mine, got, exact)
            + [slab, pl.BlockSpec((1, width, both), lambda s, p: (spot(s, p), 0, 0))]
            + [HBM] * len(deps),
            out_specs=[slab] + same(*pair_grads, query_grad),
            scratch_shapes=[
                pltpu.VMEM((rows, features), F32),
                pltpu.VMEM((2, rows, LANES), F32),
                pltpu.VMEM((rows, features), BF16),
            ],
        ),
        out_shape=[shape((2, rows, length), BF16)] + pair_grads + [query_grad],
        compiler_params=params(),
        cost_estimate=cost(5),
        name="attend_back",
    )(place, queries, mine, got, exact, probs, pairs, *deps)


BOX_SPAN = 1024
SEQ_SPAN = 512
TILE = 512


def threshold_row(edge_list, far, lane):
    borders = [-far] + [1 - edge for edge in reversed(edge_list)] + [1] + list(edge_list)
    result = jnp.zeros(lane.shape, jnp.int32)
    for at, border in enumerate(borders):
        result = jnp.where(lane == at, border, result)
    return result


def table_grad_kernel(meta_ref, key_ref, score_ref, *refs):
    out_ref, sums_ref = refs[-2:]
    _, rows, length = score_ref.shape
    half = rows // 2
    step = pl.program_id(0)
    lane = lax.broadcasted_iota(jnp.int32, (1, LANES), 1)
    level = lax.broadcasted_iota(jnp.int32, (TILE, 1), 0)

    def add(place, key_row, mine, edges, top, offset, span):
        index = jnp.clip(mine + threshold_row(edges, 4096, lane), 0, top)
        column = index & (LANES - 1)
        block = (index - offset) >> 7
        reached = (key_ref[pl.ds(key_row, 1), :] >= level + offset).astype(F32).astype(BF16)
        for head in range(2):
            sums = contract_cols(score_ref[head, span, :], reached)
            picked = jnp.zeros(column.shape, F32)
            for at in range(TILE // LANES):
                found = lookup(sums[:, at * LANES : (at + 1) * LANES], column)
                picked = picked + jnp.where(block == at, found, 0.0)
            sums_ref[place, head : head + 1, :] += jnp.sum(picked, axis=0, keepdims=True)

    @pl.when(step == 0)
    def _():
        sums_ref[...] = jnp.zeros_like(sums_ref)

    @pl.when(step < 4)
    def _():
        axis = step // 2
        mine = meta_ref[1 + axis]
        add(1 + axis, 1 + axis, mine, BOX_EDGES, BOX_SPAN - 1, (step % 2) * TILE, slice(None))

    @pl.when(step >= 4)
    def _():
        part = step - 4
        span = pl.ds(pl.multiple_of(part * half, half), half)
        mine = lax.broadcasted_iota(jnp.int32, (half, LANES), 0) + SEQ_SPAN // 4
        add(0, 3 + part, mine, SEQ_EDGES, SEQ_SPAN - 1, 0, span)

    @pl.when(step == pl.num_programs(0) - 1)
    def _():
        lanes = lax.broadcasted_iota(jnp.int32, (8, LANES), 1)
        bucket = lanes & 31
        first = jnp.where(bucket < 16, 15 - bucket, bucket)
        result = jnp.zeros((8, LANES), F32)
        for axis in range(3):
            sums = sums_ref[axis]
            part = lookup(sums, first) - jnp.where(first == 31, 0.0, lookup(sums, first + 1))
            result = jnp.where((lanes >> 5) == axis, part, result)
        out_ref[...] = result


def table_grad_sums(meta, key_meta, score_grad, deps):
    _, rows, length = score_grad.shape
    return pl.pallas_call(
        table_grad_kernel,
        grid=(6,),
        in_specs=whole(meta, key_meta, score_grad) + [HBM] * len(deps),
        out_specs=pl.BlockSpec((8, LANES), lambda s: (0, 0)),
        out_shape=shape((8, LANES), F32),
        scratch_shapes=[pltpu.VMEM((3, 8, LANES), F32)],
        compiler_params=params(),
        cost_estimate=cost(11),
        name="table_grad",
    )(meta, key_meta, score_grad, *deps)


def weight_grads_kernel(
    place_ref, query_ref, normed_ref, early_ref, gain_ref, mine_ref, got_ref, low_ref, two_ref, table_ref, *refs
):
    pair_refs, (bundle_ref, small_ref, one_ref, keep_ref, send_ref) = refs[:4], refs[4:]
    side, core = place_ref[0], place_ref[3]
    attended = jnp.concatenate(both_halves(mine_ref[...], got_ref[...], side == 0), axis=1)
    grad_out = contract_rows(attended, low_ref[...]).astype(BF16)
    total = pair_refs[0][...].astype(F32)
    for ref in pair_refs[1:]:
        total = total + ref[...].astype(F32)
    low = total.astype(BF16)
    query = query_ref[...]
    normed = normed_ref[...]
    pair = query.shape[1]
    grad_query = contract_rows(query, normed).astype(BF16)
    grad_pair = jnp.dot(low, normed, preferred_element_type=F32).astype(BF16)
    bundle_ref[:pair, :] = grad_query
    bundle_ref[pair : 3 * pair, :] = grad_pair
    bundle_ref[3 * pair : 5 * pair, :] = grad_out
    triple = jnp.concatenate([query, jnp.transpose(low)], axis=1)
    row = lax.broadcasted_iota(jnp.int32, (SMALL, LANES), 0)
    lane = lax.broadcasted_iota(jnp.int32, (8, LANES), 1)
    table = table_ref[...]
    for block in range(8):
        lanes = slice(block * LANES, (block + 1) * LANES)
        partial = contract_cols(triple, early_ref[block, :LANES, :])
        sides = both_halves(*jnp.split(partial.astype(BF16), 2, axis=0), side == 0)
        half = sides[0].shape[0] // 2
        for far in range(2):
            first, second = sides[far][:half], sides[far][half:]
            keep_ref[far, :, lanes] = jnp.where(core == 0, first, second)
            send_ref[far, :, lanes] = jnp.where(core == 0, second, first)
        one = jnp.sum(partial * normed[:, lanes].astype(F32), axis=0, keepdims=True)
        one_ref[:, lanes] = jnp.where(row == 0, one / gain_ref[0:1, lanes], 0.0).astype(BF16)
        extra = jnp.where(row == 1, two_ref[:, lanes], 0.0)
        part = lookup(table, jnp.minimum(lane + 12 * block, LANES - 1))
        for head in range(2):
            extra = jnp.where(row == 2 + head + 2 * side, part[head : head + 1], extra)
        small_ref[:, lanes] = extra.astype(BF16)


def weight_grads(place, pair_parts, query, normed, early, gains, mine, got, low, two, table):
    rows, pair = query.shape
    args = (query, normed, early, gains, mine, got, low, two, table) + tuple(pair_parts)
    half = shape((2, rows // 4, normed.shape[1]), BF16)
    small = shape((SMALL, normed.shape[1]), BF16)
    out = [shape((BUNDLE, normed.shape[1]), BF16), small, small, half, half]
    return simple(weight_grads_kernel, "weight_grads", out, args, place, micros=4)


BUNDLE = 640


def fold_bundle_kernel(parts_ref, own_ref, a_ref, b_ref, c_ref, out_ref):
    height = parts_ref.shape[1]
    for half in range(2):
        total = parts_ref[4 * half].astype(F32)
        for block in range(4 * half + 1, 4 * half + 4):
            total = total + parts_ref[block].astype(F32)
        out_ref[half * height : (half + 1) * height, :] = total.astype(BF16)
    units = own_ref[0].astype(F32)
    for ref in (a_ref, b_ref, c_ref):
        units = units + ref[...].astype(F32)
    out_ref[2 * height :, :] = units.astype(BF16)


def fold_bundle(parts, own, others):
    out = shape((2 * parts.shape[1] + own.shape[1], LANES), BF16)
    return simple(fold_bundle_kernel, "fold_bundle", out, (parts, own) + tuple(others), micros=2)


def finish_kernel(place_ref, *refs):
    parts, outs, sides = refs[:4], refs[4:-1], refs[-1]
    pair = outs[0].shape[1] // 2
    height = sides.shape[1] // 4
    block = height + SMALL
    units = (parts[0].shape[0] - 2 * block) // 3
    small = jnp.zeros((SMALL, LANES), F32)
    for hop, part in zip(HOPS, parts):
        chunk = lax.rem(place_ref[2] - hop + 4, 4)
        here = pl.ds(pl.multiple_of(chunk * height, 16), height)
        for half in range(2):
            first = half * block
            sides[half, here, :] = part[first : first + height, :].astype(F32)
            small = small + part[first + height : first + block, :].astype(F32)
        here = pl.ds(pl.multiple_of(chunk * units, 16), units)
        for at, out_ref in enumerate(outs[4:7]):
            first = 2 * block + at * units
            out_ref[here, :] = part[first : first + units, :].astype(F32)
    for half in range(2):
        cols = slice(half * pair, (half + 1) * pair)
        for at in range(3):
            outs[at][:, cols] = jnp.transpose(sides[half, at * pair : (at + 1) * pair, :])
        rows = slice((3 + half) * pair, (4 + half) * pair)
        outs[3][:, cols] = jnp.transpose(sides[0, rows, :] + sides[1, rows, :])
    outs[7][...] = small


def finish(place, parts, pair):
    units = (parts[0].shape[0] - BUNDLE // 2 - 2 * SMALL) // 3
    out = [shape((LANES, 2 * pair), F32)] * 4 + [shape((4 * units, LANES), F32)] * 3
    out = out + [shape((SMALL, LANES), F32)]
    return pl.pallas_call(
        finish_kernel,
        grid=(1,),
        in_specs=[SMEM] + whole(*parts),
        out_specs=whole(*out),
        out_shape=out,
        scratch_shapes=[pltpu.VMEM((2, BUNDLE, LANES), F32)],
        compiler_params=params(),
        cost_estimate=cost(2),
        name="finish",
    )(place, *parts)


def spread_kernel(parts_ref, small_ref, one_ref, got_ref, out_ref):
    total = parts_ref[0].astype(F32)
    for at in range(1, 4):
        total = total + parts_ref[at].astype(F32)
    small = small_ref[...].astype(F32) + one_ref[...].astype(F32) + got_ref[...].astype(F32)
    total = jnp.concatenate([total.astype(BF16), small.astype(BF16)], axis=0)
    for block in range(8):
        out_ref[block] = total[:, block * LANES : (block + 1) * LANES]


def spread(parts, small, one, one_got, deps):
    out = shape((8, parts.shape[1] + SMALL, LANES), BF16)
    return simple(spread_kernel, "spread", out, (parts, small, one, one_got), deps=deps)


def swap(values, axis_name, count, bit):
    return lax.ppermute(values, axis_name, [(at, at ^ bit) for at in range(count)])


def swap_core(values):
    return swap(values, "mp", 4, 1)


def swap_chip(values):
    return swap(values, "mp", 4, 2)


def swap_side(values):
    return swap(values, "blk", 8, 4)


def turn_z(values, hop):
    return lax.ppermute(values, "blk", [(at, at // 4 * 4 + (at - hop) % 4) for at in range(8)])


def step_dp(values, hop):
    return lax.ppermute(values, "dp", [(at, (at + hop) % 4) for at in range(4)])


def turn_dp(values):
    return [step_dp(values, hop) for hop in (1, 3, 2)]


def turn_z(values, hop):
    return lax.ppermute(values, "blk", [(at, at // 4 * 4 + (at - hop) % 4) for at in range(8)])


def spread_gather(values, axis_name, count):
    wide = jnp.broadcast_to(values[None], (count,) + values.shape)
    return lax.all_to_all(wide, axis_name, 0, 0, tiled=False)


def sum_chips(values, core, meanwhile=()):
    return join_cores(values, after(swap(values, "mp", 4, 2), meanwhile), core)


def join_cores(values, got, core):
    total = (values.astype(F32) + got.astype(F32)).astype(BF16)
    got = swap(total, "mp", 4, 1)
    first = jnp.where(core == 0, total, got)
    second = jnp.where(core == 0, got, total)
    return jnp.concatenate([first, second], axis=0)


def pick(values, at, axis):
    return lax.dynamic_index_in_dim(values, at, axis, keepdims=False)


def sum_cores(values, core):
    rows, model = values.shape
    halves = values.reshape(2, rows // 2, model)
    got = swap(pick(halves, 1 - core, 0), "mp", 4, 1)
    return (pick(halves, core, 0).astype(F32) + got.astype(F32)).astype(BF16)


def shards(
    tokens,
    cotangent,
    seg_ids,
    token_boxes,
    norm1_gain,
    w_query,
    w_key,
    w_value,
    w_out_t,
    bias_table,
    norm2_gain,
    w_gate,
    w_up,
    w_down_t,
):
    rows = tokens.shape[0]
    pair = w_query.shape[1] // 2
    blk, mp, data = lax.axis_index("blk"), lax.axis_index("mp"), lax.axis_index("dp")
    place = jnp.stack([blk // 4, blk % 4, data, mp % 2]).astype(jnp.int32)

    tokens_other = swap_side(jnp.concatenate([tokens, unfold_rows(w_out_t)], axis=0))
    table = jnp.pad(bias_table.T, ((6, 6), (0, rows - bias_table.shape[0])))
    early, late = pack(
        place,
        (
            seg_ids.reshape(1, rows),
            token_boxes,
            norm1_gain.reshape(1, LANES),
            norm2_gain.reshape(1, LANES),
            table,
        ),
        (w_query, w_key, w_value),
        (w_gate.T, w_up.T, w_down_t.T),
    )
    early_all = lax.all_to_all(early, "blk", 0, 0, tiled=False)

    turned = [turn_z(late, hop) for hop in (1, 2, 3)]
    scaled, out_w_both = scale_tokens(place, tokens, tokens_other, w_out_t)
    near = stack([late] + turned, (scaled,))
    before_near, behind_near = step_dp(near, 1), step_dp(near, 3)
    normed_one, queries, own_pairs, gains, key_meta, meta, table = project(
        place, early_all, scaled, out_w_both, ()
    )
    pairs = lax.all_to_all(
        own_pairs, "blk", 0, 0, axis_index_groups=[[0, 1, 2, 3], [4, 5, 6, 7]]
    )
    far = swap_side(near)
    after_near = step_dp(before_near, 1)
    bias = bias_scores(place, meta, key_meta, table, (before_near, behind_near))
    probs, attn_exact, attn_mine, attn_other = attend(
        place, queries, pairs, bias, (far,)
    )
    before_far, behind_far = step_dp(far, 1), step_dp(far, 3)
    after_far = step_dp(behind_far, 3)

    attn_got = swap_side(attn_other)
    keep, send = branch_part(place, attn_mine, attn_got, pairs, (before_far, behind_far, after_near))
    pieces = [near, far, before_near, before_far, behind_near, behind_far, after_near, after_far]
    ffn_w, down_w, hidden_grad = ffn_prepare(place, cotangent, pieces)
    part = add(keep, swap_core(send))
    branch = add(part, swap_chip(part), (ffn_w,))
    branch_got = swap_core(branch)
    normed_two, parts, keep, send = ffn_forward(
        place, tokens, branch, branch_got, gains, hidden_grad, ffn_w
    )
    part = add(keep, swap_core(send))
    ffn_grads = ffn_back(place, parts, normed_two, cotangent, (part,))
    grad = add(part, swap_chip(part), (ffn_grads,))
    middle_grad, branch_low, gain_two_grad, grad_mine, grad_other = middle_back(
        place, tokens, branch, branch_got, cotangent, gains, grad, swap_core(grad), pairs
    )
    ffn_grads = lax.all_to_all(ffn_grads, "dp", 0, 0, tiled=False)
    keep, send = ffn_output(place, parts, down_w, (grad_other,))
    out_part = add(keep, swap_core(send))
    out_got = swap_chip(out_part)
    score_grad, *pair_grads, query_low = attend_back(
        place, queries, grad_mine, swap_side(grad_other), attn_exact, pairs, probs, (out_part,)
    )
    pair_parts = pair_grads[:1] + [turn_z(pair_grads[hop], -hop) for hop in (1, 2, 3)]
    table_grad = table_grad_sums(meta, key_meta, score_grad, (out_got,))
    bundle, small, one, keep, send = weight_grads(
        place,
        pair_parts,
        query_low,
        normed_one,
        early_all,
        gains,
        attn_mine,
        attn_got,
        branch_low,
        gain_two_grad,
        table_grad,
    )
    bundle = bundle.reshape(4, BUNDLE // 4, -1)
    bundle = lax.all_to_all(bundle, "dp", 0, 0, tiled=False)
    ffn_parts = fold_to_blocks(place, ffn_grads, (send,))
    ffn_near = add(ffn_parts[0], swap_side(ffn_parts[1]))
    one = add(one, swap_core(one))
    bundle = spread(bundle, small, one, swap_chip(one), (ffn_near,))
    bundle = lax.all_to_all(bundle, "blk", 0, 0, tiled=False)
    ffn_turned = [turn_z(ffn_near[hop], -hop) for hop in (1, 2, 3)]
    folded = fold_bundle(bundle, ffn_near, ffn_turned)
    grad_query, grad_key, grad_value, grad_out, *ffn_final, small = finish(
        place, [folded] + turn_dp(folded), pair
    )

    part = add(keep, swap_core(send), (ffn_near,))
    part = add(part[0], swap_side(part[1]))
    grad = add(part, swap_chip(part))
    tokens_grad = tokens_back(place, tokens, gains, grad, swap_core(grad), middle_grad)

    out_sum = add(out_part, out_got, (ffn_near,))
    mixed = simple(
        mixed_kernel,
        "mixed",
        shape(tokens.shape, BF16),
        (tokens, branch, branch_got, out_sum, swap_core(out_sum)),
        place,
    )

    return (
        mixed,
        tokens_grad,
        small[0],
        grad_query,
        grad_key,
        grad_value,
        grad_out,
        small[2:6, :12].T,
        small[1],
        ffn_final[0].T,
        ffn_final[1].T,
        ffn_final[2].T,
    )


def solution(mesh):
    rows = P(("dp", "blk"), None)
    weight = P("blk", "mp")
    in_specs = (
        rows,
        rows,
        P(("dp", "blk")),
        P(None, ("dp", "blk")),
        P("blk"),
        weight,
        weight,
        weight,
        weight,
        weight,
        P("blk"),
        weight,
        weight,
        weight,
    )
    out_specs = (
        rows,
        rows,
        P("blk"),
        weight,
        weight,
        weight,
        weight,
        weight,
        P("blk"),
        weight,
        weight,
        weight,
    )
    return jax.shard_map(shards, mesh=mesh, in_specs=in_specs, out_specs=out_specs, check_vma=False)
```
